32 devices in a mesh: gx: 8 (over y, x, core), gy: 4 (over z).
Axes of the slice: x: 2, y: 2, z: 4, core: 2. Of those that a mesh axis runs over, the one named last changes fastest.
Arguments:
- fractions: float32 [3, 16384], P(None, ('gx', 'gy')), may hold values from 0 to 1
- species: int32 [16384], P(('gx', 'gy')), may hold values from 0 to 5
- send_list: int32 [8, 512], P(None, ('gx', 'gy')), may hold values from 0 to 511
- tile_list: int32 [2, 192], P(None, ('gx', 'gy')), may hold values from 0 to 9, as said below
- counts: int32 [32], P(('gx', 'gy')), may hold values from 2 to 6, as said below
- embedding: float32 [6, 128], replicated, may hold values from -6 to 6
- radial: float32 [4, 8, 128], replicated, may hold values from -0.75 to 0.75
- mixing: float32 [5, 128, 128], replicated, may hold values from -0.5 to 0.5
- readout: float32 [128], replicated, may hold values from -0.5 to 0.5
Outputs:
- atom_energy: float32 [16384], P(('gx', 'gy'))
- forces: float32 [3, 16384], P(None, ('gx', 'gy'))
The draws below stay inside these ranges and needn't reach their ends.
Inputs may be any that keep to these rules, and one draw needn't show every extreme that they name: `tile_list`: row 0 of each slot names one of the device's own 8 blocks, row 1 a block of its node list (8 own blocks, then 2 ghost blocks); slot k < 2 of every device names ghost block 8 + k. The first counts slots of a device are live, the rest are ignored.
All inputs are finite; a program needn't handle non-finite values.
Results may differ from the reference program's by a relative error of at most 0.0003.
Values sent between devices are 32-bit elements; how exact they have to be, the bound alone decides.
No kernel may reach another device: no remote copies, remote signals or barrier semaphores. Data moves between devices by JAX's collectives and lax.ppermute only.
A program may use at most 64 MiB of HBM per device.

```python
import jax
import jax.numpy as jnp
from jax import lax

CHANNELS = 128
RADIAL_BASIS = 8
ELEMENTS = 6
BLOCK_ATOMS = 64
LOCAL_BLOCKS = 8
GHOSTS = 16
TILE_SLOTS = 6
ATOMS_DEV = 512
GHOST_BLOCKS = 2
ATOMS = 16384
SEND_ROWS = 512
TILES_ALL = 192
N_GX = 8
N_GY = 4
DEVICES = 32


def draw_tile_list(key, part):
    slot_total = TILES_ALL
    first_key, second_key = jax.random.split(jax.random.fold_in(key, 3))
    left_block = jax.random.randint(first_key, (slot_total,), 0, LOCAL_BLOCKS, dtype=jnp.int32)
    slot_of = jnp.arange(slot_total, dtype=jnp.int32) % TILE_SLOTS
    anywhere = jax.random.randint(second_key, (slot_total,), 0, LOCAL_BLOCKS + GHOST_BLOCKS, dtype=jnp.int32)
    right_block = jnp.where(slot_of < GHOST_BLOCKS, LOCAL_BLOCKS + slot_of, anywhere)
    return jnp.stack([left_block, right_block]).astype(jnp.int32)


def draw_counts(key, part):
    device_total = DEVICES
    spread_key, busy_key, light_key = jax.random.split(jax.random.fold_in(key, 5), 3)
    slot_span = TILE_SLOTS - GHOST_BLOCKS
    spread = jax.random.randint(spread_key, (device_total,), 0, slot_span + 1, dtype=jnp.int32)
    live_counts = GHOST_BLOCKS + spread * spread // slot_span
    busiest = jax.random.randint(busy_key, (), 0, device_total, dtype=jnp.int32)
    lowest = (busiest + 1 + jax.random.randint(light_key, (), 0, device_total - 1, dtype=jnp.int32)) % device_total
    devices_at = jnp.arange(device_total, dtype=jnp.int32)
    live_counts = jnp.where(devices_at == busiest, TILE_SLOTS, jnp.where(devices_at == lowest, GHOST_BLOCKS, live_counts))
    return live_counts.astype(jnp.int32)


def with_ends(drawn, rng, low, high):
    longest = drawn.shape.index(max(drawn.shape))
    spots = []
    for shift in (0, 1):
        where = [jax.random.randint(jax.random.fold_in(rng, axis), (), 0, length) for axis, length in enumerate(drawn.shape)]
        where[longest] = (where[longest] + shift) % drawn.shape[longest]
        spots.append(tuple(where))
    return drawn.at[spots[0]].set(low).at[spots[1]].set(high)


def shard_levels(own_key, extent, cuts, low, largest):
    level = 1.0
    for position, shards_of in cuts:
        heights = jax.random.uniform(jax.random.fold_in(jax.random.fold_in(own_key, 6), position), (shards_of,), jnp.float32, low / len(cuts), largest / len(cuts))
        level = level * jnp.repeat(jnp.exp(heights), extent[position] // shards_of).reshape((-1,) + (1,) * (len(extent) - 1 - position))
    return level


def bell_draw(rng, extent, scale, reach, held_as=jnp.bfloat16):
    entries = jax.random.normal(rng, extent, jnp.float32) * scale
    return jnp.minimum(jnp.maximum(entries, -reach), reach).astype(held_as)


def setup_inputs(seed: int = 0) -> dict:
    keys = jax.random.split(jax.random.key(seed), 10)
    fractions = jnp.clip(1.0 * jax.random.uniform(keys[0], (3, ATOMS), jnp.float32) ** shard_levels(keys[0], (3, ATOMS), ((1, 32),), -0.2, 0.2), 0.0, 1.0)
    species = with_ends(jax.random.randint(keys[1], (ATOMS,), 0, ELEMENTS), jax.random.fold_in(keys[1], 1), 0, ELEMENTS - 1).astype(jnp.int32)
    send_list = with_ends(jax.random.randint(keys[2], (8, SEND_ROWS), 0, ATOMS_DEV), jax.random.fold_in(keys[2], 1), 0, ATOMS_DEV - 1).astype(jnp.int32)
    tile_list = draw_tile_list(jax.random.fold_in(keys[9], 71), 0)
    counts = draw_counts(jax.random.fold_in(keys[9], 71), 0)
    embedding = bell_draw(keys[5], (ELEMENTS, CHANNELS), 1.0, 6.0, jnp.float32)
    radial = bell_draw(keys[6], (4, RADIAL_BASIS, CHANNELS), BLOCK_ATOMS ** -0.5, 0.75, jnp.float32)
    mixing = bell_draw(keys[7], (5, CHANNELS, CHANNELS), CHANNELS ** -0.5, 0.5, jnp.float32)
    readout = bell_draw(keys[8], (CHANNELS,), CHANNELS ** -0.5, 0.5, jnp.float32)
    return {"fractions": fractions, "species": species, "send_list": send_list, "tile_list": tile_list, "counts": counts, "embedding": embedding, "radial": radial, "mixing": mixing, "readout": readout}


OFFSETS = ((-1, -1), (-1, 0), (-1, 1), (0, -1), (0, 1), (1, -1), (1, 0), (1, 1))
WIDTHS = (12.0, 12.0, 36.0)
CUTOFF = 5.0
SHARPNESS = 2.0
HIGHEST = lax.Precision.HIGHEST

def pair_terms(left_pos, right_pos, same_node):
    separation = right_pos[:, None, :] - left_pos[:, :, None]
    dist_sq = lax.optimization_barrier(jnp.sum(separation * separation, axis=0))
    softened = jnp.sqrt(dist_sq + 1.0)
    envelope = jnp.square(jnp.maximum(1.0 - dist_sq / (CUTOFF * CUTOFF), 0.0)) * (1.0 - same_node)
    centers = 1.0 + 0.6 * jnp.arange(RADIAL_BASIS, dtype=jnp.float32)
    radial_terms = envelope[None] * jnp.exp(-SHARPNESS * jnp.square(softened[None] - centers[:, None, None]))
    return (radial_terms, separation / softened[None])

def message_one(left_pos, right_pos, right_scalar, same_node, weight_scalar, weight_vector):
    radial_terms, direction = pair_terms(left_pos, right_pos, same_node)
    block_size = right_pos.shape[1]
    angular = jnp.concatenate([jnp.ones_like(direction[:1]), direction], axis=0)
    kernel = radial_terms[:, None] * angular[None]
    projected = jnp.dot(kernel.reshape(-1, block_size), right_scalar, precision=HIGHEST)
    projected = projected.reshape(radial_terms.shape[0], 4, left_pos.shape[1], right_scalar.shape[1])
    scalar_msg = jnp.einsum('nc,nic->ic', weight_scalar, projected[:, 0], precision=HIGHEST)
    vector_msg = jnp.einsum('nc,naic->aic', weight_vector, projected[:, 1:], precision=HIGHEST)
    return (scalar_msg, vector_msg)

def message_two(left_pos, right_pos, right_scalar, right_vector, same_node, weight_scalar, weight_vector):
    radial_terms, direction = pair_terms(left_pos, right_pos, same_node)
    basis_count = radial_terms.shape[0]
    row_count = left_pos.shape[1]
    block_size = right_pos.shape[1]
    from_scalar = jnp.dot(radial_terms.reshape(-1, block_size), right_scalar, precision=HIGHEST)
    from_scalar = from_scalar.reshape(basis_count, row_count, -1)
    kernel = radial_terms[:, :, None, :] * jnp.transpose(direction, (1, 0, 2))[None]
    from_vector = jnp.dot(kernel.reshape(basis_count * row_count, 3 * block_size), right_vector.reshape(3 * block_size, -1), precision=HIGHEST)
    from_vector = from_vector.reshape(basis_count, row_count, -1)
    return jnp.einsum('nc,nic->ic', weight_scalar, from_scalar, precision=HIGHEST) + jnp.einsum('nc,nic->ic', weight_vector, from_vector, precision=HIGHEST)

def add_rows(running, addend, offset, dimension):
    current = lax.dynamic_slice_in_dim(running, offset, addend.shape[dimension], dimension)
    return lax.dynamic_update_slice_in_dim(running, current + addend, offset, dimension)

def ghost_slots(table, send_grid):
    gathered = []
    for slot_index, (along_x, along_y) in enumerate(OFFSETS):
        chosen = send_grid[7 - slot_index]
        picked = jax.vmap(jax.vmap(lambda source, rows_at: source[rows_at]))(table, chosen)
        gathered.append(jnp.roll(picked, (-along_x, -along_y), axis=(0, 1)))
    return jnp.stack(gathered, axis=2)

def reference(fractions, species, send_list, tile_list, counts, embedding, radial, mixing, readout):
    device_total = N_GX * N_GY
    node_count = ATOMS_DEV + 8 * GHOSTS
    channels = embedding.shape[1]
    grid_frac = fractions.reshape(3, N_GX, N_GY, ATOMS_DEV)
    kind_grid = species.reshape(N_GX, N_GY, ATOMS_DEV)
    send_grid = send_list.reshape(8, N_GX, N_GY, GHOSTS)
    tile_grid = jnp.transpose(tile_list.reshape(2, device_total, TILE_SLOTS), (1, 0, 2))
    widths = jnp.array(WIDTHS, jnp.float32)
    shifts = jnp.array([[float(along_x), float(along_y), 0.0] for along_x, along_y in OFFSETS], jnp.float32)
    within = jnp.arange(BLOCK_ATOMS, dtype=jnp.int32)
    onehot = (kind_grid[..., None] == jnp.arange(ELEMENTS, dtype=jnp.int32)).astype(jnp.float32)
    local_embed = jnp.dot(onehot, embedding, precision=HIGHEST)
    ghost_embed = ghost_slots(local_embed, send_grid).reshape(N_GX, N_GY, 8 * GHOSTS, channels)
    all_embed = jnp.concatenate([local_embed, ghost_embed], axis=2).reshape(device_total, node_count, channels)

    def tile_view(tiles_here, tile_slot):
        left_start = tiles_here[0, tile_slot] * BLOCK_ATOMS
        right_start = tiles_here[1, tile_slot] * BLOCK_ATOMS
        same_node = ((left_start + within)[:, None] == (right_start + within)[None, :]).astype(jnp.float32)
        return (left_start, right_start, same_node)

    def layer_one_device(inputs_one):
        positions, scalars, tiles_here, live_count = inputs_one

        def advance(carried, tile_slot):
            scalar_acc, vector_acc = carried
            left_start, right_start, same_node = tile_view(tiles_here, tile_slot)
            left_pos = lax.dynamic_slice_in_dim(positions, left_start, BLOCK_ATOMS, 1)
            right_pos = lax.dynamic_slice_in_dim(positions, right_start, BLOCK_ATOMS, 1)
            right_scalar = lax.dynamic_slice_in_dim(scalars, right_start, BLOCK_ATOMS, 0)
            scalar_msg, vector_msg = jax.checkpoint(message_one)(left_pos, right_pos, right_scalar, same_node, radial[0], radial[1])
            live = (tile_slot < live_count).astype(jnp.float32)
            scalar_acc = add_rows(scalar_acc, live * scalar_msg, left_start, 0)
            vector_acc = add_rows(vector_acc, live * vector_msg, left_start, 1)
            return ((scalar_acc, vector_acc), None)
        initial = (jnp.zeros((ATOMS_DEV, channels), jnp.float32), jnp.zeros((3, ATOMS_DEV, channels), jnp.float32))
        result, _ = lax.scan(advance, initial, jnp.arange(TILE_SLOTS, dtype=jnp.int32))
        return result

    def layer_two_device(inputs_two):
        positions, features, tiles_here, live_count = inputs_two

        def advance(scalar_acc, tile_slot):
            left_start, right_start, same_node = tile_view(tiles_here, tile_slot)
            left_pos = lax.dynamic_slice_in_dim(positions, left_start, BLOCK_ATOMS, 1)
            right_pos = lax.dynamic_slice_in_dim(positions, right_start, BLOCK_ATOMS, 1)
            right_feat = lax.dynamic_slice_in_dim(features, right_start, BLOCK_ATOMS, 1)
            scalar_msg = jax.checkpoint(message_two)(left_pos, right_pos, right_feat[0], right_feat[1:], same_node, radial[2], radial[3])
            live = (tile_slot < live_count).astype(jnp.float32)
            return (add_rows(scalar_acc, live * scalar_msg, left_start, 0), None)
        result, _ = lax.scan(advance, jnp.zeros((ATOMS_DEV, channels), jnp.float32), jnp.arange(TILE_SLOTS, dtype=jnp.int32))
        return result

    def energies(grid_positions):
        atom_frac = jnp.moveaxis(grid_positions, 0, -1)
        ghost_frac = ghost_slots(atom_frac, send_grid) + shifts[:, None, :]
        local_cart = atom_frac * widths
        ghost_cart = (ghost_frac * widths).reshape(N_GX, N_GY, 8 * GHOSTS, 3)
        all_cart = jnp.concatenate([local_cart, ghost_cart], axis=2).reshape(device_total, node_count, 3)
        all_cart = jnp.transpose(all_cart, (0, 2, 1))
        scalar_one, vector_one = lax.map(jax.checkpoint(layer_one_device), (all_cart, all_embed, tile_grid, counts))
        own_embed = local_embed.reshape(device_total, ATOMS_DEV, channels)
        scalar_next = own_embed + jax.nn.silu(jnp.dot(scalar_one, mixing[0], precision=HIGHEST))
        gate_values = jax.nn.sigmoid(jnp.dot(scalar_one, mixing[2], precision=HIGHEST))
        vector_next = jnp.dot(vector_one, mixing[1], precision=HIGHEST) * gate_values[:, None]
        features = jnp.concatenate([scalar_next[:, None], vector_next], axis=1)
        feat_grid = jnp.moveaxis(features.reshape(N_GX, N_GY, 4, ATOMS_DEV, channels), 2, 3)
        ghost_feat = ghost_slots(feat_grid, send_grid).reshape(N_GX, N_GY, 8 * GHOSTS, 4, channels)
        all_feat = jnp.concatenate([feat_grid, ghost_feat], axis=2)
        all_feat = jnp.moveaxis(all_feat, 3, 2).reshape(device_total, 4, node_count, channels)
        scalar_two = lax.map(jax.checkpoint(layer_two_device), (all_cart, all_feat, tile_grid, counts))
        scalar_final = scalar_next + jax.nn.silu(jnp.dot(scalar_two, mixing[3], precision=HIGHEST))
        hidden = jax.nn.silu(jnp.dot(scalar_final, mixing[4], precision=HIGHEST))
        return jnp.dot(hidden, readout, precision=HIGHEST)
    energy, energy_pull = jax.vjp(energies, grid_frac)
    grad_frac, = energy_pull(jnp.ones_like(energy))
    forces = -(grad_frac / widths[:, None, None, None])
    return (energy.reshape(ATOMS), forces.reshape(3, ATOMS))
```

```python
import functools

import jax
import jax.numpy as jnp
from jax import lax
from jax.experimental import pallas as pl
from jax.experimental.pallas import tpu as pltpu
from jax.sharding import PartitionSpec as P

F32 = jnp.float32
BF16 = jnp.bfloat16

BASIS = 8
BLOCK = 64
GHOSTS = 16
SPAN = 8
HIST = BASIS * 4 * SPAN
OFFSETS = ((-1, -1), (-1, 0), (-1, 1), (0, -1), (0, 1), (1, -1), (1, 0), (1, 1))
WIDTHS = (12.0, 12.0, 36.0)
CUT_INV = 1.0 / 25.0
ROOT = 1.6986436005760381
CENTERS = tuple(1.0 + 0.6 * n for n in range(BASIS))
ROWS = 32

VMEM = pl.BlockSpec(memory_space=pltpu.VMEM)
SMEM = pl.BlockSpec(memory_space=pltpu.SMEM)
PARAMS = pltpu.CompilerParams(vmem_limit_bytes=48 * 1024 * 1024)

ROWROW = (((1,), (1,)), ((), ()))
ROWCOL = (((1,), (0,)), ((), ()))


def split(value):
    high = value.astype(BF16)
    return high, (value - high.astype(F32)).astype(BF16)


def mm(left, right, dims=ROWCOL):
    return lax.dot_general(left, right, dims, preferred_element_type=F32)


def mm3(left, right, dims=ROWCOL):
    (lh, ll), (rh, rl) = left, right
    return mm(lh, rh, dims) + mm(ll, rh, dims) + mm(lh, rl, dims)


def sigmoid(value):
    return 1.0 / (1.0 + jnp.exp(-value))


def iota(shape, dim):
    return lax.broadcasted_iota(jnp.int32, shape, dim)


def low_half():
    return iota((1, 128), 1) < BLOCK


def pick_rows(even_x, even_y, mate, far, zmate, zfar):
    x_up, x_down = jnp.where(even_x, mate, far), jnp.where(even_x, far, mate)
    y_up = [jnp.where(even_y, zmate[i], zfar[i]) for i in range(3)]
    y_down = [jnp.where(even_y, zfar[i], zmate[i]) for i in range(3)]
    sources = {
        (1, 0): x_up,
        (-1, 0): x_down,
        (0, 1): y_up[0],
        (0, -1): y_down[0],
        (1, 1): jnp.where(even_x, y_up[1], y_up[2]),
        (-1, 1): jnp.where(even_x, y_up[2], y_up[1]),
        (1, -1): jnp.where(even_x, y_down[1], y_down[2]),
        (-1, -1): jnp.where(even_x, y_down[2], y_down[1]),
    }
    slot_of = iota((8, 128), 1) // GHOSTS
    total = jnp.zeros((8, 128), F32)
    for slot, offset in enumerate(OFFSETS):
        turned = pltpu.roll(sources[offset], ((2 * slot - 7) * GHOSTS) % 128, 1)
        total = jnp.where(slot_of == slot, turned, total)
    return total


def pick_slot(slot, even_x, even_y, mate, far, zmate, zfar):
    along_x, along_y = OFFSETS[slot]
    if along_y == 0:
        near = even_x if along_x == 1 else jnp.logical_not(even_x)
        return jnp.where(near, mate[1], far[1])
    near = even_y if along_y == 1 else jnp.logical_not(even_y)
    if along_x == 0:
        return jnp.where(near, zmate[2], zfar[2])
    first = even_x if along_x == 1 else jnp.logical_not(even_x)
    return jnp.where(
        near, jnp.where(first, zmate[0], zmate[1]), jnp.where(first, zfar[0], zfar[1])
    )


def pick_all(args):
    return jnp.concatenate([pick_slot(slot, *args) for slot in range(8)], axis=0)


def put_packets(even_x, piece, mate_ref, far_ref, side_ref):
    for part in range(3):
        down, up = piece(part), piece(5 + part)
        mate_ref[part] = jnp.where(even_x, up, down)
        far_ref[part] = jnp.where(even_x, down, up)
    side_ref[0] = piece(3)
    side_ref[1] = piece(4)


def send_columns(send):
    wide = jnp.concatenate([send] * 8, axis=1)
    own = iota((8, 128), 1) // GHOSTS == iota((8, 128), 0)
    return jnp.sum(jnp.where(own, wide, 0), axis=0, keepdims=True)


def chooser(send, atoms):
    return iota((atoms, 128), 0) == send_columns(send)


def separation(col_ref, row_ref, col_block, row_block, start, sign):
    base = pl.multiple_of(col_block * BLOCK, BLOCK)
    mine = col_ref[pl.ds(base + start, ROWS), :]
    other = row_ref[row_block]
    return [sign * (other[a : a + 1, :] - mine[:, a : a + 1]) for a in range(3)]


def envelope(parts, same, start):
    dist_sq = parts[0] * parts[0] + parts[1] * parts[1] + parts[2] * parts[2]
    soft = jnp.sqrt(dist_sq + 1.0)
    rows = iota((ROWS, 128), 0) + start
    columns = iota((ROWS, 128), 1) % BLOCK
    apart = jnp.where(jnp.logical_and(rows == columns, same), 0.0, 1.0)
    margin = jnp.maximum(1.0 - dist_sq * CUT_INV, 0.0) * apart
    return soft, margin


def angular(parts, inverse):
    u = [part * inverse for part in parts]
    low = low_half()
    return jnp.where(low, 1.0, u[0]), jnp.where(low, u[1], u[2])


def pair_forward(col_ref, row_ref, left, right, high_ref, low_ref):
    for start in range(0, BLOCK, ROWS):
        parts = separation(col_ref, row_ref, left, right, start, 1.0)
        soft, margin = envelope(parts, left == right, start)
        first, second = angular(parts, 1.0 / soft)
        weight = margin * margin
        first, second = first * weight, second * weight
        scaled = soft * ROOT
        for n in range(BASIS):
            shift = scaled - ROOT * CENTERS[n]
            bell = jnp.exp2(-(shift * shift))
            here = pl.ds(n * BLOCK + start, ROWS)
            for half, factor in enumerate((first, second)):
                high, low = split(bell * factor)
                high_ref[here, half * 128 : half * 128 + 128] = high
                low_ref[here, half * 128 : half * 128 + 128] = low


def pair_swapped(col_ref, row_ref, left, right, high_ref, low_ref):
    low_lanes = low_half()
    for start in range(0, BLOCK, ROWS):
        parts = separation(col_ref, row_ref, right, left, start, -1.0)
        soft, margin = envelope(parts, left == right, start)
        inverse = 1.0 / soft
        weight = margin * margin
        factors = [weight] + [weight * (part * inverse) for part in parts]
        scaled = soft * ROOT
        for pair in range(BASIS // 2):
            center = jnp.where(low_lanes, ROOT * CENTERS[2 * pair], ROOT * CENTERS[2 * pair + 1])
            shift = scaled - center
            bell = jnp.exp2(-(shift * shift))
            for order in range(4):
                high, low = split(bell * factors[order])
                here = pl.ds(order * BLOCK + start, ROWS)
                high_ref[here, pair * 128 : pair * 128 + 128] = high
                low_ref[here, pair * 128 : pair * 128 + 128] = low


def pair_backward(col_ref, row_ref, left, right, pull_ref, grad_row, grad_col):
    low_lanes = low_half()
    lane = iota((1, 128), 1)
    sums = [jnp.zeros((1, 128), F32) for _ in range(3)]
    for start in range(0, BLOCK, ROWS):
        parts = separation(col_ref, row_ref, left, right, start, 1.0)
        soft, margin = envelope(parts, left == right, start)
        inverse = 1.0 / soft
        first, second = angular(parts, inverse)
        scaled = soft * ROOT
        by_bell = jnp.zeros((ROWS, 128), F32)
        by_shift = jnp.zeros((ROWS, 128), F32)
        by_first = jnp.zeros((ROWS, 128), F32)
        by_second = jnp.zeros((ROWS, 128), F32)
        for n in range(BASIS):
            shift = scaled - ROOT * CENTERS[n]
            bell = jnp.exp2(-(shift * shift))
            here = pl.ds(n * BLOCK + start, ROWS)
            pull_first, pull_second = pull_ref[here, 0:128], pull_ref[here, 128:256]
            both = bell * (first * pull_first + second * pull_second)
            by_bell = by_bell + both
            by_shift = by_shift + shift * both
            by_first = by_first + bell * pull_first
            by_second = by_second + bell * pull_second
        weight = margin * margin
        by_bell = by_bell + pltpu.roll(by_bell, BLOCK, 1)
        by_shift = (by_shift + pltpu.roll(by_shift, BLOCK, 1)) * weight
        by_first, by_second = by_first * weight, by_second * weight
        turned = pltpu.roll(by_second, BLOCK, 1)
        by_u = [
            jnp.where(low_lanes, pltpu.roll(by_first, BLOCK, 1), by_first),
            jnp.where(low_lanes, by_second, turned),
            jnp.where(low_lanes, turned, by_second),
        ]
        along = (by_u[0] * parts[0] + by_u[1] * parts[1] + by_u[2] * parts[2]) * inverse
        by_soft = by_shift * (-4.0 / ROOT) - along * inverse
        radial_part = by_soft * inverse + by_bell * (margin * (-4.0 * CUT_INV))
        column = jnp.zeros((ROWS, 128), F32)
        for a in range(3):
            force = by_u[a] * inverse + parts[a] * radial_part
            sums[a] = sums[a] + jnp.sum(force, axis=0, keepdims=True)
            total = jnp.sum(jnp.where(low_lanes, force, 0.0), axis=1, keepdims=True)
            column = jnp.where(lane == a, total, column)
        base = pl.multiple_of(left * BLOCK, BLOCK)
        grad_col[pl.ds(base + start, ROWS), :] -= column
    grad_row[right] += jnp.concatenate(sums + [jnp.zeros((5, 128), F32)], axis=0)


def kind_table(col_ref, block):
    base = pl.multiple_of(block * BLOCK, BLOCK)
    kind = col_ref[pl.ds(base, BLOCK), 3:4].astype(jnp.int32)
    lane = iota((BLOCK, 128), 1)
    hit = kind == lane % SPAN
    return jnp.concatenate(
        [
            jnp.where(jnp.logical_and(hit, lane // SPAN % 4 == order), 1.0, 0.0)
            for order in range(4)
        ],
        axis=0,
    ).astype(BF16)


def pack_kernel(frac_ref, kind_ref, send_ref, site_ref, out_ref):
    atoms = frac_ref.shape[1]
    rows = jnp.concatenate(
        [frac_ref[...], kind_ref[...].astype(F32), jnp.zeros((4, atoms), F32)], axis=0
    )
    site_ref[...] = rows
    out_ref[...] = exact_pick(rows, chooser(send_ref[...], atoms), ROWCOL)


def exact_pick(rows, chosen, dims):
    high = rows.astype(BF16).astype(F32)
    rest = rows - high
    middle = rest.astype(BF16).astype(F32)
    stacked = jnp.concatenate(
        [high, middle, rest - middle, jnp.zeros_like(rows)], axis=0
    ).astype(BF16)
    picked = mm(stacked, chosen.astype(F32).astype(BF16), dims)
    return picked[0:8] + picked[8:16] + picked[16:24]


def doubled(rows, block):
    chunk = rows[:, block // 2 * 128 : block // 2 * 128 + 128]
    turned = pltpu.roll(chunk, BLOCK, 1)
    low = low_half()
    return jnp.where(low, chunk, turned) if block % 2 == 0 else jnp.where(low, turned, chunk)


def upright(rows):
    return jnp.concatenate([rows, jnp.zeros((120, rows.shape[1]), F32)], axis=0).T


def first_kernel(
    tile_ref,
    count_ref,
    even_ref,
    send_ref,
    site_ref,
    mate_in,
    far_in,
    zmate_in,
    zfar_in,
    embed_ref,
    radial_ref,
    mixing_ref,
    hist_ref,
    mate_ref,
    far_ref,
    side_ref,
    col_ref,
    row_ref,
    fold_high,
    fold_low,
    fold_ref,
    high_ref,
    low_ref,
):
    atoms = site_ref.shape[1]
    blocks = atoms // BLOCK
    even_x, even_y = even_ref[0] == 0, even_ref[1] == 0
    ghosts = pick_rows(even_x, even_y, mate_in[...], far_in[...], zmate_in[...], zfar_in[...])
    row = iota((8, 128), 0)
    slot = iota((8, 128), 1) // GHOSTS
    shift_x = jnp.where(slot < 3, -1.0, jnp.where(slot < 5, 0.0, 1.0))
    down = (slot == 0) | (slot == 3) | (slot == 5)
    level = (slot == 1) | (slot == 6)
    shift_y = jnp.where(down, -1.0, jnp.where(level, 0.0, 1.0))
    shift = jnp.where(row == 0, shift_x, jnp.where(row == 1, shift_y, 0.0))
    scale = jnp.where(row < 2, WIDTHS[0], jnp.where(row == 2, WIDTHS[2], 1.0))
    ghosts = (ghosts + shift) * scale
    own = site_ref[...] * scale[:, 0:1]
    col_ref[0:atoms, :] = upright(own)
    col_ref[atoms : atoms + 128, :] = upright(ghosts)
    for block in range(blocks):
        row_ref[block] = doubled(own, block)
    for block in range(2):
        row_ref[blocks + block] = doubled(ghosts, block)
    hist_ref[...] = jnp.zeros_like(hist_ref)

    embed = jnp.concatenate([embed_ref[...], jnp.zeros((SPAN - embed_ref.shape[0], 128), F32)], axis=0)
    scalar = jnp.concatenate([radial_ref[0, n : n + 1, :] * embed for n in range(BASIS)], axis=0)
    vector = jnp.concatenate([radial_ref[1, n : n + 1, :] * embed for n in range(BASIS)], axis=0)
    scalar, vector = split(scalar), split(vector)
    to_self = mm3(scalar, split(mixing_ref[0]))
    to_gate = mm3(scalar, split(mixing_ref[2]))
    to_vector = mm3(vector, split(mixing_ref[1]))
    fold_ref[...] = jnp.zeros_like(fold_ref)
    for n in range(BASIS):
        rows = slice(n * SPAN, n * SPAN + SPAN)
        base = n * 4 * SPAN
        fold_ref[base : base + SPAN, 0:128] = to_self[rows]
        fold_ref[base : base + SPAN, 128:256] = to_gate[rows]
        for a in range(3):
            here = base + (a + 1) * SPAN
            fold_ref[here : here + SPAN, (a + 2) * 128 : (a + 3) * 128] = to_vector[rows]
    fold = split(fold_ref[...])
    fold_high[...] = fold[0]
    fold_low[...] = fold[1]

    lane_basis = iota((1, 128), 1) // (4 * SPAN)

    def tile(slot_index, carried):
        left, right = tile_ref[0, slot_index], tile_ref[1, slot_index]
        pair_forward(col_ref, row_ref, left, right, high_ref, low_ref)
        table = kind_table(col_ref, right)
        found = mm(high_ref[...], table) + mm(low_ref[...], table)
        base = pl.multiple_of(left * BLOCK, BLOCK)
        for half in range(2):
            total = jnp.zeros((BLOCK, 128), F32)
            for n in range(4):
                begin = (half * 4 + n) * BLOCK
                total = jnp.where(lane_basis == n, found[begin : begin + BLOCK], total)
            hist_ref[pl.ds(base, BLOCK), half * 128 : half * 128 + 128] += total
        return carried

    lax.fori_loop(0, count_ref[0], tile, 0)

    def piece(slot):
        return jnp.concatenate(
            [hist_ref[pl.ds(send_ref[slot, entry], 1), :] for entry in range(GHOSTS)], axis=0
        )

    put_packets(even_x, piece, mate_ref, far_ref, side_ref)


def second_kernel(
    tile_ref,
    count_ref,
    even_ref,
    hist_ref,
    mate_in,
    far_in,
    zmate_in,
    zfar_in,
    col_ref,
    row_ref,
    fold_high,
    fold_low,
    embed_ref,
    radial_ref,
    mixing_ref,
    readout_ref,
    energy_ref,
    mate_ref,
    far_ref,
    side_ref,
    pull_hist_ref,
    grad_row,
    grad_col,
    pre_ref,
    feat_high,
    feat_low,
    scalar_ref,
    high_ref,
    low_ref,
    message_ref,
    direct_ref,
    pull_message,
    grad_feat,
    swap_high,
    swap_low,
    pull_ref,
):
    atoms = hist_ref.shape[0]
    nodes = atoms + 8 * GHOSTS
    blocks = nodes // BLOCK
    even_x, even_y = even_ref[0] == 0, even_ref[1] == 0
    fold = (fold_high[...], fold_low[...])
    ghost_hist = pick_all((even_x, even_y, mate_in, far_in, zmate_in, zfar_in))
    pre_ref[0:atoms, :] = mm3(split(hist_ref[...]), fold)
    pre_ref[atoms:nodes, :] = mm3(split(ghost_hist), fold)

    def gate_of(rows):
        return sigmoid(pre_ref[rows, 128:256])

    def make_features(block, carried):
        base = pl.multiple_of(block * BLOCK, BLOCK)
        rows = pl.ds(base, BLOCK)
        kind = col_ref[rows, 3:4].astype(jnp.int32)
        scalar = jnp.zeros((BLOCK, 128), F32)
        for species in range(embed_ref.shape[0]):
            scalar = jnp.where(kind == species, embed_ref[species : species + 1, :], scalar)
        pre = pre_ref[rows, 0:128]
        scalar = scalar + pre * sigmoid(pre)
        scalar_ref[rows, :] = scalar
        gate = gate_of(rows)
        parts = [scalar] + [
            pre_ref[rows, (a + 2) * 128 : (a + 3) * 128] * gate for a in range(3)
        ]
        empty = jnp.zeros((BLOCK, 128), BF16)
        for order, part in enumerate(parts):
            high, low = split(part)
            here = pl.ds(order * BLOCK, BLOCK)
            used = 0 if order == 0 else 128
            for ref, value in ((feat_high, high), (feat_low, low)):
                ref[block, here, used : used + 128] = value
                ref[block, here, 128 - used : 256 - used] = empty
        return carried

    lax.fori_loop(0, blocks, make_features, 0)

    message_ref[...] = jnp.zeros_like(message_ref)

    def forward(slot_index, carried):
        left, right = tile_ref[0, slot_index], tile_ref[1, slot_index]
        pair_forward(col_ref, row_ref, left, right, high_ref, low_ref)
        found = mm3((high_ref[...], low_ref[...]), (feat_high[right], feat_low[right]))
        total = jnp.zeros((BLOCK, 128), F32)
        for n in range(BASIS):
            rows = slice(n * BLOCK, n * BLOCK + BLOCK)
            total = total + found[rows, 0:128] * radial_ref[2, n : n + 1, :]
            total = total + found[rows, 128:256] * radial_ref[3, n : n + 1, :]
        message_ref[pl.ds(pl.multiple_of(left * BLOCK, BLOCK), BLOCK), :] += total
        return carried

    lax.fori_loop(0, count_ref[0], forward, 0)

    mix_message, mix_hidden = split(mixing_ref[3]), split(mixing_ref[4])
    mixed = mm3(split(message_ref[...]), mix_message)
    mixed_gate = sigmoid(mixed)
    final = scalar_ref[0:atoms, :] + mixed * mixed_gate
    hidden = mm3(split(final), mix_hidden)
    hidden_gate = sigmoid(hidden)
    readout = readout_ref[...]
    energy_ref[...] = mm3(split(jnp.broadcast_to(readout, (8, 128))), split(hidden * hidden_gate), ROWROW)[0:1]
    pull_hidden = readout * (hidden_gate * (1.0 + hidden * (1.0 - hidden_gate)))
    pull_final = mm3(split(pull_hidden), mix_hidden, ROWROW)
    direct_ref[...] = pull_final
    pull_mixed = pull_final * (mixed_gate * (1.0 + mixed * (1.0 - mixed_gate)))
    pull_message[...] = mm3(split(pull_mixed), mix_message, ROWROW)

    grad_feat[...] = jnp.zeros_like(grad_feat)
    grad_row[...] = jnp.zeros_like(grad_row)
    grad_col[...] = jnp.zeros_like(grad_col)

    def backward(slot_index, carried):
        left, right = tile_ref[0, slot_index], tile_ref[1, slot_index]
        cotangent = pull_message[pl.ds(pl.multiple_of(left * BLOCK, BLOCK), BLOCK), :]
        weighted = [
            split(
                jnp.concatenate(
                    [cotangent * radial_ref[path, n : n + 1, :] for n in range(BASIS)], axis=0
                )
            )
            for path in (2, 3)
        ]
        pair_swapped(col_ref, row_ref, left, right, swap_high, swap_low)
        to_scalar = mm3((swap_high[0:BLOCK, :], swap_low[0:BLOCK, :]), weighted[0])
        to_vector = mm3((swap_high[BLOCK:, :], swap_low[BLOCK:, :]), weighted[1])
        rows = pl.ds(pl.multiple_of(right * BLOCK, BLOCK), BLOCK)
        grad_feat[rows, 0:128] += to_scalar
        for a in range(3):
            grad_feat[rows, (a + 1) * 128 : (a + 2) * 128] += to_vector[a * BLOCK : (a + 1) * BLOCK]
        both = [
            jnp.concatenate([weighted[0][part], weighted[1][part]], axis=1) for part in range(2)
        ]
        pull_ref[...] = mm3(both, (feat_high[right], feat_low[right]), ROWROW)
        pair_backward(col_ref, row_ref, left, right, pull_ref, grad_row, grad_col)
        return carried

    lax.fori_loop(0, count_ref[0], backward, 0)

    def pull_features(rows, with_direct):
        by_scalar = grad_feat[rows, 0:128]
        if with_direct:
            by_scalar = by_scalar + direct_ref[rows, :]
        pre = pre_ref[rows, 0:128]
        own_gate = sigmoid(pre)
        gate = gate_of(rows)
        by_gate = jnp.zeros_like(gate)
        by_vector = []
        for a in range(3):
            pulled = grad_feat[rows, (a + 1) * 128 : (a + 2) * 128]
            by_gate = by_gate + pulled * pre_ref[rows, (a + 2) * 128 : (a + 3) * 128]
            by_vector.append(pulled * gate)
        by_pre = by_scalar * (own_gate * (1.0 + pre * (1.0 - own_gate)))
        return jnp.concatenate([by_pre, by_gate * gate * (1.0 - gate)] + by_vector, axis=1)

    ghost_pull = mm3(split(pull_features(slice(atoms, nodes), False)), fold, ROWROW)
    put_packets(
        even_x,
        lambda slot: ghost_pull[slot * GHOSTS : slot * GHOSTS + GHOSTS],
        mate_ref,
        far_ref,
        side_ref,
    )
    pull_hist_ref[...] = mm3(split(pull_features(slice(0, atoms), True)), fold, ROWROW)


def third_kernel(
    tile_ref,
    count_ref,
    even_ref,
    send_ref,
    pull_hist_ref,
    mate_in,
    far_in,
    zmate_in,
    zfar_in,
    col_ref,
    row_ref,
    grad_row_in,
    grad_col_in,
    own_ref,
    out_ref,
    total_ref,
    grad_row,
    grad_col,
    pull_ref,
):
    atoms = pull_hist_ref.shape[0]
    blocks = atoms // BLOCK
    even_x, even_y = even_ref[0] == 0, even_ref[1] == 0
    returned = split(pick_all((even_x, even_y, mate_in, far_in, zmate_in, zfar_in)))
    chosen = chooser(send_ref[...], atoms).astype(F32).astype(BF16)
    total_ref[...] = pull_hist_ref[...] + mm(chosen, returned[0]) + mm(chosen, returned[1])
    grad_row[...] = grad_row_in[...]
    grad_col[...] = grad_col_in[...]
    lane_basis = iota((1, 128), 1) // (4 * SPAN)

    def tile(slot_index, carried):
        left, right = tile_ref[0, slot_index], tile_ref[1, slot_index]
        rows = pl.ds(pl.multiple_of(left * BLOCK, BLOCK), BLOCK)
        parts = []
        for half in range(2):
            here = total_ref[rows, half * 128 : half * 128 + 128]
            parts += [jnp.where(lane_basis == n, here, 0.0) for n in range(4)]
        high, low = split(jnp.concatenate(parts, axis=0))
        table = kind_table(col_ref, right)
        pull_ref[...] = mm(high, table, ROWROW) + mm(low, table, ROWROW)
        pair_backward(col_ref, row_ref, left, right, pull_ref, grad_row, grad_col)
        return carried

    lax.fori_loop(0, count_ref[0], tile, 0)

    low = low_half()
    out_ref[...] = jnp.where(low, grad_row[blocks], grad_row[blocks + 1])
    by_sender = jnp.concatenate(
        [jnp.where(low, grad_row[2 * k], grad_row[2 * k + 1]) for k in range(blocks // 2)], axis=1
    )
    own_ref[...] = by_sender + grad_col[...].T[0:8]


def last_kernel(even_ref, send_ref, own_ref, mate_in, far_in, zmate_in, zfar_in, force_ref):
    atoms = own_ref.shape[1]
    even_x, even_y = even_ref[0] == 0, even_ref[1] == 0
    returned = pick_rows(even_x, even_y, mate_in[...], far_in[...], zmate_in[...], zfar_in[...])
    total = own_ref[...] + exact_pick(returned, chooser(send_ref[...], atoms), ROWROW)
    force_ref[...] = -total[0:3]


def partners(axis, far):
    count = lax.axis_size(axis)
    if far:
        return [(i, (i + (1 if i % 2 else -1)) % count) for i in range(count)]
    return [(i, i ^ 1) for i in range(count)]


def swap_both(axis, to_mate, to_far):
    to_mate, to_far = lax.optimization_barrier((to_mate, to_far))
    mate = lax.ppermute(to_mate, axis, partners(axis, False))
    far = lax.ppermute(to_far, axis, partners(axis, True))
    return lax.optimization_barrier((mate, far))


def exchange_rows(rows):
    mate, far = swap_both("gx", rows, rows)
    column = jnp.stack([rows, mate, far])
    zmate, zfar = swap_both("gy", column, column)
    return mate, far, zmate, zfar


def exchange_packets(even_y, to_mate, to_far, side):
    mate, far = swap_both("gx", to_mate, to_far)
    up = jnp.concatenate([mate[2:3], far[2:3], side[1:2]], axis=0)
    down = jnp.concatenate([mate[0:1], far[0:1], side[0:1]], axis=0)
    zmate, zfar = swap_both("gy", jnp.where(even_y, up, down), jnp.where(even_y, down, up))
    return mate, far, zmate, zfar


def struct(*shape, dtype=F32):
    return jax.ShapeDtypeStruct(shape, dtype)


def call(kernel, in_specs, outs, scratch=()):
    return pl.pallas_call(
        kernel,
        in_specs=in_specs,
        out_specs=jax.tree.map(lambda _: VMEM, outs),
        out_shape=outs,
        scratch_shapes=list(scratch),
        compiler_params=PARAMS,
    )


def shards(fractions, species, send_list, tile_list, counts, embedding, radial, mixing, readout):
    atoms = fractions.shape[1]
    nodes = atoms + 8 * GHOSTS
    blocks = nodes // BLOCK
    even = jnp.stack([lax.axis_index("gx") % 2, lax.axis_index("gy") % 2]).astype(jnp.int32)
    even_y = even[1] == 0
    packets = [struct(3, GHOSTS, HIST), struct(3, GHOSTS, HIST), struct(2, GHOSTS, HIST)]
    grads = [struct(blocks, 8, 128), struct(atoms, 128)]
    pair_half = pltpu.VMEM((BASIS * BLOCK, 256), BF16)
    swap_half = pltpu.VMEM((256, BASIS * BLOCK), BF16)
    feat_half = pltpu.VMEM((blocks, 256, 256), BF16)
    pull = pltpu.VMEM((BASIS * BLOCK, 256), F32)

    site, rows = call(pack_kernel, [VMEM] * 3, [struct(8, atoms), struct(8, 128)])(
        fractions, species[None], send_list
    )
    arrived = exchange_rows(rows)
    hist, to_mate, to_far, side, col, row, fold_high, fold_low = call(
        first_kernel,
        [SMEM] * 4 + [VMEM] * 8,
        [struct(atoms, HIST)]
        + packets
        + [
            struct(nodes, 128),
            struct(blocks, 8, 128),
            struct(HIST, 640, dtype=BF16),
            struct(HIST, 640, dtype=BF16),
        ],
        [pltpu.VMEM((HIST, 640), F32), pair_half, pair_half],
    )(tile_list, counts, even, send_list, site, *arrived, embedding, radial, mixing)
    arrived = exchange_packets(even_y, to_mate, to_far, side)
    energy, to_mate, to_far, side, pull_hist, grad_row, grad_col = call(
        second_kernel,
        [SMEM] * 3 + [VMEM] * 13,
        [struct(1, atoms)] + packets + [struct(atoms, HIST)] + grads,
        [
            pltpu.VMEM((nodes, 640), F32),
            feat_half,
            feat_half,
            pltpu.VMEM((nodes, 128), F32),
            pair_half,
            pair_half,
            pltpu.VMEM((atoms, 128), F32),
            pltpu.VMEM((atoms, 128), F32),
            pltpu.VMEM((atoms, 128), F32),
            pltpu.VMEM((nodes, 512), F32),
            swap_half,
            swap_half,
            pull,
        ],
    )(
        tile_list,
        counts,
        even,
        hist,
        *arrived,
        col,
        row,
        fold_high,
        fold_low,
        embedding,
        radial,
        mixing,
        readout[None],
    )
    arrived = exchange_packets(even_y, to_mate, to_far, side)
    own, rows = call(
        third_kernel,
        [SMEM] * 3 + [VMEM] * 10,
        [struct(8, atoms), struct(8, 128)],
        [pltpu.VMEM((atoms, HIST), F32), pltpu.VMEM((blocks, 8, 128), F32), pltpu.VMEM((atoms, 128), F32), pull],
    )(tile_list, counts, even, send_list, pull_hist, *arrived, col, row, grad_row, grad_col)
    arrived = exchange_rows(rows)
    forces = call(last_kernel, [SMEM] + [VMEM] * 6, struct(3, atoms))(even, send_list, own, *arrived)
    return energy[0], forces


def solution(mesh):
    placed = (
        P(None, ("gx", "gy")),
        P(("gx", "gy")),
        P(None, ("gx", "gy")),
        P(None, ("gx", "gy")),
        P(("gx", "gy")),
        P(),
        P(),
        P(),
        P(),
    )
    return jax.shard_map(
        shards,
        mesh=mesh,
        in_specs=placed,
        out_specs=(P(("gx", "gy")), P(None, ("gx", "gy"))),
        check_vma=False,
    )
```

```python
import functools

import jax
import jax.numpy as jnp
from jax import lax
from jax.experimental import pallas as pl
from jax.experimental.pallas import tpu as pltpu
from jax.sharding import PartitionSpec as P

F32 = jnp.float32
BF16 = jnp.bfloat16

BASIS = 8
BLOCK = 64
GHOSTS = 16
SPAN = 8
HIST = BASIS * 4 * SPAN
OFFSETS = ((-1, -1), (-1, 0), (-1, 1), (0, -1), (0, 1), (1, -1), (1, 0), (1, 1))
WIDTHS = (12.0, 12.0, 36.0)
CUT_INV = 1.0 / 25.0
ROOT = 1.6986436005760381
CENTERS = tuple(1.0 + 0.6 * n for n in range(BASIS))
ROWS = 32

VMEM = pl.BlockSpec(memory_space=pltpu.VMEM)
HBM = pl.BlockSpec(memory_space=pltpu.HBM)
PARAMS = pltpu.CompilerParams(vmem_limit_bytes=16 * 1024 * 1024)

ROWROW = (((1,), (1,)), ((), ()))
ROWCOL = (((1,), (0,)), ((), ()))


def split(value):
    high = value.astype(BF16)
    return high, (value - high.astype(F32)).astype(BF16)


def mm(left, right, dims=ROWCOL):
    return lax.dot_general(left, right, dims, preferred_element_type=F32)


def mm3(left, right, dims=ROWCOL):
    (lh, ll), (rh, rl) = left, right
    summed = dims[0][1][0]
    return mm(
        jnp.concatenate([lh, ll, lh], axis=1), jnp.concatenate([rh, rh, rl], axis=summed), dims
    )


def sigmoid(value):
    return 1.0 / (1.0 + jnp.exp(-value))


def iota(shape, dim):
    return lax.broadcasted_iota(jnp.int32, shape, dim)


def low_half():
    return iota((1, 128), 1) < BLOCK


def pick_rows(even_x, even_y, mate, far, zmate, zfar):
    x_up, x_down = jnp.where(even_x, mate, far), jnp.where(even_x, far, mate)
    y_up = [jnp.where(even_y, zmate[i], zfar[i]) for i in range(3)]
    y_down = [jnp.where(even_y, zfar[i], zmate[i]) for i in range(3)]
    sources = {
        (1, 0): x_up,
        (-1, 0): x_down,
        (0, 1): y_up[0],
        (0, -1): y_down[0],
        (1, 1): jnp.where(even_x, y_up[1], y_up[2]),
        (-1, 1): jnp.where(even_x, y_up[2], y_up[1]),
        (1, -1): jnp.where(even_x, y_down[1], y_down[2]),
        (-1, -1): jnp.where(even_x, y_down[2], y_down[1]),
    }
    slot_of = iota((8, 128), 1) // GHOSTS
    total = jnp.zeros((8, 128), F32)
    for slot, offset in enumerate(OFFSETS):
        turned = pltpu.roll(sources[offset], ((2 * slot - 7) * GHOSTS) % 128, 1)
        total = jnp.where(slot_of == slot, turned, total)
    return total


def pick_slot(slot, even_x, even_y, mate, far, zmate, zfar):
    along_x, along_y = OFFSETS[slot]
    if along_y == 0:
        near = even_x if along_x == 1 else jnp.logical_not(even_x)
        return jnp.where(near, mate[1], far[1])
    near = even_y if along_y == 1 else jnp.logical_not(even_y)
    if along_x == 0:
        return jnp.where(near, zmate[2], zfar[2])
    first = even_x if along_x == 1 else jnp.logical_not(even_x)
    return jnp.where(
        near, jnp.where(first, zmate[0], zmate[1]), jnp.where(first, zfar[0], zfar[1])
    )


def pick_all(args):
    return jnp.concatenate([pick_slot(slot, *args) for slot in range(8)], axis=0)


def put_packets(even_x, piece, mate_ref, far_ref, side_ref):
    for part in range(3):
        down, up = piece(part), piece(5 + part)
        mate_ref[part] = jnp.where(even_x, up, down)
        far_ref[part] = jnp.where(even_x, down, up)
    side_ref[0] = piece(3)
    side_ref[1] = piece(4)


def send_columns(send):
    wide = jnp.concatenate([send] * 8, axis=1)
    own = iota((8, 128), 1) // GHOSTS == iota((8, 128), 0)
    return jnp.sum(jnp.where(own, wide, 0), axis=0, keepdims=True)


def chooser(send, atoms):
    return iota((atoms, 128), 0) == send_columns(send)


def block_rows(block, start=0, count=BLOCK):
    return pl.ds(pl.multiple_of(block * BLOCK, BLOCK) + start, count)


def separation(col_ref, col_block, row_ref, row_block, start, sign):
    mine = col_ref[block_rows(col_block, start, ROWS), :]
    other = row_ref[row_block]
    return [sign * (other[a : a + 1, :] - mine[:, a : a + 1]) for a in range(3)]


def envelope(parts, same, start):
    dist_sq = parts[0] * parts[0] + parts[1] * parts[1] + parts[2] * parts[2]
    soft = jnp.sqrt(dist_sq + 1.0)
    rows = iota((ROWS, 128), 0) + start
    columns = iota((ROWS, 128), 1) % BLOCK
    apart = jnp.where(jnp.logical_and(rows == columns, same), 0.0, 1.0)
    margin = jnp.maximum(1.0 - dist_sq * CUT_INV, 0.0) * apart
    return soft, margin


def angular(parts, inverse):
    u = [part * inverse for part in parts]
    low = low_half()
    return jnp.where(low, 1.0, u[0]), jnp.where(low, u[1], u[2])


def pair_forward(col_ref, left, row_ref, right, same, high_ref, low_ref):
    for start in range(0, BLOCK, ROWS):
        parts = separation(col_ref, left, row_ref, right, start, 1.0)
        soft, margin = envelope(parts, same, start)
        first, second = angular(parts, 1.0 / soft)
        weight = margin * margin
        first, second = first * weight, second * weight
        scaled = soft * ROOT
        for n in range(BASIS):
            shift = scaled - ROOT * CENTERS[n]
            bell = jnp.exp2(-(shift * shift))
            here = pl.ds(n * BLOCK + start, ROWS)
            for half, factor in enumerate((first, second)):
                high, low = split(bell * factor)
                high_ref[here, half * 128 : half * 128 + 128] = high
                low_ref[here, half * 128 : half * 128 + 128] = low


def pair_swapped(col_ref, right, row_ref, left, same, high_ref, low_ref):
    low_lanes = low_half()
    for start in range(0, BLOCK, ROWS):
        parts = separation(col_ref, right, row_ref, left, start, -1.0)
        soft, margin = envelope(parts, same, start)
        inverse = 1.0 / soft
        weight = margin * margin
        factors = [weight] + [weight * (part * inverse) for part in parts]
        scaled = soft * ROOT
        for pair in range(BASIS // 2):
            center = jnp.where(low_lanes, ROOT * CENTERS[2 * pair], ROOT * CENTERS[2 * pair + 1])
            shift = scaled - center
            bell = jnp.exp2(-(shift * shift))
            for order in range(4):
                high, low = split(bell * factors[order])
                here = pl.ds(order * BLOCK + start, ROWS)
                high_ref[here, pair * 128 : pair * 128 + 128] = high
                low_ref[here, pair * 128 : pair * 128 + 128] = low


def pair_backward(col_ref, left, row_ref, right, same, pull_ref, grad_row, grad_col):
    low_lanes = low_half()
    lane = iota((1, 128), 1)
    sums = [jnp.zeros((1, 128), F32) for _ in range(3)]
    for start in range(0, BLOCK, ROWS):
        parts = separation(col_ref, left, row_ref, right, start, 1.0)
        soft, margin = envelope(parts, same, start)
        inverse = 1.0 / soft
        first, second = angular(parts, inverse)
        scaled = soft * ROOT
        by_bell = jnp.zeros((ROWS, 128), F32)
        by_shift = jnp.zeros((ROWS, 128), F32)
        by_first = jnp.zeros((ROWS, 128), F32)
        by_second = jnp.zeros((ROWS, 128), F32)
        for n in range(BASIS):
            shift = scaled - ROOT * CENTERS[n]
            bell = jnp.exp2(-(shift * shift))
            here = pl.ds(n * BLOCK + start, ROWS)
            pull_first, pull_second = pull_ref[here, 0:128], pull_ref[here, 128:256]
            both = bell * (first * pull_first + second * pull_second)
            by_bell = by_bell + both
            by_shift = by_shift + shift * both
            by_first = by_first + bell * pull_first
            by_second = by_second + bell * pull_second
        weight = margin * margin
        by_bell = by_bell + pltpu.roll(by_bell, BLOCK, 1)
        by_shift = (by_shift + pltpu.roll(by_shift, BLOCK, 1)) * weight
        by_first, by_second = by_first * weight, by_second * weight
        turned = pltpu.roll(by_second, BLOCK, 1)
        by_u = [
            jnp.where(low_lanes, pltpu.roll(by_first, BLOCK, 1), by_first),
            jnp.where(low_lanes, by_second, turned),
            jnp.where(low_lanes, turned, by_second),
        ]
        along = (by_u[0] * parts[0] + by_u[1] * parts[1] + by_u[2] * parts[2]) * inverse
        by_soft = by_shift * (-4.0 / ROOT) - along * inverse
        radial_part = by_soft * inverse + by_bell * (margin * (-4.0 * CUT_INV))
        column = jnp.zeros((ROWS, 128), F32)
        for a in range(3):
            force = by_u[a] * inverse + parts[a] * radial_part
            sums[a] = sums[a] + jnp.sum(force, axis=0, keepdims=True)
            total = jnp.sum(jnp.where(low_lanes, force, 0.0), axis=1, keepdims=True)
            column = jnp.where(lane == a, total, column)
        grad_col[block_rows(left, start, ROWS), :] -= column
    grad_row[right] += jnp.concatenate(sums + [jnp.zeros((5, 128), F32)], axis=0)


def kind_table(col_ref, block):
    kind = col_ref[block_rows(block), 3:4].astype(jnp.int32)
    lane = iota((BLOCK, 128), 1)
    hit = kind == lane % SPAN
    return jnp.concatenate(
        [
            jnp.where(jnp.logical_and(hit, lane // SPAN % 4 == order), 1.0, 0.0)
            for order in range(4)
        ],
        axis=0,
    ).astype(BF16)


def parities(control_ref):
    return control_ref[1, 2] == 0, control_ref[2, 2] == 0


def own_tiles(control_ref, own_blocks, work):
    def step(slot, carried):
        left, right = control_ref[slot, 0], control_ref[slot, 1]

        @pl.when(right < own_blocks)
        def _():
            work(slot, left, right)

        return carried

    lax.fori_loop(2, control_ref[0, 2], step, 0)


def more_ghost_tiles(control_ref, own_blocks, work):
    def step(slot, carried):
        left, right = control_ref[slot, 0], control_ref[slot, 1]

        @pl.when(right >= own_blocks)
        def _():
            work(slot, left, right - own_blocks)

        return carried

    lax.fori_loop(2, control_ref[0, 2], step, 0)


def exact_pick(rows, chosen):
    high = rows.astype(BF16).astype(F32)
    rest = rows - high
    middle = rest.astype(BF16).astype(F32)
    stacked = jnp.concatenate(
        [high, middle, rest - middle, jnp.zeros_like(rows)], axis=0
    ).astype(BF16)
    picked = mm(stacked, chosen)
    return picked[0:8] + picked[8:16] + picked[16:24]


def fetch(pairs, sems):
    copies = [
        pltpu.make_async_copy(source, target, sems.at[i]) for i, (source, target) in enumerate(pairs)
    ]
    for copy in copies:
        copy.start()
    return copies


def pack_kernel(
    frac_in,
    kind_in,
    send_in,
    tile_in,
    site_ref,
    out_ref,
    send_ref,
    tiles_ref,
    frac_ref,
    kind_ref,
    tile_ref,
    sems,
):
    copies = fetch(
        (
            (frac_in, frac_ref),
            (kind_in, kind_ref),
            (send_in, send_ref),
            (tile_in, tile_ref),
        ),
        sems,
    )
    for copy in copies:
        copy.wait()
    atoms = frac_ref.shape[1]
    rows = jnp.concatenate(
        [frac_ref[...], kind_ref[...].astype(F32), jnp.zeros((4, atoms), F32)], axis=0
    )
    site_ref[...] = rows
    out_ref[...] = exact_pick(rows, chooser(send_ref[...], atoms).astype(F32).astype(BF16))
    slots = tile_ref.shape[1]
    lines = jnp.concatenate([tile_ref[...].astype(F32), jnp.zeros((2, 128 - slots), F32)], axis=1)
    lines = jnp.concatenate([lines, jnp.zeros((126, 128), F32)], axis=0)
    tiles_ref[...] = lines.T[0:8].astype(jnp.int32)


def doubled(rows, block):
    chunk = rows[:, block // 2 * 128 : block // 2 * 128 + 128]
    turned = pltpu.roll(chunk, BLOCK, 1)
    low = low_half()
    return jnp.where(low, chunk, turned) if block % 2 == 0 else jnp.where(low, turned, chunk)


def upright(rows):
    return jnp.concatenate([rows, jnp.zeros((120, rows.shape[1]), F32)], axis=0).T


def radial_row(weight_ref, path, n):
    row = SPAN + path * BASIS + n
    return weight_ref[row : row + 1, :]


def readout_row(weight_ref):
    row = SPAN + 4 * BASIS
    return weight_ref[row : row + 1, :]


def axis_scale():
    row = iota((8, 128), 0)
    return jnp.where(row < 2, WIDTHS[0], jnp.where(row == 2, WIDTHS[2], 1.0))


def add_histogram(col_ref, left, row_ref, right, same, kind_ref, hist_ref, high_ref, low_ref):
    pair_forward(col_ref, left, row_ref, right, same, high_ref, low_ref)
    table = kind_table(kind_ref, right)
    found = mm(high_ref[...], table) + mm(low_ref[...], table)
    lane_basis = iota((1, 128), 1) // (4 * SPAN)
    for half in range(2):
        total = jnp.zeros((BLOCK, 128), F32)
        for n in range(4):
            begin = (half * 4 + n) * BLOCK
            total = jnp.where(lane_basis == n, found[begin : begin + BLOCK], total)
        hist_ref[block_rows(left), half * 128 : half * 128 + 128] += total


def prepare_kernel(
    words_ref,
    tiles_ref,
    site_ref,
    send_ref,
    embed_in,
    radial_in,
    readout_in,
    mixing_in,
    control_ref,
    col_ref,
    row_ref,
    hist_ref,
    pair_high,
    pair_low,
    fold_high,
    fold_low,
    chosen_ref,
    mix_high,
    mix_low,
    weight_ref,
    fold_ref,
    mixing_ref,
    sems,
):
    kinds = embed_in.shape[0]
    paths = radial_in.shape[0]
    copies = fetch(
        (
            (embed_in, weight_ref.at[pl.ds(0, kinds)]),
            (radial_in, weight_ref.at[pl.ds(SPAN, paths)]),
            (readout_in, weight_ref.at[pl.ds(SPAN + paths, 1)]),
            (mixing_in, mixing_ref),
        ),
        sems,
    )
    row = iota((8, 128), 0)
    words = jnp.where(row == 0, words_ref[0, 0], jnp.where(row == 1, words_ref[0, 1], words_ref[0, 2]))
    control_ref[...] = jnp.where(iota((8, 128), 1) == 2, words, tiles_ref[...])
    atoms = site_ref.shape[1]
    blocks = atoms // BLOCK
    own = site_ref[...] * axis_scale()[:, 0:1]
    col_ref[...] = upright(own)
    for block in range(blocks):
        row_ref[block] = doubled(own, block)
    chosen_ref[...] = chooser(send_ref[...], atoms).astype(F32).astype(BF16)
    hist_ref[...] = jnp.zeros_like(hist_ref)

    def work(slot, left, right):
        add_histogram(
            col_ref, left, row_ref, right, left == right, col_ref, hist_ref,
            pair_high.at[slot], pair_low.at[slot],
        )

    own_tiles(control_ref, blocks, work)
    for copy in copies:
        copy.wait()

    embed = jnp.where(iota((SPAN, 128), 0) < kinds, weight_ref[0:SPAN, :], 0.0)
    scalar = jnp.concatenate([radial_row(weight_ref, 0, n) * embed for n in range(BASIS)], axis=0)
    vector = jnp.concatenate([radial_row(weight_ref, 1, n) * embed for n in range(BASIS)], axis=0)
    scalar, vector = split(scalar), split(vector)
    to_self = mm3(scalar, split(mixing_ref[0]))
    to_gate = mm3(scalar, split(mixing_ref[2]))
    to_vector = mm3(vector, split(mixing_ref[1]))
    fold_ref[...] = jnp.zeros_like(fold_ref)
    for n in range(BASIS):
        rows = slice(n * SPAN, n * SPAN + SPAN)
        base = n * 4 * SPAN
        fold_ref[base : base + SPAN, 0:128] = to_self[rows]
        fold_ref[base : base + SPAN, 128:256] = to_gate[rows]
        for a in range(3):
            here = base + (a + 1) * SPAN
            fold_ref[here : here + SPAN, (a + 2) * 128 : (a + 3) * 128] = to_vector[rows]
    fold_high[...], fold_low[...] = split(fold_ref[...])
    for part in range(2):
        mix_high[part], mix_low[part] = split(mixing_ref[3 + part])


def first_kernel(
    control_ref,
    send_in,
    hist_in,
    col_ref,
    mate_in,
    far_in,
    zmate_in,
    zfar_in,
    hist_ref,
    mate_ref,
    far_ref,
    side_ref,
    ghost_col,
    ghost_row,
    pair_high,
    pair_low,
    send_ref,
    sem,
):
    fetching = pltpu.make_async_copy(send_in, send_ref, sem)
    fetching.start()
    blocks = hist_in.shape[0] // BLOCK
    even_x, even_y = parities(control_ref)
    ghosts = pick_rows(even_x, even_y, mate_in[...], far_in[...], zmate_in[...], zfar_in[...])
    row = iota((8, 128), 0)
    slot = iota((8, 128), 1) // GHOSTS
    shift_x = jnp.where(slot < 3, -1.0, jnp.where(slot < 5, 0.0, 1.0))
    down = (slot == 0) | (slot == 3) | (slot == 5)
    level = (slot == 1) | (slot == 6)
    shift_y = jnp.where(down, -1.0, jnp.where(level, 0.0, 1.0))
    shift = jnp.where(row == 0, shift_x, jnp.where(row == 1, shift_y, 0.0))
    ghosts = (ghosts + shift) * axis_scale()
    ghost_col[...] = upright(ghosts)
    for block in range(2):
        ghost_row[block] = doubled(ghosts, block)
    hist_ref[...] = hist_in[...]

    def work(slot, left, right):
        add_histogram(
            col_ref, left, ghost_row, right, False, ghost_col, hist_ref,
            pair_high.at[slot], pair_low.at[slot],
        )

    for slot in range(2):
        work(slot, control_ref[slot, 0], slot)
    more_ghost_tiles(control_ref, blocks, work)
    fetching.wait()

    def piece(slot):
        return jnp.concatenate(
            [hist_ref[pl.ds(send_ref[slot, entry], 1), :] for entry in range(GHOSTS)], axis=0
        )

    put_packets(even_x, piece, mate_ref, far_ref, side_ref)


def make_features(block, col_ref, kinds, weight_ref, pre_ref, feat_high, feat_low, scalar_ref):
    rows = block_rows(block)
    kind = col_ref[rows, 3:4].astype(jnp.int32)
    scalar = jnp.zeros((BLOCK, 128), F32)
    for species in range(kinds):
        scalar = jnp.where(kind == species, weight_ref[species : species + 1, :], scalar)
    pre = pre_ref[rows, 0:128]
    scalar = scalar + pre * sigmoid(pre)
    if scalar_ref is not None:
        scalar_ref[rows, :] = scalar
    gate = sigmoid(pre_ref[rows, 128:256])
    parts = [scalar] + [pre_ref[rows, (a + 2) * 128 : (a + 3) * 128] * gate for a in range(3)]
    empty = jnp.zeros((BLOCK, 128), BF16)
    for order, part in enumerate(parts):
        high, low = split(part)
        here = pl.ds(order * BLOCK, BLOCK)
        used = 0 if order == 0 else 128
        for ref, value in ((feat_high, high), (feat_low, low)):
            ref[block, here, used : used + 128] = value
            ref[block, here, 128 - used : 256 - used] = empty


def add_message(left, right, feat_high, feat_low, weight_ref, message_ref, high_ref, low_ref):
    found = mm3((high_ref[...], low_ref[...]), (feat_high[right], feat_low[right]))
    total = jnp.zeros((BLOCK, 128), F32)
    for n in range(BASIS):
        rows = slice(n * BLOCK, n * BLOCK + BLOCK)
        total = total + found[rows, 0:128] * radial_row(weight_ref, 2, n)
        total = total + found[rows, 128:256] * radial_row(weight_ref, 3, n)
    message_ref[block_rows(left), :] += total


def feature_kernel(
    kinds,
    hist_ref,
    col_ref,
    fold_high,
    fold_low,
    weight_ref,
    pre_ref,
    feat_high,
    feat_low,
    scalar_ref,
):
    blocks = hist_ref.shape[0] // BLOCK
    pre_ref[...] = mm3(split(hist_ref[...]), (fold_high[...], fold_low[...]))

    def features(block, carried):
        make_features(block, col_ref, kinds, weight_ref, pre_ref, feat_high, feat_low, scalar_ref)
        return carried

    lax.fori_loop(0, blocks, features, 0)


def message_kernel(
    control_ref,
    row_ref,
    ghost_col,
    weight_ref,
    feat_high,
    feat_low,
    pair_high,
    pair_low,
    message_ref,
    swap_high,
    swap_low,
):
    blocks = feat_high.shape[0]
    message_ref[...] = jnp.zeros_like(message_ref)

    def work(slot, left, right):
        add_message(
            left, right, feat_high, feat_low, weight_ref, message_ref,
            pair_high.at[slot], pair_low.at[slot],
        )

    own_tiles(control_ref, blocks, work)

    def swapped(slot, left, right):
        pair_swapped(
            ghost_col, right, row_ref, left, False, swap_high.at[slot], swap_low.at[slot]
        )

    for slot in range(2):
        swapped(slot, control_ref[slot, 0], slot)
    more_ghost_tiles(control_ref, blocks, swapped)


def weighted_pull(cotangent, weight_ref, path):
    return split(
        jnp.concatenate([cotangent * radial_row(weight_ref, path, n) for n in range(BASIS)], axis=0)
    )


def add_feature_pull(right, cotangent, weight_ref, grad_feat, swap_high, swap_low):
    to_scalar = mm3(
        (swap_high[0:BLOCK, :], swap_low[0:BLOCK, :]), weighted_pull(cotangent, weight_ref, 2)
    )
    to_vector = mm3(
        (swap_high[BLOCK:, :], swap_low[BLOCK:, :]), weighted_pull(cotangent, weight_ref, 3)
    )
    rows = block_rows(right)
    grad_feat[rows, 0:128] += to_scalar
    for a in range(3):
        grad_feat[rows, (a + 1) * 128 : (a + 2) * 128] += to_vector[a * BLOCK : (a + 1) * BLOCK]


def finish(message, scalar, mix_high, mix_low, weight_ref):
    mix_message, mix_hidden = (mix_high[0], mix_low[0]), (mix_high[1], mix_low[1])
    readout = readout_row(weight_ref)
    mixed = mm3(split(message), mix_message)
    mixed_gate = sigmoid(mixed)
    final = scalar + mixed * mixed_gate
    hidden = mm3(split(final), mix_hidden)
    hidden_gate = sigmoid(hidden)
    pull_hidden = readout * (hidden_gate * (1.0 + hidden * (1.0 - hidden_gate)))
    pull_final = mm3(split(pull_hidden), mix_hidden, ROWROW)
    pull_mixed = pull_final * (mixed_gate * (1.0 + mixed * (1.0 - mixed_gate)))
    pull_message = mm3(split(pull_mixed), mix_message, ROWROW)
    return hidden * hidden_gate * readout, pull_final, pull_message


def pull_features(grad_feat, pre_ref):
    by_scalar = grad_feat[:, 0:128]
    pre = pre_ref[:, 0:128]
    own_gate = sigmoid(pre)
    gate = sigmoid(pre_ref[:, 128:256])
    by_gate = jnp.zeros_like(gate)
    by_vector = []
    for a in range(3):
        pulled = grad_feat[:, (a + 1) * 128 : (a + 2) * 128]
        by_gate = by_gate + pulled * pre_ref[:, (a + 2) * 128 : (a + 3) * 128]
        by_vector.append(pulled * gate)
    by_pre = by_scalar * (own_gate * (1.0 + pre * (1.0 - own_gate)))
    return jnp.concatenate([by_pre, by_gate * gate * (1.0 - gate)] + by_vector, axis=1)


def second_ghost_kernel(
    kinds,
    control_ref,
    mate_in,
    far_in,
    zmate_in,
    zfar_in,
    ghost_col,
    fold_high,
    fold_low,
    mix_high,
    mix_low,
    weight_ref,
    scalar_ref,
    message_in,
    pair_high,
    pair_low,
    swap_high,
    swap_low,
    mate_ref,
    far_ref,
    side_ref,
    feat_high,
    feat_low,
    message_ref,
    pre_ref,
    grad_feat,
):
    blocks = scalar_ref.shape[0] // BLOCK
    even_x, even_y = parities(control_ref)
    fold = (fold_high[...], fold_low[...])
    ghost_hist = pick_all((even_x, even_y, mate_in, far_in, zmate_in, zfar_in))
    pre_ref[...] = mm3(split(ghost_hist), fold)
    for block in range(2):
        make_features(block, ghost_col, kinds, weight_ref, pre_ref, feat_high, feat_low, None)
    message_ref[...] = message_in[...]

    def forward(slot, left, right):
        add_message(
            left, right, feat_high, feat_low, weight_ref, message_ref,
            pair_high.at[slot], pair_low.at[slot],
        )

    lefts = [control_ref[slot, 0] for slot in range(2)]
    for slot in range(2):
        forward(slot, lefts[slot], slot)
    more_ghost_tiles(control_ref, blocks, forward)

    grad_feat[...] = jnp.zeros_like(grad_feat)

    def backward(slot, right, cotangent):
        add_feature_pull(
            right, cotangent, weight_ref, grad_feat, swap_high.at[slot], swap_low.at[slot]
        )

    def finished(rows):
        take = lambda ref: jnp.concatenate([ref[row, :] for row in rows], axis=0)
        return finish(take(message_ref), take(scalar_ref), mix_high, mix_low, weight_ref)[2]

    pulled = finished([block_rows(left) for left in lefts])
    for slot in range(2):
        backward(slot, slot, pulled[slot * BLOCK : slot * BLOCK + BLOCK])
    more_ghost_tiles(
        control_ref,
        blocks,
        lambda slot, left, right: backward(slot, right, finished([block_rows(left)])),
    )

    ghost_pull = mm3(split(pull_features(grad_feat, pre_ref)), fold, ROWROW)
    put_packets(
        even_x,
        lambda slot: ghost_pull[slot * GHOSTS : slot * GHOSTS + GHOSTS],
        mate_ref,
        far_ref,
        side_ref,
    )


def second_pull_kernel(
    control_ref,
    col_ref,
    row_ref,
    mix_high,
    mix_low,
    weight_ref,
    scalar_ref,
    message_ref,
    grad_feat,
    pull_message,
    share_ref,
    swap_high,
    swap_low,
):
    blocks = scalar_ref.shape[0] // BLOCK
    share, direct, pulled = finish(
        message_ref[...], scalar_ref[...], mix_high, mix_low, weight_ref
    )
    share_ref[...] = share
    pull_message[...] = pulled
    grad_feat[:, 0:128] = direct
    grad_feat[:, 128:512] = jnp.zeros((blocks * BLOCK, 384), F32)

    def backward(slot, left, right):
        pair_swapped(col_ref, right, row_ref, left, left == right, swap_high, swap_low)
        cotangent = pull_message[block_rows(left), :]
        add_feature_pull(right, cotangent, weight_ref, grad_feat, swap_high, swap_low)

    own_tiles(control_ref, blocks, backward)


def pair_pull(left, right, pull_message, weight_ref, high_ref, low_ref):
    cotangent = pull_message[block_rows(left), :]
    first = weighted_pull(cotangent, weight_ref, 2)
    second = weighted_pull(cotangent, weight_ref, 3)
    both = [jnp.concatenate([first[part], second[part]], axis=1) for part in range(2)]
    return mm3(both, (high_ref[right], low_ref[right]), ROWROW)


def ghost_pair_kernel(
    control_ref,
    fold_high,
    fold_low,
    weight_ref,
    pre_ref,
    grad_feat,
    pull_message,
    ghost_high,
    ghost_low,
    pull_hist_ref,
    pull_ref,
):
    blocks = pre_ref.shape[0] // BLOCK
    pulled = pull_features(grad_feat, pre_ref)
    pull_hist_ref[...] = mm3(split(pulled), (fold_high[...], fold_low[...]), ROWROW)

    def work(slot, left, right):
        pull_ref[slot] = pair_pull(left, right, pull_message, weight_ref, ghost_high, ghost_low)

    for slot in range(2):
        work(slot, control_ref[slot, 0], slot)
    more_ghost_tiles(control_ref, blocks, work)


def own_pair_kernel(
    control_ref, weight_ref, pull_message, share_ref, feat_high, feat_low, pull_ref, energy_ref
):
    energy_ref[...] = jnp.sum(share_ref[...].T, axis=0, keepdims=True)

    def work(slot, left, right):
        pull_ref[slot] = pair_pull(left, right, pull_message, weight_ref, feat_high, feat_low)

    own_tiles(control_ref, feat_high.shape[0], work)


def both_pulls(total_ref, left, kind_ref, right, pull_in, pull_ref):
    lane_basis = iota((1, 128), 1) // (4 * SPAN)
    parts = []
    for half in range(2):
        here = total_ref[block_rows(left), half * 128 : half * 128 + 128]
        parts += [jnp.where(lane_basis == n, here, 0.0) for n in range(4)]
    high, low = split(jnp.concatenate(parts, axis=0))
    table = kind_table(kind_ref, right)
    pull_ref[...] = pull_in[...] + mm(high, table, ROWROW) + mm(low, table, ROWROW)


def third_ghost_kernel(
    control_ref,
    chosen_ref,
    pull_hist_ref,
    mate_in,
    far_in,
    zmate_in,
    zfar_in,
    col_ref,
    ghost_col,
    ghost_row,
    pull_in,
    out_ref,
    total_ref,
    grad_col,
    grad_ghost,
    pull_refs,
):
    blocks = pull_hist_ref.shape[0] // BLOCK
    even_x, even_y = parities(control_ref)
    returned = split(pick_all((even_x, even_y, mate_in, far_in, zmate_in, zfar_in)))
    chosen = chosen_ref[...]
    total_ref[...] = pull_hist_ref[...] + mm(chosen, returned[0]) + mm(chosen, returned[1])
    grad_ghost[...] = jnp.zeros_like(grad_ghost)
    grad_col[...] = jnp.zeros_like(grad_col)

    def work(slot, left, right, part=0):
        pull_ref = pull_refs.at[part]
        both_pulls(total_ref, left, ghost_col, right, pull_in.at[slot], pull_ref)
        pair_backward(col_ref, left, ghost_row, right, False, pull_ref, grad_ghost, grad_col)

    for slot in range(2):
        work(slot, control_ref[slot, 0], slot, slot)
    more_ghost_tiles(control_ref, blocks, work)
    out_ref[...] = jnp.where(low_half(), grad_ghost[0], grad_ghost[1])


def third_own_kernel(
    control_ref,
    chosen_ref,
    total_ref,
    col_ref,
    row_ref,
    pull_in,
    grad_col_in,
    own_ref,
    turned_ref,
    grad_row,
    grad_col,
    pull_ref,
):
    blocks = total_ref.shape[0] // BLOCK
    turned_ref[...] = chosen_ref[...].astype(F32).T.astype(BF16)
    grad_row[...] = jnp.zeros_like(grad_row)
    grad_col[...] = grad_col_in[...]

    def work(slot, left, right):
        both_pulls(total_ref, left, col_ref, right, pull_in.at[slot], pull_ref)
        pair_backward(col_ref, left, row_ref, right, left == right, pull_ref, grad_row, grad_col)

    own_tiles(control_ref, blocks, work)
    low = low_half()
    by_sender = jnp.concatenate(
        [jnp.where(low, grad_row[2 * k], grad_row[2 * k + 1]) for k in range(blocks // 2)], axis=1
    )
    own_ref[...] = by_sender + grad_col[...].T[0:8]


def last_kernel(control_ref, turned_ref, own_ref, mate_in, far_in, zmate_in, zfar_in, force_ref):
    even_x, even_y = parities(control_ref)
    returned = pick_rows(even_x, even_y, mate_in[...], far_in[...], zmate_in[...], zfar_in[...])
    total = own_ref[...] + exact_pick(returned, turned_ref[...])
    force_ref[...] = -total[0:3]


def partners(axis, far):
    count = lax.axis_size(axis)
    if far:
        return [(i, (i + (1 if i % 2 else -1)) % count) for i in range(count)]
    return [(i, i ^ 1) for i in range(count)]


def swap_both(axis, to_mate, to_far):
    to_mate, to_far = lax.optimization_barrier((to_mate, to_far))
    mate = lax.ppermute(to_mate, axis, partners(axis, False))
    far = lax.ppermute(to_far, axis, partners(axis, True))
    return lax.optimization_barrier((mate, far))


def exchange_rows(rows, beside):
    mate, far = swap_both("gx", rows, rows)
    mate, far, beside = lax.optimization_barrier((mate, far, beside))
    column = jnp.stack([rows, mate, far])
    zmate, zfar = swap_both("gy", column, column)
    return (mate, far, zmate, zfar), beside


def exchange_packets(even_y, to_mate, to_far, side, beside):
    mate, far = swap_both("gx", to_mate, to_far)
    mate, far, beside = lax.optimization_barrier((mate, far, beside))
    up = jnp.concatenate([mate[2:3], far[2:3], side[1:2]], axis=0)
    down = jnp.concatenate([mate[0:1], far[0:1], side[0:1]], axis=0)
    zmate, zfar = swap_both("gy", jnp.where(even_y, up, down), jnp.where(even_y, down, up))
    return (mate, far, zmate, zfar), beside


def struct(*shape, dtype=F32):
    return jax.ShapeDtypeStruct(shape, dtype)


def call(kernel, in_specs, outs, scratch=()):
    return pl.pallas_call(
        kernel,
        in_specs=in_specs,
        out_specs=jax.tree.map(lambda _: VMEM, outs),
        out_shape=outs,
        scratch_shapes=list(scratch),
        compiler_params=PARAMS,
    )


def shards(fractions, species, send_list, tile_list, counts, embedding, radial, mixing, readout):
    atoms = fractions.shape[1]
    blocks = atoms // BLOCK
    kinds = embedding.shape[0]
    slots = tile_list.shape[1]
    parity = [lax.axis_index("gx") % 2, lax.axis_index("gy") % 2]
    even_y = parity[1] == 0
    words = jnp.stack([counts[0], *parity]).astype(jnp.int32)[None]
    far_arrays = [
        pltpu.with_memory_space_constraint(array, pltpu.HBM)
        for array in (
            fractions,
            species[None],
            send_list,
            tile_list,
            embedding,
            radial.reshape(-1, radial.shape[2]),
            readout[None],
            mixing,
        )
    ]
    packets = [struct(3, GHOSTS, HIST), struct(3, GHOSTS, HIST), struct(2, GHOSTS, HIST)]
    hist_struct = struct(atoms, HIST)
    col_struct = struct(atoms, 128)
    own_rows, ghost_rows = struct(blocks, 8, 128), struct(2, 8, 128)
    fold_halves = [struct(HIST, 640, dtype=BF16)] * 2
    mix_halves = [struct(2, 128, 128, dtype=BF16)] * 2
    own_halves = [struct(blocks, 256, 256, dtype=BF16)] * 2
    ghost_halves = [struct(2, 256, 256, dtype=BF16)] * 2
    pairs = [struct(slots, BASIS * BLOCK, 256, dtype=BF16)] * 2
    swaps = [struct(slots, 256, BASIS * BLOCK, dtype=BF16)] * 2
    pulls = struct(slots, BASIS * BLOCK, 256)

    site, rows, send, tiles = call(
        pack_kernel,
        [HBM] * 4,
        [
            struct(8, atoms), struct(8, 128),
            struct(*send_list.shape, dtype=jnp.int32), struct(8, 128, dtype=jnp.int32),
        ],
        [
            pltpu.VMEM(fractions.shape, F32),
            pltpu.VMEM((1, atoms), jnp.int32),
            pltpu.VMEM(tile_list.shape, jnp.int32),
            pltpu.SemaphoreType.DMA((4,)),
        ],
    )(*far_arrays[0:4])
    arrived, (words, site) = exchange_rows(rows, (words, site))
    control, col, row, hist, own_high, own_low, fold_high, fold_low, chosen, *rest = call(
        prepare_kernel,
        [VMEM] * 4 + [HBM] * 4,
        [struct(8, 128, dtype=jnp.int32), col_struct, own_rows, hist_struct]
        + pairs
        + fold_halves
        + [struct(atoms, 128, dtype=BF16)]
        + mix_halves
        + [struct(2 * SPAN + 4 * BASIS, 128)],
        [
            pltpu.VMEM((HIST, 640), F32),
            pltpu.VMEM(mixing.shape, F32),
            pltpu.SemaphoreType.DMA((4,)),
        ],
    )(words, tiles, site, send, *far_arrays[4:])
    mix_high, mix_low, weights = rest
    fold, mix = (fold_high, fold_low), (mix_high, mix_low)
    hist, to_mate, to_far, side, ghost_col, ghost_row, pair_high, pair_low = call(
        first_kernel,
        [VMEM] * 8,
        [hist_struct] + packets + [struct(8 * GHOSTS, 128), ghost_rows] + pairs,
        [pltpu.SMEM(send_list.shape, jnp.int32), pltpu.SemaphoreType.DMA],
    )(control, send, hist, col, *arrived)
    features = call(
        functools.partial(feature_kernel, kinds),
        [VMEM] * 5,
        [struct(atoms, 640)] + own_halves + [col_struct],
    )(hist, col, *fold, weights)
    arrived, features = exchange_packets(even_y, to_mate, to_far, side, features)
    pre, feat_high, feat_low, scalar = features
    message, swap_high, swap_low = call(message_kernel, [VMEM] * 8, [col_struct] + swaps)(
        control, row, ghost_col, weights, feat_high, feat_low, own_high, own_low
    )
    to_mate, to_far, side, ghost_high, ghost_low, message = call(
        functools.partial(second_ghost_kernel, kinds),
        [VMEM] * 17,
        packets + ghost_halves + [col_struct],
        [pltpu.VMEM((8 * GHOSTS, 640), F32), pltpu.VMEM((8 * GHOSTS, 512), F32)],
    )(
        control, *arrived, ghost_col, *fold, *mix, weights, scalar, message,
        pair_high, pair_low, swap_high, swap_low,
    )
    second_pull = call(
        second_pull_kernel,
        [VMEM] * 8,
        [struct(atoms, 512), col_struct, col_struct],
        [pltpu.VMEM((256, BASIS * BLOCK), BF16)] * 2,
    )(control, col, row, *mix, weights, scalar, message)
    arrived, second_pull = exchange_packets(even_y, to_mate, to_far, side, second_pull)
    grad_feat, pull_message, share = second_pull
    pull_hist, pull = call(ghost_pair_kernel, [VMEM] * 9, [hist_struct, pulls])(
        control, *fold, weights, pre, grad_feat, pull_message, ghost_high, ghost_low
    )
    rows, total, grad_col = call(
        third_ghost_kernel,
        [VMEM] * 11,
        [struct(8, 128), hist_struct, col_struct],
        [pltpu.VMEM((2, 8, 128), F32), pltpu.VMEM((2, BASIS * BLOCK, 256), F32)],
    )(control, chosen, pull_hist, *arrived, col, ghost_col, ghost_row, pull)
    share, rows = lax.optimization_barrier((share, rows))
    own_pair = call(own_pair_kernel, [VMEM] * 6, [pulls, struct(1, atoms)])(
        control, weights, pull_message, share, feat_high, feat_low
    )
    arrived, own_pair = exchange_rows(rows, own_pair)
    pull, energy = own_pair
    own, turned = call(
        third_own_kernel,
        [VMEM] * 7,
        [struct(8, atoms), struct(128, atoms, dtype=BF16)],
        [
            pltpu.VMEM((blocks, 8, 128), F32),
            pltpu.VMEM((atoms, 128), F32),
            pltpu.VMEM((BASIS * BLOCK, 256), F32),
        ],
    )(control, chosen, total, col, row, pull, grad_col)
    forces = call(last_kernel, [VMEM] * 7, struct(3, atoms))(control, turned, own, *arrived)
    return energy[0], forces


def solution(mesh):
    placed = (
        P(None, ("gx", "gy")),
        P(("gx", "gy")),
        P(None, ("gx", "gy")),
        P(None, ("gx", "gy")),
        P(("gx", "gy")),
        P(),
        P(),
        P(),
        P(),
    )
    return jax.shard_map(
        shards,
        mesh=mesh,
        in_specs=placed,
        out_specs=(P(("gx", "gy")), P(None, ("gx", "gy"))),
        check_vma=False,
    )
```

```python
import functools

import jax
import jax.numpy as jnp
from jax import lax
from jax.experimental import pallas as pl
from jax.experimental.pallas import tpu as pltpu
from jax.sharding import PartitionSpec as P

F32 = jnp.float32
BF16 = jnp.bfloat16

BASIS = 8
BLOCK = 64
GHOSTS = 16
SPAN = 8
HIST = BASIS * 4 * SPAN
OFFSETS = ((-1, -1), (-1, 0), (-1, 1), (0, -1), (0, 1), (1, -1), (1, 0), (1, 1))
WIDTHS = (12.0, 12.0, 36.0)
CUT_INV = 1.0 / 25.0
ROOT = 1.6986436005760381
STEP = ROOT * 0.6
MIDDLE = 1.0 + 0.6 * (BASIS - 1) / 2
REACH = 5.125
ROWS = 32

VMEM = pl.BlockSpec(memory_space=pltpu.VMEM)
HBM = pl.BlockSpec(memory_space=pltpu.HBM)
PARAMS = pltpu.CompilerParams(vmem_limit_bytes=16 * 1024 * 1024)

ROWROW = (((1,), (1,)), ((), ()))
ROWCOL = (((1,), (0,)), ((), ()))


def split(value):
    high = value.astype(BF16)
    return high, (value - high.astype(F32)).astype(BF16)


def mm(left, right, dims=ROWCOL):
    return lax.dot_general(left, right, dims, preferred_element_type=F32)


def mm3(left, right, dims=ROWCOL):
    (lh, ll), (rh, rl) = left, right
    summed = dims[0][1][0]
    return mm(
        jnp.concatenate([lh, ll, lh], axis=1), jnp.concatenate([rh, rh, rl], axis=summed), dims
    )


def sigmoid(value):
    return 1.0 / (1.0 + jnp.exp(-value))


def iota(shape, dim):
    return lax.broadcasted_iota(jnp.int32, shape, dim)


def low_half():
    return iota((1, 128), 1) < BLOCK


def pick_rows(even_x, even_y, mate, far, zmate, zfar):
    x_up, x_down = jnp.where(even_x, mate, far), jnp.where(even_x, far, mate)
    y_up = [jnp.where(even_y, zmate[i], zfar[i]) for i in range(3)]
    y_down = [jnp.where(even_y, zfar[i], zmate[i]) for i in range(3)]
    sources = {
        (1, 0): x_up,
        (-1, 0): x_down,
        (0, 1): y_up[0],
        (0, -1): y_down[0],
        (1, 1): jnp.where(even_x, y_up[1], y_up[2]),
        (-1, 1): jnp.where(even_x, y_up[2], y_up[1]),
        (1, -1): jnp.where(even_x, y_down[1], y_down[2]),
        (-1, -1): jnp.where(even_x, y_down[2], y_down[1]),
    }
    slot_of = iota((8, 128), 1) // GHOSTS
    total = jnp.zeros((8, 128), F32)
    for slot, offset in enumerate(OFFSETS):
        turned = pltpu.roll(sources[offset], ((2 * slot - 7) * GHOSTS) % 128, 1)
        total = jnp.where(slot_of == slot, turned, total)
    return total


def pick_slot(slot, even_x, even_y, mate, far, zmate, zfar):
    along_x, along_y = OFFSETS[slot]
    if along_y == 0:
        near = even_x if along_x == 1 else jnp.logical_not(even_x)
        return jnp.where(near, mate[1], far[1])
    near = even_y if along_y == 1 else jnp.logical_not(even_y)
    if along_x == 0:
        return jnp.where(near, zmate[2], zfar[2])
    first = even_x if along_x == 1 else jnp.logical_not(even_x)
    return jnp.where(
        near, jnp.where(first, zmate[0], zmate[1]), jnp.where(first, zfar[0], zfar[1])
    )


def pick_all(args):
    return jnp.concatenate([pick_slot(slot, *args) for slot in range(8)], axis=0)


def put_packets(even_x, piece, mate_ref, far_ref, side_ref):
    for part in range(3):
        down, up = piece(part), piece(5 + part)
        mate_ref[part] = jnp.where(even_x, up, down)
        far_ref[part] = jnp.where(even_x, down, up)
    side_ref[0] = piece(3)
    side_ref[1] = piece(4)


def send_columns(send):
    wide = jnp.concatenate([send] * 8, axis=1)
    own = iota((8, 128), 1) // GHOSTS == iota((8, 128), 0)
    return jnp.sum(jnp.where(own, wide, 0), axis=0, keepdims=True)


def chooser(send, atoms):
    return iota((atoms, 128), 0) == send_columns(send)


def block_rows(block, start=0, count=BLOCK):
    return pl.ds(pl.multiple_of(block * BLOCK, BLOCK) + start, count)


def separation(col_ref, col_block, row_ref, row_block, start, sign):
    mine = col_ref[block_rows(col_block, start, ROWS), :]
    other = row_ref[row_block]
    return [sign * (other[a : a + 1, :] - mine[:, a : a + 1]) for a in range(3)]


def envelope(parts, same, start):
    dist_sq = parts[0] * parts[0] + parts[1] * parts[1] + parts[2] * parts[2]
    soft = jnp.sqrt(dist_sq + 1.0)
    rows = iota((ROWS, 128), 0) + start
    columns = iota((ROWS, 128), 1) % BLOCK
    apart = jnp.where(jnp.logical_and(rows == columns, same), 0.0, 1.0)
    margin = jnp.maximum(1.0 - dist_sq * CUT_INV, 0.0) * apart
    return soft, margin


def angular(parts, inverse):
    u = [part * inverse for part in parts]
    low = low_half()
    return jnp.where(low, 1.0, u[0]), jnp.where(low, u[1], u[2])


def basis_scale(shape):
    step = (iota(shape, 0) % BASIS).astype(F32) - (BASIS - 1) / 2
    return jnp.exp2(-(STEP * STEP) * (step * step))


def centered(soft):
    return ROOT * (jnp.minimum(soft, REACH) - MIDDLE)


def pair_forward(col_ref, left, row_ref, right, same, high_ref, low_ref):
    for start in range(0, BLOCK, ROWS):
        parts = separation(col_ref, left, row_ref, right, start, 1.0)
        soft, margin = envelope(parts, same, start)
        first, second = angular(parts, 1.0 / soft)
        z = centered(soft)
        bell = jnp.exp2(-z * (z + (BASIS - 1) * STEP)) * (margin * margin)
        growth = jnp.exp2((2.0 * STEP) * z)
        for n in range(BASIS):
            here = pl.ds(n * BLOCK + start, ROWS)
            for half, factor in enumerate((first, second)):
                high, low = split(bell * factor)
                high_ref[here, half * 128 : half * 128 + 128] = high
                low_ref[here, half * 128 : half * 128 + 128] = low
            bell = bell * growth


def pair_swapped(col_ref, right, row_ref, left, same, high_ref, low_ref):
    low_lanes = low_half()
    for start in range(0, BLOCK, ROWS):
        parts = separation(col_ref, right, row_ref, left, start, -1.0)
        soft, margin = envelope(parts, same, start)
        inverse = 1.0 / soft
        u = [part * inverse for part in parts]
        z = centered(soft)
        bell = jnp.exp2(-z * (z + jnp.where(low_lanes, (BASIS - 1) * STEP, (BASIS - 3) * STEP)))
        bell = bell * (margin * margin)
        growth = jnp.exp2((4.0 * STEP) * z)
        for pair in range(BASIS // 2):
            for order in range(4):
                high, low = split(bell if order == 0 else bell * u[order - 1])
                here = pl.ds(order * BLOCK + start, ROWS)
                high_ref[here, pair * 128 : pair * 128 + 128] = high
                low_ref[here, pair * 128 : pair * 128 + 128] = low
            bell = bell * growth


def pair_backward(col_ref, left, row_ref, right, same, pull_ref):
    low_lanes = low_half()
    lane = iota((1, 128), 1)
    sums = [jnp.zeros((1, 128), F32) for _ in range(3)]
    columns = []
    for start in range(0, BLOCK, ROWS):
        parts = separation(col_ref, left, row_ref, right, start, 1.0)
        soft, margin = envelope(parts, same, start)
        inverse = 1.0 / soft
        first, second = angular(parts, inverse)
        z = centered(soft)
        bell = jnp.exp2(-z * (z - (BASIS - 1) * STEP))
        shrink = jnp.exp2((-2.0 * STEP) * z)
        by_first = jnp.zeros((ROWS, 128), F32)
        by_second = jnp.zeros((ROWS, 128), F32)
        count_first = jnp.zeros((ROWS, 128), F32)
        count_second = jnp.zeros((ROWS, 128), F32)
        for n in reversed(range(BASIS)):
            here = pl.ds(n * BLOCK + start, ROWS)
            by_first = by_first + bell * pull_ref[here, 0:128]
            by_second = by_second + bell * pull_ref[here, 128:256]
            if n > 0:
                count_first = count_first + by_first
                count_second = count_second + by_second
                bell = bell * shrink
        weight = margin * margin
        by_bell = first * by_first + second * by_second
        by_count = first * count_first + second * count_second
        by_bell = by_bell + pltpu.roll(by_bell, BLOCK, 1)
        by_count = by_count + pltpu.roll(by_count, BLOCK, 1)
        by_shift = (ROOT * (soft - 1.0) * by_bell - STEP * by_count) * weight
        by_first, by_second = by_first * weight, by_second * weight
        turned = pltpu.roll(by_second, BLOCK, 1)
        by_u = [
            jnp.where(low_lanes, pltpu.roll(by_first, BLOCK, 1), by_first),
            jnp.where(low_lanes, by_second, turned),
            jnp.where(low_lanes, turned, by_second),
        ]
        along = (by_u[0] * parts[0] + by_u[1] * parts[1] + by_u[2] * parts[2]) * inverse
        by_soft = by_shift * (-4.0 / ROOT) - along * inverse
        radial_part = by_soft * inverse + by_bell * (margin * (-4.0 * CUT_INV))
        column = jnp.zeros((ROWS, 128), F32)
        for a in range(3):
            force = by_u[a] * inverse + parts[a] * radial_part
            sums[a] = sums[a] + jnp.sum(force, axis=0, keepdims=True)
            total = jnp.sum(jnp.where(low_lanes, force, 0.0), axis=1, keepdims=True)
            column = jnp.where(lane == a, total, column)
        columns.append(column)
    return (
        jnp.concatenate(sums + [jnp.zeros((5, 128), F32)], axis=0),
        jnp.concatenate(columns, axis=0),
    )


def kind_table(col_ref, block):
    kind = col_ref[block_rows(block), 3:4].astype(jnp.int32)
    lane = iota((BLOCK, 128), 1)
    hit = kind == lane % SPAN
    return jnp.concatenate(
        [
            jnp.where(jnp.logical_and(hit, lane // SPAN % 4 == order), 1.0, 0.0)
            for order in range(4)
        ],
        axis=0,
    ).astype(BF16)


def parities(control_ref):
    return control_ref[1, 2] == 0, control_ref[2, 2] == 0


def fill_control(control_ref, words_ref, tiles_ref, slots, own_blocks):
    row, lane = iota((8, 128), 0), iota((8, 128), 1)
    live = words_ref[0, 0]
    table = jnp.where(lane < 2, tiles_ref[...], 0)
    lengths = [jnp.int32(0), jnp.int32(0)]
    for slot in range(2, slots):
        left, right = tiles_ref[slot, 0], tiles_ref[slot, 1]
        for which in range(2):
            ghost = which == 0
            sending = right - own_blocks if ghost else right
            member = (slot < live) & ((right >= own_blocks) if ghost else (right < own_blocks))
            first = 3 + 3 * which
            entry = jnp.where(lane == first, slot, jnp.where(lane == first + 1, left, sending))
            place = (lane >= first) & (lane < first + 3) & (row == lengths[which]) & member
            table = jnp.where(place, entry, table)
            lengths[which] = lengths[which] + member.astype(jnp.int32)
    for place, word in enumerate([live, words_ref[0, 1], words_ref[0, 2], *lengths]):
        table = jnp.where((lane == 2) & (row == place), word, table)
    control_ref[...] = table


def listed_tiles(control_ref, which, work):
    first = 3 + 3 * which
    count = control_ref[3 + which, 2]

    def entry(place):
        return tuple(control_ref[place, first + k] for k in range(3))

    def step(half, carried):
        work([entry(2 * half), entry(2 * half + 1)])
        return carried

    lax.fori_loop(0, count // 2, step, 0)

    @pl.when(count % 2 == 1)
    def _():
        work([entry(count - 1)])


def own_tiles(control_ref, work):
    listed_tiles(control_ref, 1, work)


def ghost_tiles(control_ref, work):
    work([(slot, control_ref[slot, 0], slot) for slot in range(2)])
    listed_tiles(control_ref, 0, work)


def exact_pick(rows, chosen):
    high = rows.astype(BF16).astype(F32)
    rest = rows - high
    middle = rest.astype(BF16).astype(F32)
    stacked = jnp.concatenate(
        [high, middle, rest - middle, jnp.zeros_like(rows)], axis=0
    ).astype(BF16)
    picked = mm(stacked, chosen)
    return picked[0:8] + picked[8:16] + picked[16:24]


def fetch(pairs, sems):
    copies = [
        pltpu.make_async_copy(source, target, sems.at[i]) for i, (source, target) in enumerate(pairs)
    ]
    for copy in copies:
        copy.start()
    return copies


def pack_kernel(
    frac_in,
    kind_in,
    send_in,
    tile_in,
    site_ref,
    out_ref,
    send_ref,
    tiles_ref,
    frac_ref,
    kind_ref,
    tile_ref,
    sems,
):
    copies = fetch(
        (
            (frac_in, frac_ref),
            (kind_in, kind_ref),
            (send_in, send_ref),
            (tile_in, tile_ref),
        ),
        sems,
    )
    for copy in copies:
        copy.wait()
    atoms = frac_ref.shape[1]
    rows = jnp.concatenate(
        [frac_ref[...], kind_ref[...].astype(F32), jnp.zeros((4, atoms), F32)], axis=0
    )
    site_ref[...] = rows
    out_ref[...] = exact_pick(rows, chooser(send_ref[...], atoms).astype(F32).astype(BF16))
    slots = tile_ref.shape[1]
    lines = jnp.concatenate([tile_ref[...].astype(F32), jnp.zeros((2, 128 - slots), F32)], axis=1)
    lines = jnp.concatenate([lines, jnp.zeros((126, 128), F32)], axis=0)
    tiles_ref[...] = lines.T[0:8].astype(jnp.int32)


def doubled(rows, block):
    chunk = rows[:, block // 2 * 128 : block // 2 * 128 + 128]
    turned = pltpu.roll(chunk, BLOCK, 1)
    low = low_half()
    return jnp.where(low, chunk, turned) if block % 2 == 0 else jnp.where(low, turned, chunk)


def upright(rows):
    return jnp.concatenate([rows, jnp.zeros((120, rows.shape[1]), F32)], axis=0).T


def radial_row(weight_ref, path, n):
    row = SPAN + path * BASIS + n
    return weight_ref[row : row + 1, :]


def readout_row(weight_ref):
    row = SPAN + 4 * BASIS
    return weight_ref[row : row + 1, :]


def axis_scale():
    row = iota((8, 128), 0)
    return jnp.where(row < 2, WIDTHS[0], jnp.where(row == 2, WIDTHS[2], 1.0))


def add_histograms(tiles, col_ref, row_ref, own, kind_ref, hist_ref, pair_high, pair_low):
    for slot, left, right in tiles:
        same = left == right if own else False
        pair_forward(col_ref, left, row_ref, right, same, pair_high.at[slot], pair_low.at[slot])
    tables = [kind_table(kind_ref, right) for _, _, right in tiles]
    found = [
        mm(pair_high[slot], table) + mm(pair_low[slot], table)
        for (slot, _, _), table in zip(tiles, tables)
    ]
    lane_basis = iota((1, 128), 1) // (4 * SPAN)
    for (_, left, _), one in zip(tiles, found):
        for half in range(2):
            total = jnp.zeros((BLOCK, 128), F32)
            for n in range(4):
                begin = (half * 4 + n) * BLOCK
                total = jnp.where(lane_basis == n, one[begin : begin + BLOCK], total)
            hist_ref[block_rows(left), half * 128 : half * 128 + 128] += total


def prepare_kernel(
    words_ref,
    tiles_ref,
    site_ref,
    send_ref,
    control_ref,
    col_ref,
    row_ref,
    hist_ref,
    pair_high,
    pair_low,
    chosen_ref,
):
    atoms = site_ref.shape[1]
    blocks = atoms // BLOCK
    fill_control(control_ref, words_ref, tiles_ref, pair_high.shape[0], blocks)
    own = site_ref[...] * axis_scale()[:, 0:1]
    col_ref[...] = upright(own)
    for block in range(blocks):
        row_ref[block] = doubled(own, block)
    chosen_ref[...] = chooser(send_ref[...], atoms).astype(F32).astype(BF16)
    hist_ref[...] = jnp.zeros_like(hist_ref)

    own_tiles(
        control_ref,
        lambda tiles: add_histograms(
            tiles, col_ref, row_ref, True, col_ref, hist_ref, pair_high, pair_low
        ),
    )


def fold_kernel(
    embed_in,
    radial_in,
    readout_in,
    mixing_in,
    fold_high,
    fold_low,
    mix_high,
    mix_low,
    weight_ref,
    fold_ref,
    mixing_ref,
    sems,
):
    kinds = embed_in.shape[0]
    paths = radial_in.shape[0]
    copies = fetch(
        (
            (embed_in, weight_ref.at[pl.ds(0, kinds)]),
            (radial_in, weight_ref.at[pl.ds(SPAN, paths)]),
            (readout_in, weight_ref.at[pl.ds(SPAN + paths, 1)]),
            (mixing_in, mixing_ref),
        ),
        sems,
    )
    for copy in copies:
        copy.wait()

    radial = weight_ref[SPAN : SPAN + paths, :]
    weight_ref[SPAN : SPAN + paths, :] = radial * basis_scale(radial.shape)

    embed = jnp.where(iota((SPAN, 128), 0) < kinds, weight_ref[0:SPAN, :], 0.0)
    scalar = jnp.concatenate([radial_row(weight_ref, 0, n) * embed for n in range(BASIS)], axis=0)
    vector = jnp.concatenate([radial_row(weight_ref, 1, n) * embed for n in range(BASIS)], axis=0)
    scalar, vector = split(scalar), split(vector)
    to_self = mm3(scalar, split(mixing_ref[0]))
    to_gate = mm3(scalar, split(mixing_ref[2]))
    to_vector = mm3(vector, split(mixing_ref[1]))
    fold_ref[...] = jnp.zeros_like(fold_ref)
    for n in range(BASIS):
        rows = slice(n * SPAN, n * SPAN + SPAN)
        base = n * 4 * SPAN
        fold_ref[base : base + SPAN, 0:128] = to_self[rows]
        fold_ref[base : base + SPAN, 128:256] = to_gate[rows]
        for a in range(3):
            here = base + (a + 1) * SPAN
            fold_ref[here : here + SPAN, (a + 2) * 128 : (a + 3) * 128] = to_vector[rows]
    fold_high[...], fold_low[...] = split(fold_ref[...])
    for part in range(2):
        mix_high[part], mix_low[part] = split(mixing_ref[3 + part])


def first_kernel(
    control_ref,
    send_in,
    hist_in,
    col_ref,
    mate_in,
    far_in,
    zmate_in,
    zfar_in,
    hist_ref,
    mate_ref,
    far_ref,
    side_ref,
    ghost_col,
    ghost_row,
    pair_high,
    pair_low,
    send_ref,
    sem,
):
    fetching = pltpu.make_async_copy(send_in, send_ref, sem)
    fetching.start()
    even_x, even_y = parities(control_ref)
    ghosts = pick_rows(even_x, even_y, mate_in[...], far_in[...], zmate_in[...], zfar_in[...])
    row = iota((8, 128), 0)
    slot = iota((8, 128), 1) // GHOSTS
    shift_x = jnp.where(slot < 3, -1.0, jnp.where(slot < 5, 0.0, 1.0))
    down = (slot == 0) | (slot == 3) | (slot == 5)
    level = (slot == 1) | (slot == 6)
    shift_y = jnp.where(down, -1.0, jnp.where(level, 0.0, 1.0))
    shift = jnp.where(row == 0, shift_x, jnp.where(row == 1, shift_y, 0.0))
    ghosts = (ghosts + shift) * axis_scale()
    ghost_col[...] = upright(ghosts)
    for block in range(2):
        ghost_row[block] = doubled(ghosts, block)
    hist_ref[...] = hist_in[...]

    ghost_tiles(
        control_ref,
        lambda tiles: add_histograms(
            tiles, col_ref, ghost_row, False, ghost_col, hist_ref, pair_high, pair_low
        ),
    )
    fetching.wait()

    up, down = jnp.where(even_x, 5, 0), jnp.where(even_x, 0, 5)
    places = [(mate_ref, part, up + part) for part in range(3)]
    places += [(far_ref, part, down + part) for part in range(3)]
    places += [(side_ref, part, 3 + part) for part in range(2)]
    for ref, part, slot in places:
        for entry in range(GHOSTS):
            ref[part, entry : entry + 1, :] = hist_ref[pl.ds(send_ref[slot, entry], 1), :]


def make_features(block, col_ref, kinds, weight_ref, pre_ref, feat_high, feat_low, scalar_ref):
    rows = block_rows(block)
    kind = col_ref[rows, 3:4].astype(jnp.int32)
    scalar = jnp.zeros((BLOCK, 128), F32)
    for species in range(kinds):
        scalar = jnp.where(kind == species, weight_ref[species : species + 1, :], scalar)
    pre = pre_ref[rows, 0:128]
    scalar = scalar + pre * sigmoid(pre)
    if scalar_ref is not None:
        scalar_ref[rows, :] = scalar
    gate = sigmoid(pre_ref[rows, 128:256])
    parts = [scalar] + [pre_ref[rows, (a + 2) * 128 : (a + 3) * 128] * gate for a in range(3)]
    empty = jnp.zeros((BLOCK, 128), BF16)
    for order, part in enumerate(parts):
        high, low = split(part)
        here = pl.ds(order * BLOCK, BLOCK)
        used = 0 if order == 0 else 128
        for ref, value in ((feat_high, high), (feat_low, low)):
            ref[block, here, used : used + 128] = value
            ref[block, here, 128 - used : 256 - used] = empty


def add_messages(tiles, feat_high, feat_low, weight_ref, message_ref, pair_high, pair_low):
    found = [
        mm3((pair_high[slot], pair_low[slot]), (feat_high[right], feat_low[right]))
        for slot, _, right in tiles
    ]
    for (_, left, _), one in zip(tiles, found):
        total = jnp.zeros((BLOCK, 128), F32)
        for n in range(BASIS):
            rows = slice(n * BLOCK, n * BLOCK + BLOCK)
            total = total + one[rows, 0:128] * radial_row(weight_ref, 2, n)
            total = total + one[rows, 128:256] * radial_row(weight_ref, 3, n)
        message_ref[block_rows(left), :] += total


def feature_kernel(
    kinds,
    hist_ref,
    col_ref,
    fold_high,
    fold_low,
    weight_ref,
    pre_ref,
    feat_high,
    feat_low,
    scalar_ref,
):
    blocks = hist_ref.shape[0] // BLOCK
    pre_ref[...] = mm3(split(hist_ref[...]), (fold_high[...], fold_low[...]))

    def features(block, carried):
        make_features(block, col_ref, kinds, weight_ref, pre_ref, feat_high, feat_low, scalar_ref)
        return carried

    lax.fori_loop(0, blocks, features, 0)


def message_kernel(
    control_ref,
    row_ref,
    ghost_col,
    weight_ref,
    feat_high,
    feat_low,
    pair_high,
    pair_low,
    message_ref,
    swap_high,
    swap_low,
):
    blocks = feat_high.shape[0]
    message_ref[...] = jnp.zeros_like(message_ref)

    own_tiles(
        control_ref,
        lambda tiles: add_messages(
            tiles, feat_high, feat_low, weight_ref, message_ref, pair_high, pair_low
        ),
    )

    def swapped(tiles):
        for slot, left, right in tiles:
            pair_swapped(
                ghost_col, right, row_ref, left, False, swap_high.at[slot], swap_low.at[slot]
            )

    ghost_tiles(control_ref, swapped)


def weighted_pull(cotangent, weight_ref, path):
    return split(
        jnp.concatenate([cotangent * radial_row(weight_ref, path, n) for n in range(BASIS)], axis=0)
    )


def add_feature_pulls(tiles, places, pull_message, weight_ref, grad_feat, swap_high, swap_low):
    weighted = []
    for _, left, _ in tiles:
        cotangent = pull_message[block_rows(left), :]
        weighted.append([weighted_pull(cotangent, weight_ref, path) for path in (2, 3)])
    found = []
    for place, (by_scalar, by_vector) in zip(places, weighted):
        high, low = swap_high.at[place], swap_low.at[place]
        to_scalar = mm3((high[0:BLOCK, :], low[0:BLOCK, :]), by_scalar)
        to_vector = mm3((high[BLOCK:, :], low[BLOCK:, :]), by_vector)
        found.append((to_scalar, to_vector))
    for (_, _, right), (to_scalar, to_vector) in zip(tiles, found):
        rows = block_rows(right)
        grad_feat[rows, 0:128] += to_scalar
        for a in range(3):
            here = slice(a * BLOCK, (a + 1) * BLOCK)
            grad_feat[rows, (a + 1) * 128 : (a + 2) * 128] += to_vector[here]


def finish(message, scalar, mix_high, mix_low, weight_ref):
    mix_message, mix_hidden = (mix_high[0], mix_low[0]), (mix_high[1], mix_low[1])
    readout = readout_row(weight_ref)
    mixed = mm3(split(message), mix_message)
    mixed_gate = sigmoid(mixed)
    final = scalar + mixed * mixed_gate
    hidden = mm3(split(final), mix_hidden)
    hidden_gate = sigmoid(hidden)
    pull_hidden = readout * (hidden_gate * (1.0 + hidden * (1.0 - hidden_gate)))
    pull_final = mm3(split(pull_hidden), mix_hidden, ROWROW)
    pull_mixed = pull_final * (mixed_gate * (1.0 + mixed * (1.0 - mixed_gate)))
    pull_message = mm3(split(pull_mixed), mix_message, ROWROW)
    return hidden * hidden_gate * readout, pull_final, pull_message


def pull_features(grad_feat, pre_ref):
    by_scalar = grad_feat[:, 0:128]
    pre = pre_ref[:, 0:128]
    own_gate = sigmoid(pre)
    gate = sigmoid(pre_ref[:, 128:256])
    by_gate = jnp.zeros_like(gate)
    by_vector = []
    for a in range(3):
        pulled = grad_feat[:, (a + 1) * 128 : (a + 2) * 128]
        by_gate = by_gate + pulled * pre_ref[:, (a + 2) * 128 : (a + 3) * 128]
        by_vector.append(pulled * gate)
    by_pre = by_scalar * (own_gate * (1.0 + pre * (1.0 - own_gate)))
    return jnp.concatenate([by_pre, by_gate * gate * (1.0 - gate)] + by_vector, axis=1)


def second_ghost_kernel(
    kinds,
    control_ref,
    mate_in,
    far_in,
    zmate_in,
    zfar_in,
    ghost_col,
    fold_high,
    fold_low,
    mix_high,
    mix_low,
    weight_ref,
    scalar_ref,
    message_in,
    pair_high,
    pair_low,
    swap_high,
    swap_low,
    mate_ref,
    far_ref,
    side_ref,
    feat_high,
    feat_low,
    pull_message,
    direct_ref,
    share_ref,
    message_ref,
    pre_ref,
    grad_feat,
):
    even_x, even_y = parities(control_ref)
    fold = (fold_high[...], fold_low[...])
    ghost_hist = pick_all((even_x, even_y, mate_in, far_in, zmate_in, zfar_in))
    pre_ref[...] = mm3(split(ghost_hist), fold)
    for block in range(2):
        make_features(block, ghost_col, kinds, weight_ref, pre_ref, feat_high, feat_low, None)
    message_ref[...] = message_in[...]

    ghost_tiles(
        control_ref,
        lambda tiles: add_messages(
            tiles, feat_high, feat_low, weight_ref, message_ref, pair_high, pair_low
        ),
    )

    share_ref[...], direct_ref[...], pull_message[...] = finish(
        message_ref[...], scalar_ref[...], mix_high, mix_low, weight_ref
    )
    grad_feat[...] = jnp.zeros_like(grad_feat)

    ghost_tiles(
        control_ref,
        lambda tiles: add_feature_pulls(
            tiles, [slot for slot, _, _ in tiles], pull_message, weight_ref, grad_feat,
            swap_high, swap_low,
        ),
    )

    ghost_pull = mm3(split(pull_features(grad_feat, pre_ref)), fold, ROWROW)
    put_packets(
        even_x,
        lambda slot: ghost_pull[slot * GHOSTS : slot * GHOSTS + GHOSTS],
        mate_ref,
        far_ref,
        side_ref,
    )


def second_pull_kernel(
    control_ref,
    col_ref,
    row_ref,
    weight_ref,
    pull_message,
    direct_ref,
    grad_feat,
    swap_high,
    swap_low,
):
    grad_feat[:, 0:128] = direct_ref[...]
    grad_feat[:, 128:512] = jnp.zeros((direct_ref.shape[0], 384), F32)

    def backward(tiles):
        for place, (_, left, right) in enumerate(tiles):
            pair_swapped(
                col_ref, right, row_ref, left, left == right,
                swap_high.at[place], swap_low.at[place],
            )
        add_feature_pulls(
            tiles, range(len(tiles)), pull_message, weight_ref, grad_feat, swap_high, swap_low
        )

    own_tiles(control_ref, backward)


def pair_pulls(tiles, pull_message, weight_ref, high_ref, low_ref, pull_ref):
    weighted = []
    for _, left, _ in tiles:
        cotangent = pull_message[block_rows(left), :]
        first = weighted_pull(cotangent, weight_ref, 2)
        second = weighted_pull(cotangent, weight_ref, 3)
        weighted.append(
            [jnp.concatenate([first[part], second[part]], axis=1) for part in range(2)]
        )
    found = [
        mm3(one, (high_ref[right], low_ref[right]), ROWROW)
        for one, (_, _, right) in zip(weighted, tiles)
    ]
    for one, (slot, _, _) in zip(found, tiles):
        pull_ref[slot] = one


def ghost_pair_kernel(
    control_ref,
    fold_high,
    fold_low,
    weight_ref,
    pre_ref,
    grad_feat,
    pull_message,
    ghost_high,
    ghost_low,
    pull_hist_ref,
    pull_ref,
):
    pulled = pull_features(grad_feat, pre_ref)
    pull_hist_ref[...] = mm3(split(pulled), (fold_high[...], fold_low[...]), ROWROW)

    ghost_tiles(
        control_ref,
        lambda tiles: pair_pulls(tiles, pull_message, weight_ref, ghost_high, ghost_low, pull_ref),
    )


def own_pair_kernel(
    control_ref, weight_ref, pull_message, share_ref, feat_high, feat_low, pull_ref, energy_ref
):
    energy_ref[...] = jnp.sum(share_ref[...].T, axis=0, keepdims=True)

    own_tiles(
        control_ref,
        lambda tiles: pair_pulls(tiles, pull_message, weight_ref, feat_high, feat_low, pull_ref),
    )


def add_position_pulls(
    tiles, total_ref, kind_ref, col_ref, row_ref, own, pull_in, pull_refs, grad_row, grad_col
):
    lane_basis = iota((1, 128), 1) // (4 * SPAN)
    built = []
    for _, left, right in tiles:
        parts = []
        for half in range(2):
            here = total_ref[block_rows(left), half * 128 : half * 128 + 128]
            parts += [jnp.where(lane_basis == n, here, 0.0) for n in range(4)]
        high, low = split(jnp.concatenate(parts, axis=0))
        table = kind_table(kind_ref, right)
        built.append(
            (jnp.concatenate([high, low], axis=1), jnp.concatenate([table, table], axis=1))
        )
    found = [mm(both, table, ROWROW) for both, table in built]
    for place, ((slot, _, _), one) in enumerate(zip(tiles, found)):
        pull_refs[place] = pull_in[slot] + one
    grads = [
        pair_backward(
            col_ref, left, row_ref, right, left == right if own else False, pull_refs.at[place]
        )
        for place, (_, left, right) in enumerate(tiles)
    ]
    for (_, left, right), (by_row, by_col) in zip(tiles, grads):
        grad_row[right] += by_row
        grad_col[block_rows(left), :] -= by_col


def third_ghost_kernel(
    control_ref,
    chosen_ref,
    pull_hist_ref,
    mate_in,
    far_in,
    zmate_in,
    zfar_in,
    col_ref,
    ghost_col,
    ghost_row,
    pull_in,
    out_ref,
    total_ref,
    grad_col,
    grad_ghost,
    pull_refs,
):
    even_x, even_y = parities(control_ref)
    returned = split(pick_all((even_x, even_y, mate_in, far_in, zmate_in, zfar_in)))
    chosen = chosen_ref[...]
    total_ref[...] = pull_hist_ref[...] + mm(chosen, returned[0]) + mm(chosen, returned[1])
    grad_ghost[...] = jnp.zeros_like(grad_ghost)
    grad_col[...] = jnp.zeros_like(grad_col)

    ghost_tiles(
        control_ref,
        lambda tiles: add_position_pulls(
            tiles, total_ref, ghost_col, col_ref, ghost_row, False, pull_in, pull_refs,
            grad_ghost, grad_col,
        ),
    )
    out_ref[...] = jnp.where(low_half(), grad_ghost[0], grad_ghost[1])


def third_own_kernel(
    control_ref,
    chosen_ref,
    total_ref,
    col_ref,
    row_ref,
    pull_in,
    grad_col_in,
    own_ref,
    turned_ref,
    grad_row,
    grad_col,
    pull_refs,
):
    blocks = total_ref.shape[0] // BLOCK
    turned_ref[...] = chosen_ref[...].astype(F32).T.astype(BF16)
    grad_row[...] = jnp.zeros_like(grad_row)
    grad_col[...] = grad_col_in[...]

    own_tiles(
        control_ref,
        lambda tiles: add_position_pulls(
            tiles, total_ref, col_ref, col_ref, row_ref, True, pull_in, pull_refs,
            grad_row, grad_col,
        ),
    )
    low = low_half()
    by_sender = jnp.concatenate(
        [jnp.where(low, grad_row[2 * k], grad_row[2 * k + 1]) for k in range(blocks // 2)], axis=1
    )
    own_ref[...] = by_sender + grad_col[...].T[0:8]


def last_kernel(control_ref, turned_ref, own_ref, mate_in, far_in, zmate_in, zfar_in, force_ref):
    even_x, even_y = parities(control_ref)
    returned = pick_rows(even_x, even_y, mate_in[...], far_in[...], zmate_in[...], zfar_in[...])
    total = own_ref[...] + exact_pick(returned, turned_ref[...])
    force_ref[...] = -total[0:3]


def partners(axis, far):
    count = lax.axis_size(axis)
    if far:
        return [(i, (i + (1 if i % 2 else -1)) % count) for i in range(count)]
    return [(i, i ^ 1) for i in range(count)]


def swap_both(axis, to_mate, to_far):
    to_far, to_mate = lax.optimization_barrier((to_far, to_mate))
    far = lax.ppermute(to_far, axis, partners(axis, True))
    mate = lax.ppermute(to_mate, axis, partners(axis, False))
    far, mate = lax.optimization_barrier((far, mate))
    return mate, far


def exchange_rows(rows, beside):
    mate, far = swap_both("gx", rows, rows)
    far, mate, beside = lax.optimization_barrier((far, mate, beside))
    column = jnp.stack([rows, mate, far])
    zmate, zfar = swap_both("gy", column, column)
    return (mate, far, zmate, zfar), beside


def exchange_packets(even_y, to_mate, to_far, side, beside):
    mate, far = swap_both("gx", to_mate, to_far)
    far, mate, beside = lax.optimization_barrier((far, mate, beside))
    up = jnp.concatenate([mate[2:3], far[2:3], side[1:2]], axis=0)
    down = jnp.concatenate([mate[0:1], far[0:1], side[0:1]], axis=0)
    zmate, zfar = swap_both("gy", jnp.where(even_y, up, down), jnp.where(even_y, down, up))
    return (mate, far, zmate, zfar), beside


def struct(*shape, dtype=F32):
    return jax.ShapeDtypeStruct(shape, dtype)


def call(kernel, in_specs, outs, scratch=()):
    made = pl.pallas_call(
        kernel,
        in_specs=in_specs,
        out_specs=jax.tree.map(lambda _: VMEM, outs),
        out_shape=outs,
        scratch_shapes=list(scratch),
        compiler_params=PARAMS,
    )

    def run(*args):
        placed = [
            pltpu.with_memory_space_constraint(arg, pltpu.HBM if spec is HBM else pltpu.VMEM)
            for arg, spec in zip(args, in_specs, strict=True)
        ]
        return made(*placed)

    return run


def shards(fractions, species, send_list, tile_list, counts, embedding, radial, mixing, readout):
    atoms = fractions.shape[1]
    blocks = atoms // BLOCK
    kinds = embedding.shape[0]
    slots = tile_list.shape[1]
    parity = [lax.axis_index("gx") % 2, lax.axis_index("gy") % 2]
    even_y = parity[1] == 0
    words = jnp.stack([counts[0], *parity]).astype(jnp.int32)[None]
    far_arrays = (
        fractions,
        species[None],
        send_list,
        tile_list,
        embedding,
        radial.reshape(-1, radial.shape[2]),
        readout[None],
        mixing,
    )
    packets = [struct(3, GHOSTS, HIST), struct(3, GHOSTS, HIST), struct(2, GHOSTS, HIST)]
    hist_struct = struct(atoms, HIST)
    col_struct = struct(atoms, 128)
    own_rows, ghost_rows = struct(blocks, 8, 128), struct(2, 8, 128)
    fold_halves = [struct(HIST, 640, dtype=BF16)] * 2
    mix_halves = [struct(2, 128, 128, dtype=BF16)] * 2
    own_halves = [struct(blocks, 256, 256, dtype=BF16)] * 2
    ghost_halves = [struct(2, 256, 256, dtype=BF16)] * 2
    pairs = [struct(slots, BASIS * BLOCK, 256, dtype=BF16)] * 2
    swaps = [struct(slots, 256, BASIS * BLOCK, dtype=BF16)] * 2
    pulls = struct(slots, BASIS * BLOCK, 256)

    site, rows, send, tiles = call(
        pack_kernel,
        [HBM] * 4,
        [
            struct(8, atoms), struct(8, 128),
            struct(*send_list.shape, dtype=jnp.int32), struct(8, 128, dtype=jnp.int32),
        ],
        [
            pltpu.VMEM(fractions.shape, F32),
            pltpu.VMEM((1, atoms), jnp.int32),
            pltpu.VMEM(tile_list.shape, jnp.int32),
            pltpu.SemaphoreType.DMA((4,)),
        ],
    )(*far_arrays[0:4])
    folded = call(
        fold_kernel,
        [HBM] * 4,
        fold_halves + mix_halves + [struct(2 * SPAN + 4 * BASIS, 128)],
        [
            pltpu.VMEM((HIST, 640), F32),
            pltpu.VMEM(mixing.shape, F32),
            pltpu.SemaphoreType.DMA((4,)),
        ],
    )(*far_arrays[4:])
    arrived, (words, site, folded) = exchange_rows(rows, (words, site, folded))
    fold_high, fold_low, mix_high, mix_low, weights = folded
    fold, mix = (fold_high, fold_low), (mix_high, mix_low)
    control, col, row, hist, own_high, own_low, chosen = call(
        prepare_kernel,
        [VMEM] * 4,
        [struct(8, 128, dtype=jnp.int32), col_struct, own_rows, hist_struct]
        + pairs
        + [struct(atoms, 128, dtype=BF16)],
    )(words, tiles, site, send)
    hist, to_mate, to_far, side, ghost_col, ghost_row, pair_high, pair_low = call(
        first_kernel,
        [VMEM] * 8,
        [hist_struct] + packets + [struct(8 * GHOSTS, 128), ghost_rows] + pairs,
        [pltpu.SMEM(send_list.shape, jnp.int32), pltpu.SemaphoreType.DMA],
    )(control, send, hist, col, *arrived)
    features = call(
        functools.partial(feature_kernel, kinds),
        [VMEM] * 5,
        [struct(atoms, 640)] + own_halves + [col_struct],
    )(hist, col, *fold, weights)
    arrived, features = exchange_packets(even_y, to_mate, to_far, side, features)
    pre, feat_high, feat_low, scalar = features
    message, swap_high, swap_low = call(message_kernel, [VMEM] * 8, [col_struct] + swaps)(
        control, row, ghost_col, weights, feat_high, feat_low, own_high, own_low
    )
    (
        to_mate, to_far, side, ghost_high, ghost_low, pull_message, direct, share,
    ) = call(
        functools.partial(second_ghost_kernel, kinds),
        [VMEM] * 17,
        packets + ghost_halves + [col_struct] * 3,
        [
            pltpu.VMEM((atoms, 128), F32),
            pltpu.VMEM((8 * GHOSTS, 640), F32),
            pltpu.VMEM((8 * GHOSTS, 512), F32),
        ],
    )(
        control, *arrived, ghost_col, *fold, *mix, weights, scalar, message,
        pair_high, pair_low, swap_high, swap_low,
    )
    grad_feat = call(
        second_pull_kernel,
        [VMEM] * 6,
        struct(atoms, 512),
        [pltpu.VMEM((2, 256, BASIS * BLOCK), BF16)] * 2,
    )(control, col, row, weights, pull_message, direct)
    arrived, grad_feat = exchange_packets(even_y, to_mate, to_far, side, grad_feat)
    pull_hist, pull = call(ghost_pair_kernel, [VMEM] * 9, [hist_struct, pulls])(
        control, *fold, weights, pre, grad_feat, pull_message, ghost_high, ghost_low
    )
    rows, total, grad_col = call(
        third_ghost_kernel,
        [VMEM] * 11,
        [struct(8, 128), hist_struct, col_struct],
        [pltpu.VMEM((2, 8, 128), F32), pltpu.VMEM((2, BASIS * BLOCK, 256), F32)],
    )(control, chosen, pull_hist, *arrived, col, ghost_col, ghost_row, pull)
    share, rows = lax.optimization_barrier((share, rows))
    own_pair = call(own_pair_kernel, [VMEM] * 6, [pulls, struct(1, atoms)])(
        control, weights, pull_message, share, feat_high, feat_low
    )
    arrived, own_pair = exchange_rows(rows, own_pair)
    pull, energy = own_pair
    own, turned = call(
        third_own_kernel,
        [VMEM] * 7,
        [struct(8, atoms), struct(128, atoms, dtype=BF16)],
        [
            pltpu.VMEM((blocks, 8, 128), F32),
            pltpu.VMEM((atoms, 128), F32),
            pltpu.VMEM((2, BASIS * BLOCK, 256), F32),
        ],
    )(control, chosen, total, col, row, pull, grad_col)
    forces = call(last_kernel, [VMEM] * 7, struct(3, atoms))(control, turned, own, *arrived)
    return energy[0], forces


def solution(mesh):
    placed = (
        P(None, ("gx", "gy")),
        P(("gx", "gy")),
        P(None, ("gx", "gy")),
        P(None, ("gx", "gy")),
        P(("gx", "gy")),
        P(),
        P(),
        P(),
        P(),
    )
    return jax.shard_map(
        shards,
        mesh=mesh,
        in_specs=placed,
        out_specs=(P(("gx", "gy")), P(None, ("gx", "gy"))),
        check_vma=False,
    )
```

```python
import functools

import jax
import jax.numpy as jnp
from jax import lax
from jax.experimental import pallas as pl
from jax.experimental.pallas import tpu as pltpu
from jax.sharding import PartitionSpec as P

F32 = jnp.float32
BF16 = jnp.bfloat16

BASIS = 8
BLOCK = 64
GHOSTS = 16
SPAN = 8
HIST = BASIS * 4 * SPAN
OFFSETS = ((-1, -1), (-1, 0), (-1, 1), (0, -1), (0, 1), (1, -1), (1, 0), (1, 1))
WIDTHS = (12.0, 12.0, 36.0)
CUT_INV = 1.0 / 25.0
ROOT = 1.6986436005760381
STEP = ROOT * 0.6
MIDDLE = 1.0 + 0.6 * (BASIS - 1) / 2
REACH = 5.125
ROWS = 32

VMEM = pl.BlockSpec(memory_space=pltpu.VMEM)
HBM = pl.BlockSpec(memory_space=pltpu.HBM)
PARAMS = pltpu.CompilerParams(vmem_limit_bytes=16 * 1024 * 1024)

ROWROW = (((1,), (1,)), ((), ()))
ROWCOL = (((1,), (0,)), ((), ()))


def split(value):
    high = value.astype(BF16)
    return high, (value - high.astype(F32)).astype(BF16)


def mm(left, right, dims=ROWCOL):
    return lax.dot_general(left, right, dims, preferred_element_type=F32)


def mm3(left, right, dims=ROWCOL):
    (lh, ll), (rh, rl) = left, right
    summed = dims[0][1][0]
    return mm(
        jnp.concatenate([lh, ll, lh], axis=1), jnp.concatenate([rh, rh, rl], axis=summed), dims
    )


def sigmoid(value):
    return 1.0 / (1.0 + jnp.exp(-value))


def iota(shape, dim):
    return lax.broadcasted_iota(jnp.int32, shape, dim)


def low_half():
    return iota((1, 128), 1) < BLOCK


def pick_rows(even_x, even_y, mate, far, zmate, zfar):
    x_up, x_down = jnp.where(even_x, mate, far), jnp.where(even_x, far, mate)
    y_up = [jnp.where(even_y, zmate[i], zfar[i]) for i in range(3)]
    y_down = [jnp.where(even_y, zfar[i], zmate[i]) for i in range(3)]
    sources = {
        (1, 0): x_up,
        (-1, 0): x_down,
        (0, 1): y_up[0],
        (0, -1): y_down[0],
        (1, 1): jnp.where(even_x, y_up[1], y_up[2]),
        (-1, 1): jnp.where(even_x, y_up[2], y_up[1]),
        (1, -1): jnp.where(even_x, y_down[1], y_down[2]),
        (-1, -1): jnp.where(even_x, y_down[2], y_down[1]),
    }
    slot_of = iota((8, 128), 1) // GHOSTS
    total = jnp.zeros((8, 128), F32)
    for slot, offset in enumerate(OFFSETS):
        turned = pltpu.roll(sources[offset], ((2 * slot - 7) * GHOSTS) % 128, 1)
        total = jnp.where(slot_of == slot, turned, total)
    return total


def pick_slot(slot, even_x, even_y, mate, far, zmate, zfar):
    along_x, along_y = OFFSETS[slot]
    if along_y == 0:
        near = even_x if along_x == 1 else jnp.logical_not(even_x)
        return jnp.where(near, mate[1], far[1])
    near = even_y if along_y == 1 else jnp.logical_not(even_y)
    if along_x == 0:
        return jnp.where(near, zmate[2], zfar[2])
    first = even_x if along_x == 1 else jnp.logical_not(even_x)
    return jnp.where(
        near, jnp.where(first, zmate[0], zmate[1]), jnp.where(first, zfar[0], zfar[1])
    )


def pick_all(args):
    return jnp.concatenate([unpack(pick_slot(slot, *args)) for slot in range(8)], axis=0)


def pack(rows):
    free = iota((8, 128), 1) % SPAN >= 6
    carried = rows[8:16, 128:256]
    quarters = (rows[0:8, 0:128], rows[8:16, 0:128], rows[0:8, 128:256])
    return jnp.concatenate(
        [
            jnp.where(free, pltpu.roll(carried, 6 - 2 * part, 1), quarter)
            for part, quarter in enumerate(quarters)
        ],
        axis=0,
    )


def unpack(packet):
    place = iota((8, 128), 1) % SPAN
    turned = [
        pltpu.roll(packet[8 * part : 8 * part + 8], 128 - (6 - 2 * part), 1) for part in range(3)
    ]
    carried = jnp.where(place < 2, turned[0], jnp.where(place < 4, turned[1], turned[2]))
    return jnp.concatenate(
        [packet[0:16], jnp.concatenate([packet[16:24], carried], axis=0)], axis=1
    )


def put_packets(even_x, piece, mate_ref, far_ref, side_ref):
    for part in range(3):
        down, up = pack(piece(part)), pack(piece(5 + part))
        mate_ref[part] = jnp.where(even_x, up, down)
        far_ref[part] = jnp.where(even_x, down, up)
    side_ref[0] = pack(piece(3))
    side_ref[1] = pack(piece(4))


def send_columns(send):
    wide = jnp.concatenate([send] * 8, axis=1)
    own = iota((8, 128), 1) // GHOSTS == iota((8, 128), 0)
    return jnp.sum(jnp.where(own, wide, 0), axis=0, keepdims=True)


def chooser(send, atoms):
    return iota((atoms, 128), 0) == send_columns(send)


def block_rows(block, start=0, count=BLOCK):
    return pl.ds(pl.multiple_of(block * BLOCK, BLOCK) + start, count)


def separation(col_ref, col_block, row_ref, row_block, start, sign):
    mine = col_ref[block_rows(col_block, start, ROWS), :]
    other = row_ref[row_block]
    return [sign * (other[a : a + 1, :] - mine[:, a : a + 1]) for a in range(3)]


def envelope(parts, same, start):
    dist_sq = parts[0] * parts[0] + parts[1] * parts[1] + parts[2] * parts[2]
    soft = jnp.sqrt(dist_sq + 1.0)
    rows = iota((ROWS, 128), 0) + start
    columns = iota((ROWS, 128), 1) % BLOCK
    apart = jnp.where(jnp.logical_and(rows == columns, same), 0.0, 1.0)
    margin = jnp.maximum(1.0 - dist_sq * CUT_INV, 0.0) * apart
    return soft, margin


def angular(parts, inverse):
    u = [part * inverse for part in parts]
    low = low_half()
    return jnp.where(low, 1.0, u[0]), jnp.where(low, u[1], u[2])


def basis_scale(shape):
    step = (iota(shape, 0) % BASIS).astype(F32) - (BASIS - 1) / 2
    return jnp.exp2(-(STEP * STEP) * (step * step))


def centered(soft):
    return ROOT * (jnp.minimum(soft, REACH) - MIDDLE)


def pair_forward(col_ref, left, row_ref, right, same, high_ref, low_ref):
    for start in range(0, BLOCK, ROWS):
        parts = separation(col_ref, left, row_ref, right, start, 1.0)
        soft, margin = envelope(parts, same, start)
        first, second = angular(parts, 1.0 / soft)
        z = centered(soft)
        bell = jnp.exp2(-z * (z + (BASIS - 1) * STEP)) * (margin * margin)
        growth = jnp.exp2((2.0 * STEP) * z)
        for n in range(BASIS):
            here = pl.ds(n * BLOCK + start, ROWS)
            for half, factor in enumerate((first, second)):
                high, low = split(bell * factor)
                high_ref[here, half * 128 : half * 128 + 128] = high
                low_ref[here, half * 128 : half * 128 + 128] = low
            bell = bell * growth


def pair_swapped(col_ref, right, row_ref, left, same, high_ref, low_ref):
    low_lanes = low_half()
    for start in range(0, BLOCK, ROWS):
        parts = separation(col_ref, right, row_ref, left, start, -1.0)
        soft, margin = envelope(parts, same, start)
        inverse = 1.0 / soft
        u = [part * inverse for part in parts]
        z = centered(soft)
        bell = jnp.exp2(-z * (z + jnp.where(low_lanes, (BASIS - 1) * STEP, (BASIS - 3) * STEP)))
        bell = bell * (margin * margin)
        growth = jnp.exp2((4.0 * STEP) * z)
        for pair in range(BASIS // 2):
            for order in range(4):
                high, low = split(bell if order == 0 else bell * u[order - 1])
                here = pl.ds(order * BLOCK + start, ROWS)
                high_ref[here, pair * 128 : pair * 128 + 128] = high
                low_ref[here, pair * 128 : pair * 128 + 128] = low
            bell = bell * growth


def pair_backward(col_ref, left, row_ref, right, same, pull_ref):
    low_lanes = low_half()
    lane = iota((1, 128), 1)
    sums = [jnp.zeros((1, 128), F32) for _ in range(3)]
    columns = []
    for start in range(0, BLOCK, ROWS):
        parts = separation(col_ref, left, row_ref, right, start, 1.0)
        soft, margin = envelope(parts, same, start)
        inverse = 1.0 / soft
        first, second = angular(parts, inverse)
        z = centered(soft)
        bell = jnp.exp2(-z * (z - (BASIS - 1) * STEP))
        shrink = jnp.exp2((-2.0 * STEP) * z)
        by_first = jnp.zeros((ROWS, 128), F32)
        by_second = jnp.zeros((ROWS, 128), F32)
        count_first = jnp.zeros((ROWS, 128), F32)
        count_second = jnp.zeros((ROWS, 128), F32)
        for n in reversed(range(BASIS)):
            here = pl.ds(n * BLOCK + start, ROWS)
            by_first = by_first + bell * pull_ref[here, 0:128]
            by_second = by_second + bell * pull_ref[here, 128:256]
            if n > 0:
                count_first = count_first + by_first
                count_second = count_second + by_second
                bell = bell * shrink
        weight = margin * margin
        by_bell = first * by_first + second * by_second
        by_count = first * count_first + second * count_second
        by_bell = by_bell + pltpu.roll(by_bell, BLOCK, 1)
        by_count = by_count + pltpu.roll(by_count, BLOCK, 1)
        by_shift = (ROOT * (soft - 1.0) * by_bell - STEP * by_count) * weight
        by_first, by_second = by_first * weight, by_second * weight
        turned = pltpu.roll(by_second, BLOCK, 1)
        by_u = [
            jnp.where(low_lanes, pltpu.roll(by_first, BLOCK, 1), by_first),
            jnp.where(low_lanes, by_second, turned),
            jnp.where(low_lanes, turned, by_second),
        ]
        along = (by_u[0] * parts[0] + by_u[1] * parts[1] + by_u[2] * parts[2]) * inverse
        by_soft = by_shift * (-4.0 / ROOT) - along * inverse
        radial_part = by_soft * inverse + by_bell * (margin * (-4.0 * CUT_INV))
        column = jnp.zeros((ROWS, 128), F32)
        for a in range(3):
            force = by_u[a] * inverse + parts[a] * radial_part
            sums[a] = sums[a] + jnp.sum(force, axis=0, keepdims=True)
            total = jnp.sum(jnp.where(low_lanes, force, 0.0), axis=1, keepdims=True)
            column = jnp.where(lane == a, total, column)
        columns.append(column)
    return (
        jnp.concatenate(sums + [jnp.zeros((5, 128), F32)], axis=0),
        jnp.concatenate(columns, axis=0),
    )


def kind_table(col_ref, block):
    kind = col_ref[block_rows(block), 3:4].astype(jnp.int32)
    lane = iota((BLOCK, 128), 1)
    hit = kind == lane % SPAN
    return jnp.concatenate(
        [
            jnp.where(jnp.logical_and(hit, lane // SPAN % 4 == order), 1.0, 0.0)
            for order in range(4)
        ],
        axis=0,
    ).astype(BF16)


def parities(control_ref):
    return control_ref[1, 2] == 0, control_ref[2, 2] == 0


def fill_control(control_ref, words_ref, tiles_ref, slots, own_blocks):
    row, lane = iota((8, 128), 0), iota((8, 128), 1)
    live = words_ref[0, 0]
    table = jnp.where(lane < 2, tiles_ref[...], 0)
    lengths = [jnp.int32(0), jnp.int32(0)]
    for slot in range(2, slots):
        left, right = tiles_ref[slot, 0], tiles_ref[slot, 1]
        for which in range(2):
            ghost = which == 0
            sending = right - own_blocks if ghost else right
            member = (slot < live) & ((right >= own_blocks) if ghost else (right < own_blocks))
            first = 3 + 3 * which
            entry = jnp.where(lane == first, slot, jnp.where(lane == first + 1, left, sending))
            place = (lane >= first) & (lane < first + 3) & (row == lengths[which]) & member
            table = jnp.where(place, entry, table)
            lengths[which] = lengths[which] + member.astype(jnp.int32)
    for place, word in enumerate([live, words_ref[0, 1], words_ref[0, 2], *lengths]):
        table = jnp.where((lane == 2) & (row == place), word, table)
    control_ref[...] = table


def listed_tile(control_ref, which, place):
    first = 3 + 3 * which
    return tuple(control_ref[place, first + k] for k in range(3))


def listed_tiles(control_ref, which, work, start=0):
    count = control_ref[3 + which, 2] - start

    def step(half, carried):
        place = start + 2 * half
        work([listed_tile(control_ref, which, place + k) for k in range(2)])
        return carried

    lax.fori_loop(0, count // 2, step, 0)

    @pl.when(count % 2 == 1)
    def _():
        work([listed_tile(control_ref, which, start + count - 1)])


def own_tiles(control_ref, work):
    listed_tiles(control_ref, 1, work)


def ghost_tiles(control_ref, work):
    more = control_ref[3, 2]

    def fixed():
        return [(slot, control_ref[slot, 0], slot) for slot in range(2)]

    @pl.when(more == 0)
    def _():
        work(fixed())

    @pl.when(more > 0)
    def _():
        @pl.when(more == 1)
        def _():
            work(fixed() + [listed_tile(control_ref, 0, 0)])

        @pl.when(more > 1)
        def _():
            work(fixed() + [listed_tile(control_ref, 0, place) for place in range(2)])
            listed_tiles(control_ref, 0, work, 2)


def exact_pick(rows, chosen):
    high = rows.astype(BF16).astype(F32)
    rest = rows - high
    middle = rest.astype(BF16).astype(F32)
    stacked = jnp.concatenate(
        [high, middle, rest - middle, jnp.zeros_like(rows)], axis=0
    ).astype(BF16)
    picked = mm(stacked, chosen)
    return picked[0:8] + picked[8:16] + picked[16:24]


def fetch(pairs, sems):
    copies = [
        pltpu.make_async_copy(source, target, sems.at[i]) for i, (source, target) in enumerate(pairs)
    ]
    for copy in copies:
        copy.start()
    return copies


def pack_kernel(
    frac_in,
    kind_in,
    send_in,
    tile_in,
    site_ref,
    out_ref,
    send_ref,
    tiles_ref,
    frac_ref,
    kind_ref,
    tile_ref,
    sems,
):
    copies = fetch(
        (
            (frac_in, frac_ref),
            (kind_in, kind_ref),
            (send_in, send_ref),
            (tile_in, tile_ref),
        ),
        sems,
    )
    for copy in copies:
        copy.wait()
    atoms = frac_ref.shape[1]
    rows = jnp.concatenate(
        [frac_ref[...], kind_ref[...].astype(F32), jnp.zeros((4, atoms), F32)], axis=0
    )
    site_ref[...] = rows
    out_ref[...] = exact_pick(rows, chooser(send_ref[...], atoms).astype(F32).astype(BF16))
    slots = tile_ref.shape[1]
    lines = jnp.concatenate([tile_ref[...].astype(F32), jnp.zeros((2, 128 - slots), F32)], axis=1)
    lines = jnp.concatenate([lines, jnp.zeros((126, 128), F32)], axis=0)
    tiles_ref[...] = lines.T[0:8].astype(jnp.int32)


def doubled(rows, block):
    chunk = rows[:, block // 2 * 128 : block // 2 * 128 + 128]
    turned = pltpu.roll(chunk, BLOCK, 1)
    low = low_half()
    return jnp.where(low, chunk, turned) if block % 2 == 0 else jnp.where(low, turned, chunk)


def upright(rows):
    return jnp.concatenate([rows, jnp.zeros((120, rows.shape[1]), F32)], axis=0).T


def radial_row(weight_ref, path, n):
    row = SPAN + path * BASIS + n
    return weight_ref[row : row + 1, :]


def readout_row(weight_ref):
    row = SPAN + 4 * BASIS
    return weight_ref[row : row + 1, :]


def axis_scale():
    row = iota((8, 128), 0)
    return jnp.where(row < 2, WIDTHS[0], jnp.where(row == 2, WIDTHS[2], 1.0))


def add_histograms(tiles, col_ref, row_ref, own, kind_ref, hist_ref, pair_high, pair_low):
    for slot, left, right in tiles:
        same = left == right if own else False
        pair_forward(col_ref, left, row_ref, right, same, pair_high.at[slot], pair_low.at[slot])
    tables = [kind_table(kind_ref, right) for _, _, right in tiles]
    found = [
        mm(pair_high[slot], table) + mm(pair_low[slot], table)
        for (slot, _, _), table in zip(tiles, tables)
    ]
    lane_basis = iota((1, 128), 1) // (4 * SPAN)
    for (_, left, _), one in zip(tiles, found):
        for half in range(2):
            total = jnp.zeros((BLOCK, 128), F32)
            for n in range(4):
                begin = (half * 4 + n) * BLOCK
                total = jnp.where(lane_basis == n, one[begin : begin + BLOCK], total)
            hist_ref[block_rows(left), half * 128 : half * 128 + 128] += total


def own_histogram_kernel(
    control_ref, col_ref, row_ref, hist_ref, pair_high, pair_low
):
    hist_ref[...] = jnp.zeros_like(hist_ref)
    own_tiles(
        control_ref,
        lambda tiles: add_histograms(
            tiles, col_ref, row_ref, True, col_ref, hist_ref, pair_high, pair_low
        ),
    )


def prepare_kernel(
    slots,
    words_ref,
    tiles_ref,
    site_ref,
    send_ref,
    embed_in,
    radial_in,
    readout_in,
    mixing_in,
    control_ref,
    col_ref,
    row_ref,
    chosen_ref,
    fold_high,
    fold_low,
    mix_high,
    mix_low,
    weight_ref,
    fold_ref,
    mixing_ref,
    sems,
):
    kinds = embed_in.shape[0]
    paths = radial_in.shape[0]
    copies = fetch(
        (
            (embed_in, weight_ref.at[pl.ds(0, kinds)]),
            (radial_in, weight_ref.at[pl.ds(SPAN, paths)]),
            (readout_in, weight_ref.at[pl.ds(SPAN + paths, 1)]),
            (mixing_in, mixing_ref),
        ),
        sems,
    )
    atoms = site_ref.shape[1]
    blocks = atoms // BLOCK
    fill_control(control_ref, words_ref, tiles_ref, slots, blocks)
    own = site_ref[...] * axis_scale()[:, 0:1]
    col_ref[...] = upright(own)
    for block in range(blocks):
        row_ref[block] = doubled(own, block)
    chosen_ref[...] = chooser(send_ref[...], atoms).astype(F32).astype(BF16)
    for copy in copies:
        copy.wait()

    radial = weight_ref[SPAN : SPAN + paths, :]
    weight_ref[SPAN : SPAN + paths, :] = radial * basis_scale(radial.shape)

    embed = jnp.where(iota((SPAN, 128), 0) < kinds, weight_ref[0:SPAN, :], 0.0)
    scalar = jnp.concatenate([radial_row(weight_ref, 0, n) * embed for n in range(BASIS)], axis=0)
    vector = jnp.concatenate([radial_row(weight_ref, 1, n) * embed for n in range(BASIS)], axis=0)
    scalar, vector = split(scalar), split(vector)
    to_self = mm3(scalar, split(mixing_ref[0]))
    to_gate = mm3(scalar, split(mixing_ref[2]))
    to_vector = mm3(vector, split(mixing_ref[1]))
    fold_ref[...] = jnp.zeros_like(fold_ref)
    for n in range(BASIS):
        rows = slice(n * SPAN, n * SPAN + SPAN)
        base = n * 4 * SPAN
        fold_ref[base : base + SPAN, 0:128] = to_self[rows]
        fold_ref[base : base + SPAN, 128:256] = to_gate[rows]
        for a in range(3):
            here = base + (a + 1) * SPAN
            fold_ref[here : here + SPAN, (a + 2) * 128 : (a + 3) * 128] = to_vector[rows]
    fold_high[...], fold_low[...] = split(fold_ref[...])
    for part in range(2):
        mix_high[part], mix_low[part] = split(mixing_ref[3 + part])


def first_kernel(
    control_ref,
    send_in,
    hist_in,
    col_ref,
    mate_in,
    far_in,
    zmate_in,
    zfar_in,
    hist_ref,
    mate_ref,
    far_ref,
    side_ref,
    ghost_col,
    ghost_row,
    pair_high,
    pair_low,
    gather_ref,
    send_ref,
    sem,
):
    fetching = pltpu.make_async_copy(send_in, send_ref, sem)
    fetching.start()
    even_x, even_y = parities(control_ref)
    ghosts = pick_rows(even_x, even_y, mate_in[...], far_in[...], zmate_in[...], zfar_in[...])
    row = iota((8, 128), 0)
    slot = iota((8, 128), 1) // GHOSTS
    shift_x = jnp.where(slot < 3, -1.0, jnp.where(slot < 5, 0.0, 1.0))
    down = (slot == 0) | (slot == 3) | (slot == 5)
    level = (slot == 1) | (slot == 6)
    shift_y = jnp.where(down, -1.0, jnp.where(level, 0.0, 1.0))
    shift = jnp.where(row == 0, shift_x, jnp.where(row == 1, shift_y, 0.0))
    ghosts = (ghosts + shift) * axis_scale()
    ghost_col[...] = upright(ghosts)
    for block in range(2):
        ghost_row[block] = doubled(ghosts, block)
    hist_ref[...] = hist_in[...]

    ghost_tiles(
        control_ref,
        lambda tiles: add_histograms(
            tiles, col_ref, ghost_row, False, ghost_col, hist_ref, pair_high, pair_low
        ),
    )
    fetching.wait()

    up, down = jnp.where(even_x, 5, 0), jnp.where(even_x, 0, 5)
    places = [(mate_ref, part, up + part) for part in range(3)]
    places += [(far_ref, part, down + part) for part in range(3)]
    places += [(side_ref, part, 3 + part) for part in range(2)]
    for place, (_, _, slot) in enumerate(places):
        for entry in range(GHOSTS):
            row = place * GHOSTS + entry
            gather_ref[row : row + 1, :] = hist_ref[pl.ds(send_ref[slot, entry], 1), :]
    for place, (ref, part, _) in enumerate(places):
        ref[part] = pack(gather_ref[place * GHOSTS : place * GHOSTS + GHOSTS, :])


def make_features(block, col_ref, kinds, weight_ref, pre_ref, feat_high, feat_low, scalar_ref):
    rows = block_rows(block)
    kind = col_ref[rows, 3:4].astype(jnp.int32)
    scalar = jnp.zeros((BLOCK, 128), F32)
    for species in range(kinds):
        scalar = jnp.where(kind == species, weight_ref[species : species + 1, :], scalar)
    pre = pre_ref[rows, 0:128]
    scalar = scalar + pre * sigmoid(pre)
    if scalar_ref is not None:
        scalar_ref[rows, :] = scalar
    gate = sigmoid(pre_ref[rows, 128:256])
    parts = [scalar] + [pre_ref[rows, (a + 2) * 128 : (a + 3) * 128] * gate for a in range(3)]
    empty = jnp.zeros((BLOCK, 128), BF16)
    for order, part in enumerate(parts):
        high, low = split(part)
        here = pl.ds(order * BLOCK, BLOCK)
        used = 0 if order == 0 else 128
        for ref, value in ((feat_high, high), (feat_low, low)):
            ref[block, here, used : used + 128] = value
            ref[block, here, 128 - used : 256 - used] = empty


def add_messages(tiles, feat_high, feat_low, weight_ref, message_ref, pair_high, pair_low):
    found = [
        mm3((pair_high[slot], pair_low[slot]), (feat_high[right], feat_low[right]))
        for slot, _, right in tiles
    ]
    for (_, left, _), one in zip(tiles, found):
        total = jnp.zeros((BLOCK, 128), F32)
        for n in range(BASIS):
            rows = slice(n * BLOCK, n * BLOCK + BLOCK)
            total = total + one[rows, 0:128] * radial_row(weight_ref, 2, n)
            total = total + one[rows, 128:256] * radial_row(weight_ref, 3, n)
        message_ref[block_rows(left), :] += total


def feature_kernel(
    kinds,
    hist_ref,
    col_ref,
    fold_high,
    fold_low,
    weight_ref,
    pre_ref,
    feat_high,
    feat_low,
    scalar_ref,
):
    blocks = hist_ref.shape[0] // BLOCK
    pre_ref[...] = mm3(split(hist_ref[...]), (fold_high[...], fold_low[...]))

    def features(block, carried):
        make_features(block, col_ref, kinds, weight_ref, pre_ref, feat_high, feat_low, scalar_ref)
        return carried

    lax.fori_loop(0, blocks, features, 0)


def message_kernel(
    control_ref,
    row_ref,
    ghost_col,
    weight_ref,
    feat_high,
    feat_low,
    pair_high,
    pair_low,
    message_ref,
    swap_high,
    swap_low,
):
    blocks = feat_high.shape[0]
    message_ref[...] = jnp.zeros_like(message_ref)

    own_tiles(
        control_ref,
        lambda tiles: add_messages(
            tiles, feat_high, feat_low, weight_ref, message_ref, pair_high, pair_low
        ),
    )

    def swapped(tiles):
        for slot, left, right in tiles:
            pair_swapped(
                ghost_col, right, row_ref, left, False, swap_high.at[slot], swap_low.at[slot]
            )

    ghost_tiles(control_ref, swapped)


def weighted_pull(cotangent, weight_ref, path):
    return split(
        jnp.concatenate([cotangent * radial_row(weight_ref, path, n) for n in range(BASIS)], axis=0)
    )


def add_feature_pulls(tiles, places, pull_message, weight_ref, grad_feat, swap_high, swap_low):
    weighted = []
    for _, left, _ in tiles:
        cotangent = pull_message[block_rows(left), :]
        weighted.append([weighted_pull(cotangent, weight_ref, path) for path in (2, 3)])
    found = []
    for place, (by_scalar, by_vector) in zip(places, weighted):
        high, low = swap_high.at[place], swap_low.at[place]
        to_scalar = mm3((high[0:BLOCK, :], low[0:BLOCK, :]), by_scalar)
        to_vector = mm3((high[BLOCK:, :], low[BLOCK:, :]), by_vector)
        found.append((to_scalar, to_vector))
    for (_, _, right), (to_scalar, to_vector) in zip(tiles, found):
        rows = block_rows(right)
        grad_feat[rows, 0:128] += to_scalar
        for a in range(3):
            here = slice(a * BLOCK, (a + 1) * BLOCK)
            grad_feat[rows, (a + 1) * 128 : (a + 2) * 128] += to_vector[here]


def finish(message, scalar, mix_high, mix_low, weight_ref):
    mix_message, mix_hidden = (mix_high[0], mix_low[0]), (mix_high[1], mix_low[1])
    readout = readout_row(weight_ref)
    mixed = mm3(split(message), mix_message)
    mixed_gate = sigmoid(mixed)
    final = scalar + mixed * mixed_gate
    hidden = mm3(split(final), mix_hidden)
    hidden_gate = sigmoid(hidden)
    pull_hidden = readout * (hidden_gate * (1.0 + hidden * (1.0 - hidden_gate)))
    pull_final = mm3(split(pull_hidden), mix_hidden, ROWROW)
    pull_mixed = pull_final * (mixed_gate * (1.0 + mixed * (1.0 - mixed_gate)))
    pull_message = mm3(split(pull_mixed), mix_message, ROWROW)
    return hidden * hidden_gate * readout, pull_final, pull_message


def pull_features(grad_feat, pre_ref):
    by_scalar = grad_feat[:, 0:128]
    pre = pre_ref[:, 0:128]
    own_gate = sigmoid(pre)
    gate = sigmoid(pre_ref[:, 128:256])
    by_gate = jnp.zeros_like(gate)
    by_vector = []
    for a in range(3):
        pulled = grad_feat[:, (a + 1) * 128 : (a + 2) * 128]
        by_gate = by_gate + pulled * pre_ref[:, (a + 2) * 128 : (a + 3) * 128]
        by_vector.append(pulled * gate)
    by_pre = by_scalar * (own_gate * (1.0 + pre * (1.0 - own_gate)))
    return jnp.concatenate([by_pre, by_gate * gate * (1.0 - gate)] + by_vector, axis=1)


def second_ghost_kernel(
    kinds,
    control_ref,
    mate_in,
    far_in,
    zmate_in,
    zfar_in,
    ghost_col,
    fold_high,
    fold_low,
    mix_high,
    mix_low,
    weight_ref,
    scalar_ref,
    message_in,
    pair_high,
    pair_low,
    swap_high,
    swap_low,
    mate_ref,
    far_ref,
    side_ref,
    feat_high,
    feat_low,
    pull_message,
    direct_ref,
    share_ref,
    message_ref,
    pre_ref,
    grad_feat,
):
    even_x, even_y = parities(control_ref)
    fold = (fold_high[...], fold_low[...])
    ghost_hist = pick_all((even_x, even_y, mate_in, far_in, zmate_in, zfar_in))
    pre_ref[...] = mm3(split(ghost_hist), fold)
    for block in range(2):
        make_features(block, ghost_col, kinds, weight_ref, pre_ref, feat_high, feat_low, None)
    message_ref[...] = message_in[...]

    ghost_tiles(
        control_ref,
        lambda tiles: add_messages(
            tiles, feat_high, feat_low, weight_ref, message_ref, pair_high, pair_low
        ),
    )

    share_ref[...], direct_ref[...], pull_message[...] = finish(
        message_ref[...], scalar_ref[...], mix_high, mix_low, weight_ref
    )
    grad_feat[...] = jnp.zeros_like(grad_feat)

    ghost_tiles(
        control_ref,
        lambda tiles: add_feature_pulls(
            tiles, [slot for slot, _, _ in tiles], pull_message, weight_ref, grad_feat,
            swap_high, swap_low,
        ),
    )

    ghost_pull = mm3(split(pull_features(grad_feat, pre_ref)), fold, ROWROW)
    put_packets(
        even_x,
        lambda slot: ghost_pull[slot * GHOSTS : slot * GHOSTS + GHOSTS],
        mate_ref,
        far_ref,
        side_ref,
    )


def own_pull_kernel(
    control_ref,
    col_ref,
    row_ref,
    fold_high,
    fold_low,
    weight_ref,
    pre_ref,
    pull_message,
    direct_ref,
    pull_hist_ref,
    grad_feat,
    swap_high,
    swap_low,
):
    grad_feat[:, 0:128] = direct_ref[...]
    grad_feat[:, 128:512] = jnp.zeros((direct_ref.shape[0], 384), F32)

    def backward(tiles):
        for place, (_, left, right) in enumerate(tiles):
            pair_swapped(
                col_ref, right, row_ref, left, left == right,
                swap_high.at[place], swap_low.at[place],
            )
        add_feature_pulls(
            tiles, range(len(tiles)), pull_message, weight_ref, grad_feat, swap_high, swap_low
        )

    own_tiles(control_ref, backward)
    pulled = pull_features(grad_feat, pre_ref)
    pull_hist_ref[...] = mm3(split(pulled), (fold_high[...], fold_low[...]), ROWROW)


def pair_pulls(tiles, pull_message, weight_ref, high_ref, low_ref, pull_ref):
    weighted = []
    for _, left, _ in tiles:
        cotangent = pull_message[block_rows(left), :]
        first = weighted_pull(cotangent, weight_ref, 2)
        second = weighted_pull(cotangent, weight_ref, 3)
        weighted.append(
            [jnp.concatenate([first[part], second[part]], axis=1) for part in range(2)]
        )
    found = [
        mm3(one, (high_ref[right], low_ref[right]), ROWROW)
        for one, (_, _, right) in zip(weighted, tiles)
    ]
    for one, (slot, _, _) in zip(found, tiles):
        pull_ref[slot] = one


def ghost_pair_kernel(control_ref, weight_ref, pull_message, ghost_high, ghost_low, pull_ref):
    ghost_tiles(
        control_ref,
        lambda tiles: pair_pulls(tiles, pull_message, weight_ref, ghost_high, ghost_low, pull_ref),
    )


def own_pair_kernel(
    control_ref, weight_ref, pull_message, share_ref, feat_high, feat_low, pull_ref, energy_ref
):
    energy_ref[...] = jnp.sum(share_ref[...].T, axis=0, keepdims=True)

    own_tiles(
        control_ref,
        lambda tiles: pair_pulls(tiles, pull_message, weight_ref, feat_high, feat_low, pull_ref),
    )


def add_position_pulls(
    tiles, total_ref, kind_ref, col_ref, row_ref, own, pull_in, pull_refs, grad_row, grad_col
):
    lane_basis = iota((1, 128), 1) // (4 * SPAN)
    built = []
    for _, left, right in tiles:
        parts = []
        for half in range(2):
            here = total_ref[block_rows(left), half * 128 : half * 128 + 128]
            parts += [jnp.where(lane_basis == n, here, 0.0) for n in range(4)]
        high, low = split(jnp.concatenate(parts, axis=0))
        table = kind_table(kind_ref, right)
        built.append(
            (jnp.concatenate([high, low], axis=1), jnp.concatenate([table, table], axis=1))
        )
    found = [mm(both, table, ROWROW) for both, table in built]
    for place, ((slot, _, _), one) in enumerate(zip(tiles, found)):
        pull_refs[place] = pull_in[slot] + one
    grads = [
        pair_backward(
            col_ref, left, row_ref, right, left == right if own else False, pull_refs.at[place]
        )
        for place, (_, left, right) in enumerate(tiles)
    ]
    for (_, left, right), (by_row, by_col) in zip(tiles, grads):
        grad_row[right] += by_row
        grad_col[block_rows(left), :] -= by_col


def third_ghost_kernel(
    control_ref,
    chosen_ref,
    pull_hist_ref,
    mate_in,
    far_in,
    zmate_in,
    zfar_in,
    col_ref,
    ghost_col,
    ghost_row,
    pull_in,
    out_ref,
    total_ref,
    grad_col,
    grad_ghost,
    pull_refs,
):
    even_x, even_y = parities(control_ref)
    returned = split(pick_all((even_x, even_y, mate_in, far_in, zmate_in, zfar_in)))
    chosen = chosen_ref[...]
    total_ref[...] = pull_hist_ref[...] + mm(chosen, returned[0]) + mm(chosen, returned[1])
    grad_ghost[...] = jnp.zeros_like(grad_ghost)
    grad_col[...] = jnp.zeros_like(grad_col)

    ghost_tiles(
        control_ref,
        lambda tiles: add_position_pulls(
            tiles, total_ref, ghost_col, col_ref, ghost_row, False, pull_in, pull_refs,
            grad_ghost, grad_col,
        ),
    )
    out_ref[...] = jnp.where(low_half(), grad_ghost[0], grad_ghost[1])


def third_own_kernel(
    control_ref,
    chosen_ref,
    total_ref,
    col_ref,
    row_ref,
    pull_in,
    grad_col_in,
    own_ref,
    turned_ref,
    grad_row,
    grad_col,
    pull_refs,
):
    blocks = total_ref.shape[0] // BLOCK
    turned_ref[...] = chosen_ref[...].astype(F32).T.astype(BF16)
    grad_row[...] = jnp.zeros_like(grad_row)
    grad_col[...] = grad_col_in[...]

    own_tiles(
        control_ref,
        lambda tiles: add_position_pulls(
            tiles, total_ref, col_ref, col_ref, row_ref, True, pull_in, pull_refs,
            grad_row, grad_col,
        ),
    )
    low = low_half()
    by_sender = jnp.concatenate(
        [jnp.where(low, grad_row[2 * k], grad_row[2 * k + 1]) for k in range(blocks // 2)], axis=1
    )
    own_ref[...] = by_sender + grad_col[...].T[0:8]


def last_kernel(control_ref, turned_ref, own_ref, mate_in, far_in, zmate_in, zfar_in, force_ref):
    even_x, even_y = parities(control_ref)
    returned = pick_rows(even_x, even_y, mate_in[...], far_in[...], zmate_in[...], zfar_in[...])
    total = own_ref[...] + exact_pick(returned, turned_ref[...])
    force_ref[...] = -total[0:3]


def partners(axis, far):
    count = lax.axis_size(axis)
    if far:
        return [(i, (i + (1 if i % 2 else -1)) % count) for i in range(count)]
    return [(i, i ^ 1) for i in range(count)]


def swap_both(axis, to_mate, to_far):
    to_far, to_mate = lax.optimization_barrier((to_far, to_mate))
    far = lax.ppermute(to_far, axis, partners(axis, True))
    mate = lax.ppermute(to_mate, axis, partners(axis, False))
    far, mate = lax.optimization_barrier((far, mate))
    return mate, far


def exchange_rows(rows, beside):
    mate, far = swap_both("gx", rows, rows)
    far, mate, beside = lax.optimization_barrier((far, mate, beside))
    column = jnp.stack([rows, mate, far])
    zmate, zfar = swap_both("gy", column, column)
    return (mate, far, zmate, zfar), beside


def exchange_packets(even_y, to_mate, to_far, side, beside):
    mate, far = swap_both("gx", to_mate, to_far)
    far, mate, beside = lax.optimization_barrier((far, mate, beside))
    up = jnp.concatenate([mate[2:3], far[2:3], side[1:2]], axis=0)
    down = jnp.concatenate([mate[0:1], far[0:1], side[0:1]], axis=0)
    zmate, zfar = swap_both("gy", jnp.where(even_y, up, down), jnp.where(even_y, down, up))
    return (mate, far, zmate, zfar), beside


def struct(*shape, dtype=F32):
    return jax.ShapeDtypeStruct(shape, dtype)


def call(kernel, in_specs, outs, scratch=()):
    made = pl.pallas_call(
        kernel,
        in_specs=in_specs,
        out_specs=jax.tree.map(lambda _: VMEM, outs),
        out_shape=outs,
        scratch_shapes=list(scratch),
        compiler_params=PARAMS,
    )

    def run(*args):
        placed = [
            pltpu.with_memory_space_constraint(arg, pltpu.HBM if spec is HBM else pltpu.VMEM)
            for arg, spec in zip(args, in_specs, strict=True)
        ]
        return made(*placed)

    return run


def shards(fractions, species, send_list, tile_list, counts, embedding, radial, mixing, readout):
    atoms = fractions.shape[1]
    blocks = atoms // BLOCK
    kinds = embedding.shape[0]
    slots = tile_list.shape[1]
    parity = [lax.axis_index("gx") % 2, lax.axis_index("gy") % 2]
    even_y = parity[1] == 0
    words = jnp.stack([counts[0], *parity]).astype(jnp.int32)[None]
    far_arrays = (
        fractions,
        species[None],
        send_list,
        tile_list,
        embedding,
        radial.reshape(-1, radial.shape[2]),
        readout[None],
        mixing,
    )
    packets = [struct(3, 24, 128), struct(3, 24, 128), struct(2, 24, 128)]
    hist_struct = struct(atoms, HIST)
    col_struct = struct(atoms, 128)
    own_rows, ghost_rows = struct(blocks, 8, 128), struct(2, 8, 128)
    fold_halves = [struct(HIST, 640, dtype=BF16)] * 2
    mix_halves = [struct(2, 128, 128, dtype=BF16)] * 2
    own_halves = [struct(blocks, 256, 256, dtype=BF16)] * 2
    ghost_halves = [struct(2, 256, 256, dtype=BF16)] * 2
    pairs = [struct(slots, BASIS * BLOCK, 256, dtype=BF16)] * 2
    swaps = [struct(slots, 256, BASIS * BLOCK, dtype=BF16)] * 2
    pulls = struct(slots, BASIS * BLOCK, 256)

    site, rows, send, tiles = call(
        pack_kernel,
        [HBM] * 4,
        [
            struct(8, atoms), struct(8, 128),
            struct(*send_list.shape, dtype=jnp.int32), struct(8, 128, dtype=jnp.int32),
        ],
        [
            pltpu.VMEM(fractions.shape, F32),
            pltpu.VMEM((1, atoms), jnp.int32),
            pltpu.VMEM(tile_list.shape, jnp.int32),
            pltpu.SemaphoreType.DMA((4,)),
        ],
    )(*far_arrays[0:4])
    prepared = call(
        functools.partial(prepare_kernel, slots),
        [VMEM] * 4 + [HBM] * 4,
        [
            struct(8, 128, dtype=jnp.int32), col_struct, own_rows,
            struct(atoms, 128, dtype=BF16),
        ]
        + fold_halves
        + mix_halves
        + [struct(2 * SPAN + 4 * BASIS, 128)],
        [
            pltpu.VMEM((HIST, 640), F32),
            pltpu.VMEM(mixing.shape, F32),
            pltpu.SemaphoreType.DMA((4,)),
        ],
    )(words, tiles, site, send, *far_arrays[4:])
    arrived, prepared = exchange_rows(rows, prepared)
    control, col, row, chosen, fold_high, fold_low, mix_high, mix_low, weights = prepared
    fold, mix = (fold_high, fold_low), (mix_high, mix_low)
    hist, own_high, own_low = call(
        own_histogram_kernel, [VMEM] * 3, [hist_struct] + pairs
    )(control, col, row)
    hist, to_mate, to_far, side, ghost_col, ghost_row, pair_high, pair_low = call(
        first_kernel,
        [VMEM] * 8,
        [hist_struct] + packets + [struct(8 * GHOSTS, 128), ghost_rows] + pairs,
        [
            pltpu.VMEM((8 * GHOSTS, HIST), F32),
            pltpu.SMEM(send_list.shape, jnp.int32),
            pltpu.SemaphoreType.DMA,
        ],
    )(control, send, hist, col, *arrived)
    features = call(
        functools.partial(feature_kernel, kinds),
        [VMEM] * 5,
        [struct(atoms, 640)] + own_halves + [col_struct],
    )(hist, col, *fold, weights)
    arrived, features = exchange_packets(even_y, to_mate, to_far, side, features)
    pre, feat_high, feat_low, scalar = features
    message, swap_high, swap_low = call(message_kernel, [VMEM] * 8, [col_struct] + swaps)(
        control, row, ghost_col, weights, feat_high, feat_low, own_high, own_low
    )
    (
        to_mate, to_far, side, ghost_high, ghost_low, pull_message, direct, share,
    ) = call(
        functools.partial(second_ghost_kernel, kinds),
        [VMEM] * 17,
        packets + ghost_halves + [col_struct] * 3,
        [
            pltpu.VMEM((atoms, 128), F32),
            pltpu.VMEM((8 * GHOSTS, 640), F32),
            pltpu.VMEM((8 * GHOSTS, 512), F32),
        ],
    )(
        control, *arrived, ghost_col, *fold, *mix, weights, scalar, message,
        pair_high, pair_low, swap_high, swap_low,
    )
    pull = call(ghost_pair_kernel, [VMEM] * 5, pulls)(
        control, weights, pull_message, ghost_high, ghost_low
    )
    arrived, (pull, direct) = exchange_packets(even_y, to_mate, to_far, side, (pull, direct))
    pull_hist = call(
        own_pull_kernel,
        [VMEM] * 9,
        hist_struct,
        [pltpu.VMEM((atoms, 512), F32)] + [pltpu.VMEM((2, 256, BASIS * BLOCK), BF16)] * 2,
    )(control, col, row, *fold, weights, pre, pull_message, direct)
    rows, total, grad_col = call(
        third_ghost_kernel,
        [VMEM] * 11,
        [struct(8, 128), hist_struct, col_struct],
        [pltpu.VMEM((2, 8, 128), F32), pltpu.VMEM((4, BASIS * BLOCK, 256), F32)],
    )(control, chosen, pull_hist, *arrived, col, ghost_col, ghost_row, pull)
    share, rows = lax.optimization_barrier((share, rows))
    own_pair = call(own_pair_kernel, [VMEM] * 6, [pulls, struct(1, atoms)])(
        control, weights, pull_message, share, feat_high, feat_low
    )
    arrived, own_pair = exchange_rows(rows, own_pair)
    pull, energy = own_pair
    own, turned = call(
        third_own_kernel,
        [VMEM] * 7,
        [struct(8, atoms), struct(128, atoms, dtype=BF16)],
        [
            pltpu.VMEM((blocks, 8, 128), F32),
            pltpu.VMEM((atoms, 128), F32),
            pltpu.VMEM((2, BASIS * BLOCK, 256), F32),
        ],
    )(control, chosen, total, col, row, pull, grad_col)
    forces = call(last_kernel, [VMEM] * 7, struct(3, atoms))(control, turned, own, *arrived)
    return energy[0], forces


def solution(mesh):
    placed = (
        P(None, ("gx", "gy")),
        P(("gx", "gy")),
        P(None, ("gx", "gy")),
        P(None, ("gx", "gy")),
        P(("gx", "gy")),
        P(),
        P(),
        P(),
        P(),
    )
    return jax.shard_map(
        shards,
        mesh=mesh,
        in_specs=placed,
        out_specs=(P(("gx", "gy")), P(None, ("gx", "gy"))),
        check_vma=False,
    )
```

```python
import functools

import jax
import jax.numpy as jnp
from jax import lax
from jax.experimental import pallas as pl
from jax.experimental.pallas import tpu as pltpu
from jax.sharding import PartitionSpec as P

F32 = jnp.float32
BF16 = jnp.bfloat16

BASIS = 8
BLOCK = 64
GHOSTS = 16
SPAN = 8
HIST = BASIS * 4 * SPAN
OFFSETS = ((-1, -1), (-1, 0), (-1, 1), (0, -1), (0, 1), (1, -1), (1, 0), (1, 1))
WIDTHS = (12.0, 12.0, 36.0)
CUT_INV = 1.0 / 25.0
ROOT = 1.6986436005760381
STEP = ROOT * 0.6
MIDDLE = 1.0 + 0.6 * (BASIS - 1) / 2
REACH = 5.125
ROWS = 32

VMEM = pl.BlockSpec(memory_space=pltpu.VMEM)
HBM = pl.BlockSpec(memory_space=pltpu.HBM)
PARAMS = pltpu.CompilerParams(vmem_limit_bytes=16 * 1024 * 1024)

ROWROW = (((1,), (1,)), ((), ()))
ROWCOL = (((1,), (0,)), ((), ()))


def split(value):
    high = value.astype(BF16)
    return high, (value - high.astype(F32)).astype(BF16)


def mm(left, right, dims=ROWCOL):
    return lax.dot_general(left, right, dims, preferred_element_type=F32)


def mm3(left, right, dims=ROWCOL):
    (lh, ll), (rh, rl) = left, right
    summed = dims[0][1][0]
    return mm(
        jnp.concatenate([lh, ll, lh], axis=1), jnp.concatenate([rh, rh, rl], axis=summed), dims
    )


def sigmoid(value):
    return 1.0 / (1.0 + jnp.exp(-value))


def iota(shape, dim):
    return lax.broadcasted_iota(jnp.int32, shape, dim)


def low_half():
    return iota((1, 128), 1) < BLOCK


def pick_rows(even_x, even_y, mate, far, zmate, zfar):
    x_up, x_down = jnp.where(even_x, mate, far), jnp.where(even_x, far, mate)
    y_up = [jnp.where(even_y, zmate[i], zfar[i]) for i in range(3)]
    y_down = [jnp.where(even_y, zfar[i], zmate[i]) for i in range(3)]
    sources = {
        (1, 0): x_up,
        (-1, 0): x_down,
        (0, 1): y_up[0],
        (0, -1): y_down[0],
        (1, 1): jnp.where(even_x, y_up[1], y_up[2]),
        (-1, 1): jnp.where(even_x, y_up[2], y_up[1]),
        (1, -1): jnp.where(even_x, y_down[1], y_down[2]),
        (-1, -1): jnp.where(even_x, y_down[2], y_down[1]),
    }
    slot_of = iota((8, 128), 1) // GHOSTS
    total = jnp.zeros((8, 128), F32)
    for slot, offset in enumerate(OFFSETS):
        turned = pltpu.roll(sources[offset], ((2 * slot - 7) * GHOSTS) % 128, 1)
        total = jnp.where(slot_of == slot, turned, total)
    return total


def pick_slot(slot, even_x, even_y, mate, far, zmate, zfar):
    along_x, along_y = OFFSETS[slot]
    if along_y == 0:
        near = even_x if along_x == 1 else jnp.logical_not(even_x)
        return jnp.where(near, mate[1], far[1])
    near = even_y if along_y == 1 else jnp.logical_not(even_y)
    if along_x == 0:
        return jnp.where(near, zmate[2], zfar[2])
    first = even_x if along_x == 1 else jnp.logical_not(even_x)
    return jnp.where(
        near, jnp.where(first, zmate[0], zmate[1]), jnp.where(first, zfar[0], zfar[1])
    )


def pick_all(args):
    return jnp.concatenate([unpack(pick_slot(slot, *args)) for slot in range(8)], axis=0)


def pack(rows):
    free = iota((8, 128), 1) % SPAN >= 6
    carried = rows[8:16, 128:256]
    quarters = (rows[0:8, 0:128], rows[8:16, 0:128], rows[0:8, 128:256])
    return jnp.concatenate(
        [
            jnp.where(free, pltpu.roll(carried, 6 - 2 * part, 1), quarter)
            for part, quarter in enumerate(quarters)
        ],
        axis=0,
    )


def unpack(packet):
    place = iota((8, 128), 1) % SPAN
    turned = [
        pltpu.roll(packet[8 * part : 8 * part + 8], 128 - (6 - 2 * part), 1) for part in range(3)
    ]
    carried = jnp.where(place < 2, turned[0], jnp.where(place < 4, turned[1], turned[2]))
    return jnp.concatenate(
        [packet[0:16], jnp.concatenate([packet[16:24], carried], axis=0)], axis=1
    )


def put_packets(even_x, piece, mate_ref, far_ref, side_ref):
    for part in range(3):
        down, up = pack(piece(part)), pack(piece(5 + part))
        mate_ref[part] = jnp.where(even_x, up, down)
        far_ref[part] = jnp.where(even_x, down, up)
    side_ref[0] = pack(piece(3))
    side_ref[1] = pack(piece(4))


def send_columns(send):
    wide = jnp.concatenate([send] * 8, axis=1)
    own = iota((8, 128), 1) // GHOSTS == iota((8, 128), 0)
    return jnp.sum(jnp.where(own, wide, 0), axis=0, keepdims=True)


def chooser(send, atoms):
    return iota((atoms, 128), 0) == send_columns(send)


def block_rows(block, start=0, count=BLOCK):
    return pl.ds(pl.multiple_of(block * BLOCK, BLOCK) + start, count)


def separation(col_ref, col_block, row_ref, row_block, start, sign):
    mine = col_ref[block_rows(col_block, start, ROWS), :]
    other = row_ref[row_block]
    return [sign * (other[a : a + 1, :] - mine[:, a : a + 1]) for a in range(3)]


def envelope(parts, same, start):
    dist_sq = parts[0] * parts[0] + parts[1] * parts[1] + parts[2] * parts[2]
    soft = jnp.sqrt(dist_sq + 1.0)
    rows = iota((ROWS, 128), 0) + start
    columns = iota((ROWS, 128), 1) % BLOCK
    apart = jnp.where(jnp.logical_and(rows == columns, same), 0.0, 1.0)
    margin = jnp.maximum(1.0 - dist_sq * CUT_INV, 0.0) * apart
    return soft, margin


def angular(parts, inverse):
    u = [part * inverse for part in parts]
    low = low_half()
    return jnp.where(low, 1.0, u[0]), jnp.where(low, u[1], u[2])


def basis_scale(shape):
    step = (iota(shape, 0) % BASIS).astype(F32) - (BASIS - 1) / 2
    return jnp.exp2(-(STEP * STEP) * (step * step))


def centered(soft):
    return ROOT * (jnp.minimum(soft, REACH) - MIDDLE)


def pair_forward(col_ref, left, row_ref, right, same, high_ref, low_ref):
    for start in range(0, BLOCK, ROWS):
        parts = separation(col_ref, left, row_ref, right, start, 1.0)
        soft, margin = envelope(parts, same, start)
        first, second = angular(parts, 1.0 / soft)
        z = centered(soft)
        bell = jnp.exp2(-z * (z + (BASIS - 1) * STEP)) * (margin * margin)
        growth = jnp.exp2((2.0 * STEP) * z)
        for n in range(BASIS):
            here = pl.ds(n * BLOCK + start, ROWS)
            for half, factor in enumerate((first, second)):
                high, low = split(bell * factor)
                high_ref[here, half * 128 : half * 128 + 128] = high
                low_ref[here, half * 128 : half * 128 + 128] = low
            bell = bell * growth


def pair_swapped(col_ref, right, row_ref, left, same, high_ref, low_ref):
    low_lanes = low_half()
    for start in range(0, BLOCK, ROWS):
        parts = separation(col_ref, right, row_ref, left, start, -1.0)
        soft, margin = envelope(parts, same, start)
        inverse = 1.0 / soft
        u = [part * inverse for part in parts]
        z = centered(soft)
        bell = jnp.exp2(-z * (z + jnp.where(low_lanes, (BASIS - 1) * STEP, (BASIS - 3) * STEP)))
        bell = bell * (margin * margin)
        growth = jnp.exp2((4.0 * STEP) * z)
        for pair in range(BASIS // 2):
            for order in range(4):
                high, low = split(bell if order == 0 else bell * u[order - 1])
                here = pl.ds(order * BLOCK + start, ROWS)
                high_ref[here, pair * 128 : pair * 128 + 128] = high
                low_ref[here, pair * 128 : pair * 128 + 128] = low
            bell = bell * growth


def pair_backward(col_ref, left, row_ref, right, same, pull_ref):
    low_lanes = low_half()
    lane = iota((1, 128), 1)
    sums = [jnp.zeros((1, 128), F32) for _ in range(3)]
    columns = []
    for start in range(0, BLOCK, ROWS):
        parts = separation(col_ref, left, row_ref, right, start, 1.0)
        soft, margin = envelope(parts, same, start)
        inverse = 1.0 / soft
        first, second = angular(parts, inverse)
        z = centered(soft)
        bell = jnp.exp2(-z * (z - (BASIS - 1) * STEP))
        shrink = jnp.exp2((-2.0 * STEP) * z)
        by_first = jnp.zeros((ROWS, 128), F32)
        by_second = jnp.zeros((ROWS, 128), F32)
        count_first = jnp.zeros((ROWS, 128), F32)
        count_second = jnp.zeros((ROWS, 128), F32)
        for n in reversed(range(BASIS)):
            here = pl.ds(n * BLOCK + start, ROWS)
            by_first = by_first + bell * pull_ref[here, 0:128]
            by_second = by_second + bell * pull_ref[here, 128:256]
            if n > 0:
                count_first = count_first + by_first
                count_second = count_second + by_second
                bell = bell * shrink
        weight = margin * margin
        by_bell = first * by_first + second * by_second
        by_count = first * count_first + second * count_second
        by_bell = by_bell + pltpu.roll(by_bell, BLOCK, 1)
        by_count = by_count + pltpu.roll(by_count, BLOCK, 1)
        by_shift = (ROOT * (soft - 1.0) * by_bell - STEP * by_count) * weight
        by_first, by_second = by_first * weight, by_second * weight
        turned = pltpu.roll(by_second, BLOCK, 1)
        by_u = [
            jnp.where(low_lanes, pltpu.roll(by_first, BLOCK, 1), by_first),
            jnp.where(low_lanes, by_second, turned),
            jnp.where(low_lanes, turned, by_second),
        ]
        along = (by_u[0] * parts[0] + by_u[1] * parts[1] + by_u[2] * parts[2]) * inverse
        by_soft = by_shift * (-4.0 / ROOT) - along * inverse
        radial_part = by_soft * inverse + by_bell * (margin * (-4.0 * CUT_INV))
        column = jnp.zeros((ROWS, 128), F32)
        for a in range(3):
            force = by_u[a] * inverse + parts[a] * radial_part
            sums[a] = sums[a] + jnp.sum(force, axis=0, keepdims=True)
            total = jnp.sum(jnp.where(low_lanes, force, 0.0), axis=1, keepdims=True)
            column = jnp.where(lane == a, total, column)
        columns.append(column)
    return (
        jnp.concatenate(sums + [jnp.zeros((5, 128), F32)], axis=0),
        jnp.concatenate(columns, axis=0),
    )


def kind_table(col_ref, block):
    kind = col_ref[block_rows(block), 3:4].astype(jnp.int32)
    lane = iota((BLOCK, 128), 1)
    hit = kind == lane % SPAN
    return jnp.concatenate(
        [
            jnp.where(jnp.logical_and(hit, lane // SPAN % 4 == order), 1.0, 0.0)
            for order in range(4)
        ],
        axis=0,
    ).astype(BF16)


def parities(control_ref):
    return control_ref[1, 2] == 0, control_ref[2, 2] == 0


def fill_control(control_ref, words_ref, tiles_ref, slots, own_blocks):
    row, lane = iota((8, 128), 0), iota((8, 128), 1)
    live = words_ref[0, 0]
    table = jnp.where(lane < 2, tiles_ref[...], 0)
    lengths = [jnp.int32(0), jnp.int32(0)]
    for slot in range(2, slots):
        left, right = tiles_ref[slot, 0], tiles_ref[slot, 1]
        for which in range(2):
            ghost = which == 0
            sending = right - own_blocks if ghost else right
            member = (slot < live) & ((right >= own_blocks) if ghost else (right < own_blocks))
            first = 3 + 3 * which
            entry = jnp.where(lane == first, slot, jnp.where(lane == first + 1, left, sending))
            place = (lane >= first) & (lane < first + 3) & (row == lengths[which]) & member
            table = jnp.where(place, entry, table)
            lengths[which] = lengths[which] + member.astype(jnp.int32)
    for place, word in enumerate([live, words_ref[0, 1], words_ref[0, 2], *lengths]):
        table = jnp.where((lane == 2) & (row == place), word, table)
    control_ref[...] = table


def listed_tile(control_ref, which, place):
    first = 3 + 3 * which
    return tuple(control_ref[place, first + k] for k in range(3))


def single_tiles(control_ref, which, work, start):
    def step(place, carried):
        work([listed_tile(control_ref, which, place)])
        return carried

    lax.fori_loop(start, control_ref[3 + which, 2], step, 0)


def own_tiles(control_ref, work):
    count = control_ref[4, 2]

    def group(place, size):
        work([listed_tile(control_ref, 1, place + k) for k in range(size)])

    def step(quarter, carried):
        group(4 * quarter, 4)
        return carried

    lax.fori_loop(0, count // 4, step, 0)
    rest = count % 4

    @pl.when(rest >= 2)
    def _():
        group(count - rest, 2)

    @pl.when(rest % 2 == 1)
    def _():
        group(count - 1, 1)


def ghost_tiles(control_ref, work):
    more = control_ref[3, 2]

    def fixed():
        return [(slot, control_ref[slot, 0], slot) for slot in range(2)]

    @pl.when(more == 0)
    def _():
        work(fixed())

    @pl.when(more > 0)
    def _():
        @pl.when(more == 1)
        def _():
            work(fixed() + [listed_tile(control_ref, 0, 0)])

        @pl.when(more > 1)
        def _():
            work(fixed() + [listed_tile(control_ref, 0, place) for place in range(2)])
            single_tiles(control_ref, 0, work, 2)


def exact_pick(rows, chosen):
    high = rows.astype(BF16).astype(F32)
    rest = rows - high
    middle = rest.astype(BF16).astype(F32)
    stacked = jnp.concatenate(
        [high, middle, rest - middle, jnp.zeros_like(rows)], axis=0
    ).astype(BF16)
    picked = mm(stacked, chosen)
    return picked[0:8] + picked[8:16] + picked[16:24]


def fetch(pairs, sems):
    copies = [
        pltpu.make_async_copy(source, target, sems.at[i]) for i, (source, target) in enumerate(pairs)
    ]
    for copy in copies:
        copy.start()
    return copies


def pack_kernel(
    frac_in,
    kind_in,
    send_in,
    tile_in,
    site_ref,
    out_ref,
    send_ref,
    tiles_ref,
    frac_ref,
    kind_ref,
    tile_ref,
    sems,
):
    copies = fetch(
        (
            (frac_in, frac_ref),
            (kind_in, kind_ref),
            (send_in, send_ref),
            (tile_in, tile_ref),
        ),
        sems,
    )
    for copy in copies:
        copy.wait()
    atoms = frac_ref.shape[1]
    rows = jnp.concatenate(
        [frac_ref[...], kind_ref[...].astype(F32), jnp.zeros((4, atoms), F32)], axis=0
    )
    site_ref[...] = rows
    out_ref[...] = exact_pick(rows, chooser(send_ref[...], atoms).astype(F32).astype(BF16))
    slots = tile_ref.shape[1]
    lines = jnp.concatenate([tile_ref[...].astype(F32), jnp.zeros((2, 128 - slots), F32)], axis=1)
    lines = jnp.concatenate([lines, jnp.zeros((126, 128), F32)], axis=0)
    tiles_ref[...] = lines.T[0:8].astype(jnp.int32)


def doubled(rows, block):
    chunk = rows[:, block // 2 * 128 : block // 2 * 128 + 128]
    turned = pltpu.roll(chunk, BLOCK, 1)
    low = low_half()
    return jnp.where(low, chunk, turned) if block % 2 == 0 else jnp.where(low, turned, chunk)


def upright(rows):
    return jnp.concatenate([rows, jnp.zeros((120, rows.shape[1]), F32)], axis=0).T


def radial_row(weight_ref, path, n):
    row = SPAN + path * BASIS + n
    return weight_ref[row : row + 1, :]


def readout_row(weight_ref):
    row = SPAN + 4 * BASIS
    return weight_ref[row : row + 1, :]


def axis_scale():
    row = iota((8, 128), 0)
    return jnp.where(row < 2, WIDTHS[0], jnp.where(row == 2, WIDTHS[2], 1.0))


def add_histograms(tiles, col_ref, row_ref, own, kind_ref, hist_ref, pair_high, pair_low):
    for slot, left, right in tiles:
        same = left == right if own else False
        pair_forward(col_ref, left, row_ref, right, same, pair_high.at[slot], pair_low.at[slot])
    tables = [kind_table(kind_ref, right) for _, _, right in tiles]
    found = [
        mm(pair_high[slot], table) + mm(pair_low[slot], table)
        for (slot, _, _), table in zip(tiles, tables)
    ]
    lane_basis = iota((1, 128), 1) // (4 * SPAN)
    for (_, left, _), one in zip(tiles, found):
        for half in range(2):
            total = jnp.zeros((BLOCK, 128), F32)
            for n in range(4):
                begin = (half * 4 + n) * BLOCK
                total = jnp.where(lane_basis == n, one[begin : begin + BLOCK], total)
            hist_ref[block_rows(left), half * 128 : half * 128 + 128] += total


def own_histogram_kernel(
    control_ref, col_ref, row_ref, hist_ref, pair_high, pair_low
):
    hist_ref[...] = jnp.zeros_like(hist_ref)
    own_tiles(
        control_ref,
        lambda tiles: add_histograms(
            tiles, col_ref, row_ref, True, col_ref, hist_ref, pair_high, pair_low
        ),
    )


def prepare_kernel(
    slots,
    words_ref,
    tiles_ref,
    site_ref,
    send_ref,
    embed_in,
    radial_in,
    readout_in,
    mixing_in,
    control_ref,
    col_ref,
    row_ref,
    chosen_ref,
    weight_ref,
    mixing_ref,
    sems,
):
    kinds = embed_in.shape[0]
    paths = radial_in.shape[0]
    copies = fetch(
        (
            (embed_in, weight_ref.at[pl.ds(0, kinds)]),
            (radial_in, weight_ref.at[pl.ds(SPAN, paths)]),
            (readout_in, weight_ref.at[pl.ds(SPAN + paths, 1)]),
            (mixing_in, mixing_ref),
        ),
        sems,
    )
    atoms = site_ref.shape[1]
    blocks = atoms // BLOCK
    fill_control(control_ref, words_ref, tiles_ref, slots, blocks)
    own = site_ref[...] * axis_scale()[:, 0:1]
    col_ref[...] = upright(own)
    for block in range(blocks):
        row_ref[block] = doubled(own, block)
    chosen_ref[...] = chooser(send_ref[...], atoms).astype(F32).astype(BF16)
    for copy in copies:
        copy.wait()
    radial = weight_ref[SPAN : SPAN + paths, :]
    weight_ref[SPAN : SPAN + paths, :] = radial * basis_scale(radial.shape)


def first_kernel(
    control_ref,
    send_in,
    hist_in,
    col_ref,
    mate_in,
    far_in,
    zmate_in,
    zfar_in,
    hist_ref,
    mate_ref,
    far_ref,
    side_ref,
    ghost_col,
    ghost_row,
    pair_high,
    pair_low,
    gather_ref,
    send_ref,
    sem,
):
    fetching = pltpu.make_async_copy(send_in, send_ref, sem)
    fetching.start()
    even_x, even_y = parities(control_ref)
    ghosts = pick_rows(even_x, even_y, mate_in[...], far_in[...], zmate_in[...], zfar_in[...])
    row = iota((8, 128), 0)
    slot = iota((8, 128), 1) // GHOSTS
    shift_x = jnp.where(slot < 3, -1.0, jnp.where(slot < 5, 0.0, 1.0))
    down = (slot == 0) | (slot == 3) | (slot == 5)
    level = (slot == 1) | (slot == 6)
    shift_y = jnp.where(down, -1.0, jnp.where(level, 0.0, 1.0))
    shift = jnp.where(row == 0, shift_x, jnp.where(row == 1, shift_y, 0.0))
    ghosts = (ghosts + shift) * axis_scale()
    ghost_col[...] = upright(ghosts)
    for block in range(2):
        ghost_row[block] = doubled(ghosts, block)
    hist_ref[...] = hist_in[...]

    ghost_tiles(
        control_ref,
        lambda tiles: add_histograms(
            tiles, col_ref, ghost_row, False, ghost_col, hist_ref, pair_high, pair_low
        ),
    )
    fetching.wait()

    up, down = jnp.where(even_x, 5, 0), jnp.where(even_x, 0, 5)
    places = [(mate_ref, part, up + part) for part in range(3)]
    places += [(far_ref, part, down + part) for part in range(3)]
    places += [(side_ref, part, 3 + part) for part in range(2)]
    for place, (_, _, slot) in enumerate(places):
        for entry in range(GHOSTS):
            row = place * GHOSTS + entry
            gather_ref[row : row + 1, :] = hist_ref[pl.ds(send_ref[slot, entry], 1), :]
    for place, (ref, part, _) in enumerate(places):
        ref[part] = pack(gather_ref[place * GHOSTS : place * GHOSTS + GHOSTS, :])


def make_features(block, col_ref, kinds, weight_ref, pre_ref, feat_high, feat_low, scalar_ref):
    rows = block_rows(block)
    kind = col_ref[rows, 3:4].astype(jnp.int32)
    scalar = jnp.zeros((BLOCK, 128), F32)
    for species in range(kinds):
        scalar = jnp.where(kind == species, weight_ref[species : species + 1, :], scalar)
    pre = pre_ref[rows, 0:128]
    scalar = scalar + pre * sigmoid(pre)
    if scalar_ref is not None:
        scalar_ref[rows, :] = scalar
    gate = sigmoid(pre_ref[rows, 128:256])
    parts = [scalar] + [pre_ref[rows, (a + 2) * 128 : (a + 3) * 128] * gate for a in range(3)]
    empty = jnp.zeros((BLOCK, 128), BF16)
    for order, part in enumerate(parts):
        high, low = split(part)
        here = pl.ds(order * BLOCK, BLOCK)
        used = 0 if order == 0 else 128
        for ref, value in ((feat_high, high), (feat_low, low)):
            ref[block, here, used : used + 128] = value
            ref[block, here, 128 - used : 256 - used] = empty


def add_messages(tiles, feat_high, feat_low, weight_ref, message_ref, pair_high, pair_low):
    found = [
        mm3((pair_high[slot], pair_low[slot]), (feat_high[right], feat_low[right]))
        for slot, _, right in tiles
    ]
    for (_, left, _), one in zip(tiles, found):
        total = jnp.zeros((BLOCK, 128), F32)
        for n in range(BASIS):
            rows = slice(n * BLOCK, n * BLOCK + BLOCK)
            total = total + one[rows, 0:128] * radial_row(weight_ref, 2, n)
            total = total + one[rows, 128:256] * radial_row(weight_ref, 3, n)
        message_ref[block_rows(left), :] += total


def feature_kernel(
    kinds,
    hist_ref,
    col_ref,
    weight_ref,
    mixing_ref,
    pre_ref,
    feat_high,
    feat_low,
    scalar_ref,
    fold_high,
    fold_low,
    mix_high,
    mix_low,
    fold_ref,
):
    embed = jnp.where(iota((SPAN, 128), 0) < kinds, weight_ref[0:SPAN, :], 0.0)
    scalar = jnp.concatenate([radial_row(weight_ref, 0, n) * embed for n in range(BASIS)], axis=0)
    vector = jnp.concatenate([radial_row(weight_ref, 1, n) * embed for n in range(BASIS)], axis=0)
    scalar, vector = split(scalar), split(vector)
    to_self = mm3(scalar, split(mixing_ref[0]))
    to_gate = mm3(scalar, split(mixing_ref[2]))
    to_vector = mm3(vector, split(mixing_ref[1]))
    fold_ref[...] = jnp.zeros_like(fold_ref)
    for n in range(BASIS):
        rows = slice(n * SPAN, n * SPAN + SPAN)
        base = n * 4 * SPAN
        fold_ref[base : base + SPAN, 0:128] = to_self[rows]
        fold_ref[base : base + SPAN, 128:256] = to_gate[rows]
        for a in range(3):
            here = base + (a + 1) * SPAN
            fold_ref[here : here + SPAN, (a + 2) * 128 : (a + 3) * 128] = to_vector[rows]
    fold_high[...], fold_low[...] = split(fold_ref[...])
    for part in range(2):
        mix_high[part], mix_low[part] = split(mixing_ref[3 + part])
    blocks = hist_ref.shape[0] // BLOCK
    pre_ref[...] = mm3(split(hist_ref[...]), (fold_high[...], fold_low[...]))

    def features(block, carried):
        make_features(block, col_ref, kinds, weight_ref, pre_ref, feat_high, feat_low, scalar_ref)
        return carried

    lax.fori_loop(0, blocks, features, 0)


def message_kernel(
    control_ref,
    row_ref,
    ghost_col,
    weight_ref,
    feat_high,
    feat_low,
    pair_high,
    pair_low,
    message_ref,
    swap_high,
    swap_low,
):
    blocks = feat_high.shape[0]
    message_ref[...] = jnp.zeros_like(message_ref)

    own_tiles(
        control_ref,
        lambda tiles: add_messages(
            tiles, feat_high, feat_low, weight_ref, message_ref, pair_high, pair_low
        ),
    )

    def swapped(tiles):
        for slot, left, right in tiles:
            pair_swapped(
                ghost_col, right, row_ref, left, False, swap_high.at[slot], swap_low.at[slot]
            )

    for slot in range(2):
        swapped([(slot, control_ref[slot, 0], slot)])
    single_tiles(control_ref, 0, swapped, 0)


def weighted_pull(cotangent, weight_ref, path):
    return split(
        jnp.concatenate([cotangent * radial_row(weight_ref, path, n) for n in range(BASIS)], axis=0)
    )


def add_feature_pulls(tiles, places, pull_message, weight_ref, grad_feat, swap_high, swap_low):
    weighted = []
    for _, left, _ in tiles:
        cotangent = pull_message[block_rows(left), :]
        weighted.append([weighted_pull(cotangent, weight_ref, path) for path in (2, 3)])
    found = []
    for place, (by_scalar, by_vector) in zip(places, weighted):
        high, low = swap_high.at[place], swap_low.at[place]
        to_scalar = mm3((high[0:BLOCK, :], low[0:BLOCK, :]), by_scalar)
        to_vector = mm3((high[BLOCK:, :], low[BLOCK:, :]), by_vector)
        found.append((to_scalar, to_vector))
    for (_, _, right), (to_scalar, to_vector) in zip(tiles, found):
        rows = block_rows(right)
        grad_feat[rows, 0:128] += to_scalar
        for a in range(3):
            here = slice(a * BLOCK, (a + 1) * BLOCK)
            grad_feat[rows, (a + 1) * 128 : (a + 2) * 128] += to_vector[here]


def finish(message, scalar, mix_high, mix_low, weight_ref):
    mix_message, mix_hidden = (mix_high[0], mix_low[0]), (mix_high[1], mix_low[1])
    readout = readout_row(weight_ref)
    mixed = mm3(split(message), mix_message)
    mixed_gate = sigmoid(mixed)
    final = scalar + mixed * mixed_gate
    hidden = mm3(split(final), mix_hidden)
    hidden_gate = sigmoid(hidden)
    pull_hidden = readout * (hidden_gate * (1.0 + hidden * (1.0 - hidden_gate)))
    pull_final = mm3(split(pull_hidden), mix_hidden, ROWROW)
    pull_mixed = pull_final * (mixed_gate * (1.0 + mixed * (1.0 - mixed_gate)))
    pull_message = mm3(split(pull_mixed), mix_message, ROWROW)
    return hidden * hidden_gate * readout, pull_final, pull_message


def pull_features(grad_feat, pre_ref):
    by_scalar = grad_feat[:, 0:128]
    pre = pre_ref[:, 0:128]
    own_gate = sigmoid(pre)
    gate = sigmoid(pre_ref[:, 128:256])
    by_gate = jnp.zeros_like(gate)
    by_vector = []
    for a in range(3):
        pulled = grad_feat[:, (a + 1) * 128 : (a + 2) * 128]
        by_gate = by_gate + pulled * pre_ref[:, (a + 2) * 128 : (a + 3) * 128]
        by_vector.append(pulled * gate)
    by_pre = by_scalar * (own_gate * (1.0 + pre * (1.0 - own_gate)))
    return jnp.concatenate([by_pre, by_gate * gate * (1.0 - gate)] + by_vector, axis=1)


def second_ghost_kernel(
    kinds,
    control_ref,
    mate_in,
    far_in,
    zmate_in,
    zfar_in,
    ghost_col,
    fold_high,
    fold_low,
    mix_high,
    mix_low,
    weight_ref,
    scalar_ref,
    message_in,
    pair_high,
    pair_low,
    swap_high,
    swap_low,
    mate_ref,
    far_ref,
    side_ref,
    feat_high,
    feat_low,
    pull_message,
    direct_ref,
    share_ref,
    message_ref,
    pre_ref,
    grad_feat,
):
    even_x, even_y = parities(control_ref)
    fold = (fold_high[...], fold_low[...])
    ghost_hist = pick_all((even_x, even_y, mate_in, far_in, zmate_in, zfar_in))
    pre_ref[...] = mm3(split(ghost_hist), fold)
    for block in range(2):
        make_features(block, ghost_col, kinds, weight_ref, pre_ref, feat_high, feat_low, None)
    message_ref[...] = message_in[...]

    ghost_tiles(
        control_ref,
        lambda tiles: add_messages(
            tiles, feat_high, feat_low, weight_ref, message_ref, pair_high, pair_low
        ),
    )

    share_ref[...], direct_ref[...], pull_message[...] = finish(
        message_ref[...], scalar_ref[...], mix_high, mix_low, weight_ref
    )
    grad_feat[...] = jnp.zeros_like(grad_feat)

    ghost_tiles(
        control_ref,
        lambda tiles: add_feature_pulls(
            tiles, [slot for slot, _, _ in tiles], pull_message, weight_ref, grad_feat,
            swap_high, swap_low,
        ),
    )

    ghost_pull = mm3(split(pull_features(grad_feat, pre_ref)), fold, ROWROW)
    put_packets(
        even_x,
        lambda slot: ghost_pull[slot * GHOSTS : slot * GHOSTS + GHOSTS],
        mate_ref,
        far_ref,
        side_ref,
    )


def own_pull_kernel(
    control_ref,
    col_ref,
    row_ref,
    fold_high,
    fold_low,
    weight_ref,
    pre_ref,
    pull_message,
    direct_ref,
    pull_hist_ref,
    grad_feat,
    swap_high,
    swap_low,
):
    grad_feat[:, 0:128] = direct_ref[...]
    grad_feat[:, 128:512] = jnp.zeros((direct_ref.shape[0], 384), F32)

    def backward(tiles):
        for place, (_, left, right) in enumerate(tiles):
            pair_swapped(
                col_ref, right, row_ref, left, left == right,
                swap_high.at[place], swap_low.at[place],
            )
        add_feature_pulls(
            tiles, range(len(tiles)), pull_message, weight_ref, grad_feat, swap_high, swap_low
        )

    own_tiles(control_ref, backward)
    pulled = pull_features(grad_feat, pre_ref)
    pull_hist_ref[...] = mm3(split(pulled), (fold_high[...], fold_low[...]), ROWROW)


def pair_pulls(tiles, pull_message, weight_ref, high_ref, low_ref, pull_ref):
    weighted = []
    for _, left, _ in tiles:
        cotangent = pull_message[block_rows(left), :]
        first = weighted_pull(cotangent, weight_ref, 2)
        second = weighted_pull(cotangent, weight_ref, 3)
        weighted.append(
            [jnp.concatenate([first[part], second[part]], axis=1) for part in range(2)]
        )
    found = [
        mm3(one, (high_ref[right], low_ref[right]), ROWROW)
        for one, (_, _, right) in zip(weighted, tiles)
    ]
    for one, (slot, _, _) in zip(found, tiles):
        pull_ref[slot] = one


def ghost_pair_kernel(control_ref, weight_ref, pull_message, ghost_high, ghost_low, pull_ref):
    ghost_tiles(
        control_ref,
        lambda tiles: pair_pulls(tiles, pull_message, weight_ref, ghost_high, ghost_low, pull_ref),
    )


def own_pair_kernel(
    control_ref, weight_ref, pull_message, share_ref, feat_high, feat_low, pull_ref, energy_ref
):
    energy_ref[...] = jnp.sum(share_ref[...].T, axis=0, keepdims=True)

    own_tiles(
        control_ref,
        lambda tiles: pair_pulls(tiles, pull_message, weight_ref, feat_high, feat_low, pull_ref),
    )


def add_position_pulls(
    tiles, total_ref, kind_ref, col_ref, row_ref, own, pull_in, pull_refs, grad_row, grad_col
):
    lane_basis = iota((1, 128), 1) // (4 * SPAN)
    built = []
    for _, left, right in tiles:
        parts = []
        for half in range(2):
            here = total_ref[block_rows(left), half * 128 : half * 128 + 128]
            parts += [jnp.where(lane_basis == n, here, 0.0) for n in range(4)]
        high, low = split(jnp.concatenate(parts, axis=0))
        table = kind_table(kind_ref, right)
        built.append(
            (jnp.concatenate([high, low], axis=1), jnp.concatenate([table, table], axis=1))
        )
    found = [mm(both, table, ROWROW) for both, table in built]
    for place, ((slot, _, _), one) in enumerate(zip(tiles, found)):
        pull_refs[place] = pull_in[slot] + one
    grads = [
        pair_backward(
            col_ref, left, row_ref, right, left == right if own else False, pull_refs.at[place]
        )
        for place, (_, left, right) in enumerate(tiles)
    ]
    for (_, left, right), (by_row, by_col) in zip(tiles, grads):
        grad_row[right] += by_row
        grad_col[block_rows(left), :] -= by_col


def third_ghost_kernel(
    control_ref,
    chosen_ref,
    pull_hist_ref,
    mate_in,
    far_in,
    zmate_in,
    zfar_in,
    col_ref,
    ghost_col,
    ghost_row,
    pull_in,
    out_ref,
    total_ref,
    grad_col,
    grad_ghost,
    pull_refs,
):
    even_x, even_y = parities(control_ref)
    returned = split(pick_all((even_x, even_y, mate_in, far_in, zmate_in, zfar_in)))
    chosen = chosen_ref[...]
    total_ref[...] = pull_hist_ref[...] + mm(chosen, returned[0]) + mm(chosen, returned[1])
    grad_ghost[...] = jnp.zeros_like(grad_ghost)
    grad_col[...] = jnp.zeros_like(grad_col)

    ghost_tiles(
        control_ref,
        lambda tiles: add_position_pulls(
            tiles, total_ref, ghost_col, col_ref, ghost_row, False, pull_in, pull_refs,
            grad_ghost, grad_col,
        ),
    )
    out_ref[...] = jnp.where(low_half(), grad_ghost[0], grad_ghost[1])


def third_own_kernel(
    control_ref,
    chosen_ref,
    total_ref,
    col_ref,
    row_ref,
    pull_in,
    grad_col_in,
    own_ref,
    turned_ref,
    grad_row,
    grad_col,
    pull_refs,
):
    blocks = total_ref.shape[0] // BLOCK
    turned_ref[...] = chosen_ref[...].astype(F32).T.astype(BF16)
    grad_row[...] = jnp.zeros_like(grad_row)
    grad_col[...] = grad_col_in[...]

    own_tiles(
        control_ref,
        lambda tiles: add_position_pulls(
            tiles, total_ref, col_ref, col_ref, row_ref, True, pull_in, pull_refs,
            grad_row, grad_col,
        ),
    )
    low = low_half()
    by_sender = jnp.concatenate(
        [jnp.where(low, grad_row[2 * k], grad_row[2 * k + 1]) for k in range(blocks // 2)], axis=1
    )
    own_ref[...] = by_sender + grad_col[...].T[0:8]


def last_kernel(control_ref, turned_ref, own_ref, mate_in, far_in, zmate_in, zfar_in, force_ref):
    even_x, even_y = parities(control_ref)
    returned = pick_rows(even_x, even_y, mate_in[...], far_in[...], zmate_in[...], zfar_in[...])
    total = own_ref[...] + exact_pick(returned, turned_ref[...])
    force_ref[...] = -total[0:3]


def partners(axis, far):
    count = lax.axis_size(axis)
    if far:
        return [(i, (i + (1 if i % 2 else -1)) % count) for i in range(count)]
    return [(i, i ^ 1) for i in range(count)]


def swap_both(axis, to_mate, to_far, far_first):
    def swap(value, far):
        return lax.ppermute(value, axis, partners(axis, far))

    if far_first:
        to_far, to_mate = lax.optimization_barrier((to_far, to_mate))
        far, mate = lax.optimization_barrier((swap(to_far, True), swap(to_mate, False)))
    else:
        to_mate, to_far = lax.optimization_barrier((to_mate, to_far))
        mate, far = lax.optimization_barrier((swap(to_mate, False), swap(to_far, True)))
    return mate, far


def exchange_rows(rows, beside):
    mate, far = swap_both("gx", rows, rows, True)
    far, mate, beside = lax.optimization_barrier((far, mate, beside))
    column = jnp.stack([rows, mate, far])
    zmate, zfar = swap_both("gy", column, column, False)
    return (mate, far, zmate, zfar), beside


def exchange_packets(even_y, to_mate, to_far, side, beside):
    mate, far = swap_both("gx", to_mate, to_far, True)
    far, mate, beside = lax.optimization_barrier((far, mate, beside))
    up = jnp.concatenate([mate[2:3], far[2:3], side[1:2]], axis=0)
    down = jnp.concatenate([mate[0:1], far[0:1], side[0:1]], axis=0)
    to_mate, to_far = jnp.where(even_y, up, down), jnp.where(even_y, down, up)
    zmate, zfar = swap_both("gy", to_mate, to_far, False)
    return (mate, far, zmate, zfar), beside


def struct(*shape, dtype=F32):
    return jax.ShapeDtypeStruct(shape, dtype)


def call(kernel, in_specs, outs, scratch=()):
    made = pl.pallas_call(
        kernel,
        in_specs=in_specs,
        out_specs=jax.tree.map(lambda _: VMEM, outs),
        out_shape=outs,
        scratch_shapes=list(scratch),
        compiler_params=PARAMS,
    )

    def run(*args):
        placed = [
            pltpu.with_memory_space_constraint(arg, pltpu.HBM if spec is HBM else pltpu.VMEM)
            for arg, spec in zip(args, in_specs, strict=True)
        ]
        return made(*placed)

    return run


def shards(fractions, species, send_list, tile_list, counts, embedding, radial, mixing, readout):
    atoms = fractions.shape[1]
    blocks = atoms // BLOCK
    kinds = embedding.shape[0]
    slots = tile_list.shape[1]
    parity = [lax.axis_index("gx") % 2, lax.axis_index("gy") % 2]
    even_y = parity[1] == 0
    words = jnp.stack([counts[0], *parity]).astype(jnp.int32)[None]
    far_arrays = (
        fractions,
        species[None],
        send_list,
        tile_list,
        embedding,
        radial.reshape(-1, radial.shape[2]),
        readout[None],
        mixing,
    )
    packets = [struct(3, 24, 128), struct(3, 24, 128), struct(2, 24, 128)]
    hist_struct = struct(atoms, HIST)
    col_struct = struct(atoms, 128)
    own_rows, ghost_rows = struct(blocks, 8, 128), struct(2, 8, 128)
    fold_halves = [struct(HIST, 640, dtype=BF16)] * 2
    mix_halves = [struct(2, 128, 128, dtype=BF16)] * 2
    own_halves = [struct(blocks, 256, 256, dtype=BF16)] * 2
    ghost_halves = [struct(2, 256, 256, dtype=BF16)] * 2
    pairs = [struct(slots, BASIS * BLOCK, 256, dtype=BF16)] * 2
    swaps = [struct(slots, 256, BASIS * BLOCK, dtype=BF16)] * 2
    pulls = struct(slots, BASIS * BLOCK, 256)

    site, rows, send, tiles = call(
        pack_kernel,
        [HBM] * 4,
        [
            struct(8, atoms), struct(8, 128),
            struct(*send_list.shape, dtype=jnp.int32), struct(8, 128, dtype=jnp.int32),
        ],
        [
            pltpu.VMEM(fractions.shape, F32),
            pltpu.VMEM((1, atoms), jnp.int32),
            pltpu.VMEM(tile_list.shape, jnp.int32),
            pltpu.SemaphoreType.DMA((4,)),
        ],
    )(*far_arrays[0:4])
    prepared = call(
        functools.partial(prepare_kernel, slots),
        [VMEM] * 4 + [HBM] * 4,
        [
            struct(8, 128, dtype=jnp.int32), col_struct, own_rows,
            struct(atoms, 128, dtype=BF16),
        ]
        + [struct(2 * SPAN + 4 * BASIS, 128), struct(*mixing.shape)],
        [pltpu.SemaphoreType.DMA((4,))],
    )(words, tiles, site, send, *far_arrays[4:])
    arrived, prepared = exchange_rows(rows, prepared)
    control, col, row, chosen, weights, mixers = prepared
    hist, own_high, own_low = call(
        own_histogram_kernel, [VMEM] * 3, [hist_struct] + pairs
    )(control, col, row)
    hist, to_mate, to_far, side, ghost_col, ghost_row, pair_high, pair_low = call(
        first_kernel,
        [VMEM] * 8,
        [hist_struct] + packets + [struct(8 * GHOSTS, 128), ghost_rows] + pairs,
        [
            pltpu.VMEM((8 * GHOSTS, HIST), F32),
            pltpu.SMEM(send_list.shape, jnp.int32),
            pltpu.SemaphoreType.DMA,
        ],
    )(control, send, hist, col, *arrived)
    features = call(
        functools.partial(feature_kernel, kinds),
        [VMEM] * 4,
        [struct(atoms, 640)] + own_halves + [col_struct] + fold_halves + mix_halves,
        [pltpu.VMEM((HIST, 640), F32)],
    )(hist, col, weights, mixers)
    arrived, features = exchange_packets(even_y, to_mate, to_far, side, features)
    pre, feat_high, feat_low, scalar, *folded = features
    fold, mix = folded[0:2], folded[2:4]
    message, swap_high, swap_low = call(message_kernel, [VMEM] * 8, [col_struct] + swaps)(
        control, row, ghost_col, weights, feat_high, feat_low, own_high, own_low
    )
    (
        to_mate, to_far, side, ghost_high, ghost_low, pull_message, direct, share,
    ) = call(
        functools.partial(second_ghost_kernel, kinds),
        [VMEM] * 17,
        packets + ghost_halves + [col_struct] * 3,
        [
            pltpu.VMEM((atoms, 128), F32),
            pltpu.VMEM((8 * GHOSTS, 640), F32),
            pltpu.VMEM((8 * GHOSTS, 512), F32),
        ],
    )(
        control, *arrived, ghost_col, *fold, *mix, weights, scalar, message,
        pair_high, pair_low, swap_high, swap_low,
    )
    pull = call(ghost_pair_kernel, [VMEM] * 5, pulls)(
        control, weights, pull_message, ghost_high, ghost_low
    )
    arrived, (pull, direct) = exchange_packets(even_y, to_mate, to_far, side, (pull, direct))
    pull_hist = call(
        own_pull_kernel,
        [VMEM] * 9,
        hist_struct,
        [pltpu.VMEM((atoms, 512), F32)] + [pltpu.VMEM((4, 256, BASIS * BLOCK), BF16)] * 2,
    )(control, col, row, *fold, weights, pre, pull_message, direct)
    rows, total, grad_col = call(
        third_ghost_kernel,
        [VMEM] * 11,
        [struct(8, 128), hist_struct, col_struct],
        [pltpu.VMEM((2, 8, 128), F32), pltpu.VMEM((4, BASIS * BLOCK, 256), F32)],
    )(control, chosen, pull_hist, *arrived, col, ghost_col, ghost_row, pull)
    share, rows = lax.optimization_barrier((share, rows))
    own_pair = call(own_pair_kernel, [VMEM] * 6, [pulls, struct(1, atoms)])(
        control, weights, pull_message, share, feat_high, feat_low
    )
    arrived, own_pair = exchange_rows(rows, own_pair)
    pull, energy = own_pair
    own, turned = call(
        third_own_kernel,
        [VMEM] * 7,
        [struct(8, atoms), struct(128, atoms, dtype=BF16)],
        [
            pltpu.VMEM((blocks, 8, 128), F32),
            pltpu.VMEM((atoms, 128), F32),
            pltpu.VMEM((4, BASIS * BLOCK, 256), F32),
        ],
    )(control, chosen, total, col, row, pull, grad_col)
    forces = call(last_kernel, [VMEM] * 7, struct(3, atoms))(control, turned, own, *arrived)
    return energy[0], forces


def solution(mesh):
    placed = (
        P(None, ("gx", "gy")),
        P(("gx", "gy")),
        P(None, ("gx", "gy")),
        P(None, ("gx", "gy")),
        P(("gx", "gy")),
        P(),
        P(),
        P(),
        P(),
    )
    return jax.shard_map(
        shards,
        mesh=mesh,
        in_specs=placed,
        out_specs=(P(("gx", "gy")), P(None, ("gx", "gy"))),
        check_vma=False,
    )
```

```python
import functools

import jax
import jax.numpy as jnp
from jax import lax
from jax.experimental import pallas as pl
from jax.experimental.pallas import tpu as pltpu
from jax.sharding import PartitionSpec as P

F32 = jnp.float32
BF16 = jnp.bfloat16

BASIS = 8
BLOCK = 64
GHOSTS = 16
SPAN = 8
HIST = BASIS * 4 * SPAN
OFFSETS = ((-1, -1), (-1, 0), (-1, 1), (0, -1), (0, 1), (1, -1), (1, 0), (1, 1))
WIDTHS = (12.0, 12.0, 36.0)
CUT_INV = 1.0 / 25.0
ROOT = 1.6986436005760381
STEP = ROOT * 0.6
MIDDLE = 1.0 + 0.6 * (BASIS - 1) / 2
REACH = 5.125
ROWS = 32

VMEM = pl.BlockSpec(memory_space=pltpu.VMEM)
HBM = pl.BlockSpec(memory_space=pltpu.HBM)
PARAMS = pltpu.CompilerParams(vmem_limit_bytes=16 * 1024 * 1024)

ROWROW = (((1,), (1,)), ((), ()))
ROWCOL = (((1,), (0,)), ((), ()))


def split(value):
    high = value.astype(BF16)
    return high, (value - high.astype(F32)).astype(BF16)


def mm(left, right, dims=ROWCOL):
    return lax.dot_general(left, right, dims, preferred_element_type=F32)


def mm3(left, right, dims=ROWCOL):
    (lh, ll), (rh, rl) = left, right
    summed = dims[0][1][0]
    return mm(
        jnp.concatenate([lh, ll, lh], axis=1), jnp.concatenate([rh, rh, rl], axis=summed), dims
    )


def sigmoid(value):
    return 1.0 / (1.0 + jnp.exp(-value))


def iota(shape, dim):
    return lax.broadcasted_iota(jnp.int32, shape, dim)


def low_half():
    return iota((1, 128), 1) < BLOCK


def pick_rows(even_x, even_y, mate, far, zmate, zfar):
    x_up, x_down = jnp.where(even_x, mate, far), jnp.where(even_x, far, mate)
    y_up = [jnp.where(even_y, zmate[i], zfar[i]) for i in range(3)]
    y_down = [jnp.where(even_y, zfar[i], zmate[i]) for i in range(3)]
    sources = {
        (1, 0): x_up,
        (-1, 0): x_down,
        (0, 1): y_up[0],
        (0, -1): y_down[0],
        (1, 1): jnp.where(even_x, y_up[1], y_up[2]),
        (-1, 1): jnp.where(even_x, y_up[2], y_up[1]),
        (1, -1): jnp.where(even_x, y_down[1], y_down[2]),
        (-1, -1): jnp.where(even_x, y_down[2], y_down[1]),
    }
    slot_of = iota((8, 128), 1) // GHOSTS
    total = jnp.zeros((8, 128), F32)
    for slot, offset in enumerate(OFFSETS):
        turned = pltpu.roll(sources[offset], ((2 * slot - 7) * GHOSTS) % 128, 1)
        total = jnp.where(slot_of == slot, turned, total)
    return total


def pick_slot(slot, even_x, even_y, mate, far, zmate, zfar):
    along_x, along_y = OFFSETS[slot]
    if along_y == 0:
        near = even_x if along_x == 1 else jnp.logical_not(even_x)
        return jnp.where(near, mate[1], far[1])
    near = even_y if along_y == 1 else jnp.logical_not(even_y)
    if along_x == 0:
        return jnp.where(near, zmate[2], zfar[2])
    first = even_x if along_x == 1 else jnp.logical_not(even_x)
    return jnp.where(
        near, jnp.where(first, zmate[0], zmate[1]), jnp.where(first, zfar[0], zfar[1])
    )


def pick_all(args):
    return jnp.concatenate([unpack(pick_slot(slot, *args)) for slot in range(8)], axis=0)


def pack(rows):
    free = iota((8, 128), 1) % SPAN >= 6
    carried = rows[8:16, 128:256]
    quarters = (rows[0:8, 0:128], rows[8:16, 0:128], rows[0:8, 128:256])
    return jnp.concatenate(
        [
            jnp.where(free, pltpu.roll(carried, 6 - 2 * part, 1), quarter)
            for part, quarter in enumerate(quarters)
        ],
        axis=0,
    )


def unpack(packet):
    place = iota((8, 128), 1) % SPAN
    turned = [
        pltpu.roll(packet[8 * part : 8 * part + 8], 128 - (6 - 2 * part), 1) for part in range(3)
    ]
    carried = jnp.where(place < 2, turned[0], jnp.where(place < 4, turned[1], turned[2]))
    return jnp.concatenate(
        [packet[0:16], jnp.concatenate([packet[16:24], carried], axis=0)], axis=1
    )


def put_packets(even_x, piece, mate_ref, far_ref, side_ref):
    for part in range(3):
        down, up = pack(piece(part)), pack(piece(5 + part))
        mate_ref[part] = jnp.where(even_x, up, down)
        far_ref[part] = jnp.where(even_x, down, up)
    side_ref[0] = pack(piece(3))
    side_ref[1] = pack(piece(4))


def send_columns(send):
    wide = jnp.concatenate([send] * 8, axis=1)
    own = iota((8, 128), 1) // GHOSTS == iota((8, 128), 0)
    return jnp.sum(jnp.where(own, wide, 0), axis=0, keepdims=True)


def chooser(send, atoms):
    return iota((atoms, 128), 0) == send_columns(send)


def block_rows(block, start=0, count=BLOCK):
    return pl.ds(pl.multiple_of(block * BLOCK, BLOCK) + start, count)


def separation(col_ref, col_block, row_ref, row_block, start, sign):
    mine = col_ref[block_rows(col_block, start, ROWS), :]
    other = row_ref[row_block]
    return [sign * (other[a : a + 1, :] - mine[:, a : a + 1]) for a in range(3)]


def envelope(parts, same, start):
    dist_sq = parts[0] * parts[0] + parts[1] * parts[1] + parts[2] * parts[2]
    soft = jnp.sqrt(dist_sq + 1.0)
    rows = iota((ROWS, 128), 0) + start
    columns = iota((ROWS, 128), 1) % BLOCK
    apart = jnp.where(jnp.logical_and(rows == columns, same), 0.0, 1.0)
    margin = jnp.maximum(1.0 - dist_sq * CUT_INV, 0.0) * apart
    return soft, margin


def angular(parts, inverse):
    u = [part * inverse for part in parts]
    low = low_half()
    return jnp.where(low, 1.0, u[0]), jnp.where(low, u[1], u[2])


def basis_scale(shape):
    step = (iota(shape, 0) % BASIS).astype(F32) - (BASIS - 1) / 2
    return jnp.exp2(-(STEP * STEP) * (step * step))


def centered(soft):
    return ROOT * (jnp.minimum(soft, REACH) - MIDDLE)


def pair_forward(col_ref, left, row_ref, right, same, high_ref, low_ref):
    for start in range(0, BLOCK, ROWS):
        parts = separation(col_ref, left, row_ref, right, start, 1.0)
        soft, margin = envelope(parts, same, start)
        first, second = angular(parts, 1.0 / soft)
        z = centered(soft)
        bell = jnp.exp2(-z * (z + (BASIS - 1) * STEP)) * (margin * margin)
        growth = jnp.exp2((2.0 * STEP) * z)
        for n in range(BASIS):
            here = pl.ds(n * BLOCK + start, ROWS)
            for half, factor in enumerate((first, second)):
                high, low = split(bell * factor)
                high_ref[here, half * 128 : half * 128 + 128] = high
                low_ref[here, half * 128 : half * 128 + 128] = low
            bell = bell * growth


def pair_swapped(col_ref, right, row_ref, left, same, high_ref, low_ref):
    low_lanes = low_half()
    for start in range(0, BLOCK, ROWS):
        parts = separation(col_ref, right, row_ref, left, start, -1.0)
        soft, margin = envelope(parts, same, start)
        inverse = 1.0 / soft
        u = [part * inverse for part in parts]
        z = centered(soft)
        bell = jnp.exp2(-z * (z + jnp.where(low_lanes, (BASIS - 1) * STEP, (BASIS - 3) * STEP)))
        bell = bell * (margin * margin)
        growth = jnp.exp2((4.0 * STEP) * z)
        for pair in range(BASIS // 2):
            for order in range(4):
                high, low = split(bell if order == 0 else bell * u[order - 1])
                here = pl.ds(order * BLOCK + start, ROWS)
                high_ref[here, pair * 128 : pair * 128 + 128] = high
                low_ref[here, pair * 128 : pair * 128 + 128] = low
            bell = bell * growth


def pair_backward(col_ref, left, row_ref, right, same, pull_ref):
    low_lanes = low_half()
    lane = iota((1, 128), 1)
    sums = [jnp.zeros((1, 128), F32) for _ in range(3)]
    columns = []
    for start in range(0, BLOCK, ROWS):
        parts = separation(col_ref, left, row_ref, right, start, 1.0)
        soft, margin = envelope(parts, same, start)
        inverse = 1.0 / soft
        first, second = angular(parts, inverse)
        z = centered(soft)
        bell = jnp.exp2(-z * (z - (BASIS - 1) * STEP))
        shrink = jnp.exp2((-2.0 * STEP) * z)
        by_first = jnp.zeros((ROWS, 128), F32)
        by_second = jnp.zeros((ROWS, 128), F32)
        count_first = jnp.zeros((ROWS, 128), F32)
        count_second = jnp.zeros((ROWS, 128), F32)
        for n in reversed(range(BASIS)):
            here = pl.ds(n * BLOCK + start, ROWS)
            by_first = by_first + bell * pull_ref[here, 0:128]
            by_second = by_second + bell * pull_ref[here, 128:256]
            if n > 0:
                count_first = count_first + by_first
                count_second = count_second + by_second
                bell = bell * shrink
        weight = margin * margin
        by_bell = first * by_first + second * by_second
        by_count = first * count_first + second * count_second
        by_bell = by_bell + pltpu.roll(by_bell, BLOCK, 1)
        by_count = by_count + pltpu.roll(by_count, BLOCK, 1)
        by_shift = (ROOT * (soft - 1.0) * by_bell - STEP * by_count) * weight
        by_first, by_second = by_first * weight, by_second * weight
        turned = pltpu.roll(by_second, BLOCK, 1)
        by_u = [
            jnp.where(low_lanes, pltpu.roll(by_first, BLOCK, 1), by_first),
            jnp.where(low_lanes, by_second, turned),
            jnp.where(low_lanes, turned, by_second),
        ]
        along = (by_u[0] * parts[0] + by_u[1] * parts[1] + by_u[2] * parts[2]) * inverse
        by_soft = by_shift * (-4.0 / ROOT) - along * inverse
        radial_part = by_soft * inverse + by_bell * (margin * (-4.0 * CUT_INV))
        column = jnp.zeros((ROWS, 128), F32)
        for a in range(3):
            force = by_u[a] * inverse + parts[a] * radial_part
            sums[a] = sums[a] + jnp.sum(force, axis=0, keepdims=True)
            total = jnp.sum(jnp.where(low_lanes, force, 0.0), axis=1, keepdims=True)
            column = jnp.where(lane == a, total, column)
        columns.append(column)
    return (
        jnp.concatenate(sums + [jnp.zeros((5, 128), F32)], axis=0),
        jnp.concatenate(columns, axis=0),
    )


def kind_table(col_ref, block):
    kind = col_ref[block_rows(block), 3:4].astype(jnp.int32)
    lane = iota((BLOCK, 128), 1)
    hit = kind == lane % SPAN
    return jnp.concatenate(
        [
            jnp.where(jnp.logical_and(hit, lane // SPAN % 4 == order), 1.0, 0.0)
            for order in range(4)
        ],
        axis=0,
    ).astype(BF16)


def parities(control_ref):
    return control_ref[1, 2] == 0, control_ref[2, 2] == 0


def fill_control(control_ref, words_ref, tiles_ref, slots, own_blocks):
    row, lane = iota((8, 128), 0), iota((8, 128), 1)
    live = words_ref[0, 0]
    table = jnp.where(lane < 2, tiles_ref[...], 0)
    lengths = [jnp.int32(0), jnp.int32(0)]
    for slot in range(2, slots):
        left, right = tiles_ref[slot, 0], tiles_ref[slot, 1]
        for which in range(2):
            ghost = which == 0
            sending = right - own_blocks if ghost else right
            member = (slot < live) & ((right >= own_blocks) if ghost else (right < own_blocks))
            first = 3 + 3 * which
            entry = jnp.where(lane == first, slot, jnp.where(lane == first + 1, left, sending))
            place = (lane >= first) & (lane < first + 3) & (row == lengths[which]) & member
            table = jnp.where(place, entry, table)
            lengths[which] = lengths[which] + member.astype(jnp.int32)
    for place, word in enumerate([live, words_ref[0, 1], words_ref[0, 2], *lengths]):
        table = jnp.where((lane == 2) & (row == place), word, table)
    control_ref[...] = table


def listed_tile(control_ref, which, place):
    first = 3 + 3 * which
    return tuple(control_ref[place, first + k] for k in range(3))


def single_tiles(control_ref, which, work, start):
    def step(place, carried):
        work([listed_tile(control_ref, which, place)])
        return carried

    lax.fori_loop(start, control_ref[3 + which, 2], step, 0)


def own_tiles(control_ref, work):
    count = control_ref[4, 2]

    def group(place, size):
        work([listed_tile(control_ref, 1, place + k) for k in range(size)])

    def step(quarter, carried):
        group(4 * quarter, 4)
        return carried

    lax.fori_loop(0, count // 4, step, 0)
    rest = count % 4

    @pl.when(rest >= 2)
    def _():
        group(count - rest, 2)

    @pl.when(rest % 2 == 1)
    def _():
        group(count - 1, 1)


def ghost_tiles(control_ref, work):
    more = control_ref[3, 2]

    def fixed():
        return [(slot, control_ref[slot, 0], slot) for slot in range(2)]

    @pl.when(more == 0)
    def _():
        work(fixed())

    @pl.when(more > 0)
    def _():
        @pl.when(more == 1)
        def _():
            work(fixed() + [listed_tile(control_ref, 0, 0)])

        @pl.when(more > 1)
        def _():
            work(fixed() + [listed_tile(control_ref, 0, place) for place in range(2)])
            single_tiles(control_ref, 0, work, 2)


def exact_pick(rows, chosen):
    high = rows.astype(BF16).astype(F32)
    rest = rows - high
    middle = rest.astype(BF16).astype(F32)
    stacked = jnp.concatenate(
        [high, middle, rest - middle, jnp.zeros_like(rows)], axis=0
    ).astype(BF16)
    picked = mm(stacked, chosen)
    return picked[0:8] + picked[8:16] + picked[16:24]


def fetch(pairs, sems):
    copies = [
        pltpu.make_async_copy(source, target, sems.at[i]) for i, (source, target) in enumerate(pairs)
    ]
    for copy in copies:
        copy.start()
    return copies


def pack_kernel(
    frac_in,
    kind_in,
    send_in,
    tile_in,
    site_ref,
    out_ref,
    send_ref,
    tiles_ref,
    frac_ref,
    kind_ref,
    tile_ref,
    sems,
):
    copies = fetch(
        (
            (frac_in, frac_ref),
            (kind_in, kind_ref),
            (send_in, send_ref),
            (tile_in, tile_ref),
        ),
        sems,
    )
    for copy in copies:
        copy.wait()
    atoms = frac_ref.shape[1]
    rows = jnp.concatenate(
        [frac_ref[...], kind_ref[...].astype(F32), jnp.zeros((4, atoms), F32)], axis=0
    )
    site_ref[...] = rows
    out_ref[...] = exact_pick(rows, chooser(send_ref[...], atoms).astype(F32).astype(BF16))
    slots = tile_ref.shape[1]
    lines = jnp.concatenate([tile_ref[...].astype(F32), jnp.zeros((2, 128 - slots), F32)], axis=1)
    lines = jnp.concatenate([lines, jnp.zeros((126, 128), F32)], axis=0)
    tiles_ref[...] = lines.T[0:8].astype(jnp.int32)


def doubled(rows, block):
    chunk = rows[:, block // 2 * 128 : block // 2 * 128 + 128]
    turned = pltpu.roll(chunk, BLOCK, 1)
    low = low_half()
    return jnp.where(low, chunk, turned) if block % 2 == 0 else jnp.where(low, turned, chunk)


def upright(rows):
    return jnp.concatenate([rows, jnp.zeros((120, rows.shape[1]), F32)], axis=0).T


def radial_row(weight_ref, path, n):
    row = SPAN + path * BASIS + n
    return weight_ref[row : row + 1, :]


def readout_row(weight_ref):
    row = SPAN + 4 * BASIS
    return weight_ref[row : row + 1, :]


def axis_scale():
    row = iota((8, 128), 0)
    return jnp.where(row < 2, WIDTHS[0], jnp.where(row == 2, WIDTHS[2], 1.0))


def add_histograms(tiles, col_ref, row_ref, own, kind_ref, hist_ref, pair_high, pair_low):
    for slot, left, right in tiles:
        same = left == right if own else False
        pair_forward(col_ref, left, row_ref, right, same, pair_high.at[slot], pair_low.at[slot])
    tables = [kind_table(kind_ref, right) for _, _, right in tiles]
    found = [
        mm(pair_high[slot], table) + mm(pair_low[slot], table)
        for (slot, _, _), table in zip(tiles, tables)
    ]
    lane_basis = iota((1, 128), 1) // (4 * SPAN)
    for (_, left, _), one in zip(tiles, found):
        for half in range(2):
            total = jnp.zeros((BLOCK, 128), F32)
            for n in range(4):
                begin = (half * 4 + n) * BLOCK
                total = jnp.where(lane_basis == n, one[begin : begin + BLOCK], total)
            hist_ref[block_rows(left), half * 128 : half * 128 + 128] += total


def own_histogram_kernel(
    control_ref, col_ref, row_ref, hist_ref, pair_high, pair_low
):
    hist_ref[...] = jnp.zeros_like(hist_ref)
    own_tiles(
        control_ref,
        lambda tiles: add_histograms(
            tiles, col_ref, row_ref, True, col_ref, hist_ref, pair_high, pair_low
        ),
    )


def prepare_kernel(
    slots,
    words_ref,
    tiles_ref,
    site_ref,
    send_ref,
    embed_in,
    radial_in,
    readout_in,
    mixing_in,
    control_ref,
    col_ref,
    row_ref,
    chosen_ref,
    weight_ref,
    mixing_ref,
    sems,
):
    kinds = embed_in.shape[0]
    paths = radial_in.shape[0]
    copies = fetch(
        (
            (embed_in, weight_ref.at[pl.ds(0, kinds)]),
            (radial_in, weight_ref.at[pl.ds(SPAN, paths)]),
            (readout_in, weight_ref.at[pl.ds(SPAN + paths, 1)]),
            (mixing_in, mixing_ref),
        ),
        sems,
    )
    atoms = site_ref.shape[1]
    blocks = atoms // BLOCK
    fill_control(control_ref, words_ref, tiles_ref, slots, blocks)
    own = site_ref[...] * axis_scale()[:, 0:1]
    col_ref[...] = upright(own)
    for block in range(blocks):
        row_ref[block] = doubled(own, block)
    chosen_ref[...] = chooser(send_ref[...], atoms).astype(F32).astype(BF16)
    for copy in copies:
        copy.wait()
    radial = weight_ref[SPAN : SPAN + paths, :]
    weight_ref[SPAN : SPAN + paths, :] = radial * basis_scale(radial.shape)


def first_kernel(
    control_ref,
    send_in,
    hist_in,
    col_ref,
    mate_in,
    far_in,
    zmate_in,
    zfar_in,
    hist_ref,
    mate_ref,
    far_ref,
    side_ref,
    ghost_col,
    ghost_row,
    pair_high,
    pair_low,
    gather_ref,
    send_ref,
    sem,
):
    fetching = pltpu.make_async_copy(send_in, send_ref, sem)
    fetching.start()
    even_x, even_y = parities(control_ref)
    ghosts = pick_rows(even_x, even_y, mate_in[...], far_in[...], zmate_in[...], zfar_in[...])
    row = iota((8, 128), 0)
    slot = iota((8, 128), 1) // GHOSTS
    shift_x = jnp.where(slot < 3, -1.0, jnp.where(slot < 5, 0.0, 1.0))
    down = (slot == 0) | (slot == 3) | (slot == 5)
    level = (slot == 1) | (slot == 6)
    shift_y = jnp.where(down, -1.0, jnp.where(level, 0.0, 1.0))
    shift = jnp.where(row == 0, shift_x, jnp.where(row == 1, shift_y, 0.0))
    ghosts = (ghosts + shift) * axis_scale()
    ghost_col[...] = upright(ghosts)
    for block in range(2):
        ghost_row[block] = doubled(ghosts, block)
    hist_ref[...] = hist_in[...]

    ghost_tiles(
        control_ref,
        lambda tiles: add_histograms(
            tiles, col_ref, ghost_row, False, ghost_col, hist_ref, pair_high, pair_low
        ),
    )
    fetching.wait()

    up, down = jnp.where(even_x, 5, 0), jnp.where(even_x, 0, 5)
    places = [(mate_ref, part, up + part) for part in range(3)]
    places += [(far_ref, part, down + part) for part in range(3)]
    places += [(side_ref, part, 3 + part) for part in range(2)]
    for place, (_, _, slot) in enumerate(places):
        for entry in range(GHOSTS):
            row = place * GHOSTS + entry
            gather_ref[row : row + 1, :] = hist_ref[pl.ds(send_ref[slot, entry], 1), :]
    for place, (ref, part, _) in enumerate(places):
        ref[part] = pack(gather_ref[place * GHOSTS : place * GHOSTS + GHOSTS, :])


def make_features(block, col_ref, kinds, weight_ref, pre_ref, feat_high, feat_low, scalar_ref, gate_ref):
    rows = block_rows(block)
    kind = col_ref[rows, 3:4].astype(jnp.int32)
    scalar = jnp.zeros((BLOCK, 128), F32)
    for species in range(kinds):
        scalar = jnp.where(kind == species, weight_ref[species : species + 1, :], scalar)
    pre = pre_ref[rows, 0:128]
    own_gate = sigmoid(pre)
    scalar = scalar + pre * own_gate
    if scalar_ref is not None:
        scalar_ref[rows, :] = scalar
    gate = sigmoid(pre_ref[rows, 128:256])
    if gate_ref is not None:
        gate_ref[rows, 0:128] = own_gate
        gate_ref[rows, 128:256] = gate
    parts = [scalar] + [pre_ref[rows, (a + 2) * 128 : (a + 3) * 128] * gate for a in range(3)]
    empty = jnp.zeros((BLOCK, 128), BF16)
    for order, part in enumerate(parts):
        high, low = split(part)
        here = pl.ds(order * BLOCK, BLOCK)
        used = 0 if order == 0 else 128
        for ref, value in ((feat_high, high), (feat_low, low)):
            ref[block, here, used : used + 128] = value
            ref[block, here, 128 - used : 256 - used] = empty


def add_messages(tiles, feat_high, feat_low, weight_ref, message_ref, pair_high, pair_low):
    found = [
        mm3((pair_high[slot], pair_low[slot]), (feat_high[right], feat_low[right]))
        for slot, _, right in tiles
    ]
    for (_, left, _), one in zip(tiles, found):
        total = jnp.zeros((BLOCK, 128), F32)
        for n in range(BASIS):
            rows = slice(n * BLOCK, n * BLOCK + BLOCK)
            total = total + one[rows, 0:128] * radial_row(weight_ref, 2, n)
            total = total + one[rows, 128:256] * radial_row(weight_ref, 3, n)
        message_ref[block_rows(left), :] += total


def feature_kernel(
    kinds,
    hist_ref,
    col_ref,
    weight_ref,
    mixing_ref,
    pre_ref,
    feat_high,
    feat_low,
    scalar_ref,
    fold_high,
    fold_low,
    mix_high,
    mix_low,
    fold_ref,
):
    embed = jnp.where(iota((SPAN, 128), 0) < kinds, weight_ref[0:SPAN, :], 0.0)
    scalar = jnp.concatenate([radial_row(weight_ref, 0, n) * embed for n in range(BASIS)], axis=0)
    vector = jnp.concatenate([radial_row(weight_ref, 1, n) * embed for n in range(BASIS)], axis=0)
    scalar, vector = split(scalar), split(vector)
    to_self = mm3(scalar, split(mixing_ref[0]))
    to_gate = mm3(scalar, split(mixing_ref[2]))
    to_vector = mm3(vector, split(mixing_ref[1]))
    fold_ref[...] = jnp.zeros_like(fold_ref)
    for n in range(BASIS):
        rows = slice(n * SPAN, n * SPAN + SPAN)
        base = n * 4 * SPAN
        fold_ref[base : base + SPAN, 0:128] = to_self[rows]
        fold_ref[base : base + SPAN, 128:256] = to_gate[rows]
        for a in range(3):
            here = base + (a + 1) * SPAN
            fold_ref[here : here + SPAN, (a + 2) * 128 : (a + 3) * 128] = to_vector[rows]
    fold_high[...], fold_low[...] = split(fold_ref[...])
    for part in range(2):
        mix_high[part], mix_low[part] = split(mixing_ref[3 + part])
    blocks = hist_ref.shape[0] // BLOCK
    pre_ref[...] = mm3(split(hist_ref[...]), (fold_high[...], fold_low[...]))

    def features(block, carried):
        make_features(
            block, col_ref, kinds, weight_ref, pre_ref, feat_high, feat_low, scalar_ref, None
        )
        return carried

    lax.fori_loop(0, blocks, features, 0)


def message_kernel(
    control_ref,
    row_ref,
    ghost_col,
    weight_ref,
    feat_high,
    feat_low,
    pair_high,
    pair_low,
    message_ref,
    swap_high,
    swap_low,
):
    blocks = feat_high.shape[0]
    message_ref[...] = jnp.zeros_like(message_ref)

    own_tiles(
        control_ref,
        lambda tiles: add_messages(
            tiles, feat_high, feat_low, weight_ref, message_ref, pair_high, pair_low
        ),
    )

    def swapped(tiles):
        for slot, left, right in tiles:
            pair_swapped(
                ghost_col, right, row_ref, left, False, swap_high.at[slot], swap_low.at[slot]
            )

    for slot in range(2):
        swapped([(slot, control_ref[slot, 0], slot)])
    single_tiles(control_ref, 0, swapped, 0)


def weighted_pull(cotangent, weight_ref, path):
    return split(
        jnp.concatenate([cotangent * radial_row(weight_ref, path, n) for n in range(BASIS)], axis=0)
    )


def add_feature_pulls(tiles, places, pull_message, weight_ref, grad_feat, swap_high, swap_low):
    weighted = []
    for _, left, _ in tiles:
        cotangent = pull_message[block_rows(left), :]
        weighted.append([weighted_pull(cotangent, weight_ref, path) for path in (2, 3)])
    found = []
    for place, (by_scalar, by_vector) in zip(places, weighted):
        high, low = swap_high.at[place], swap_low.at[place]
        to_scalar = mm3((high[0:BLOCK, :], low[0:BLOCK, :]), by_scalar)
        to_vector = mm3((high[BLOCK:, :], low[BLOCK:, :]), by_vector)
        found.append((to_scalar, to_vector))
    for (_, _, right), (to_scalar, to_vector) in zip(tiles, found):
        rows = block_rows(right)
        grad_feat[rows, 0:128] += to_scalar
        for a in range(3):
            here = slice(a * BLOCK, (a + 1) * BLOCK)
            grad_feat[rows, (a + 1) * 128 : (a + 2) * 128] += to_vector[here]


def finish(message, scalar, mix_high, mix_low, weight_ref):
    mix_message, mix_hidden = (mix_high[0], mix_low[0]), (mix_high[1], mix_low[1])
    readout = readout_row(weight_ref)
    mixed = mm3(split(message), mix_message)
    mixed_gate = sigmoid(mixed)
    final = scalar + mixed * mixed_gate
    hidden = mm3(split(final), mix_hidden)
    hidden_gate = sigmoid(hidden)
    pull_hidden = readout * (hidden_gate * (1.0 + hidden * (1.0 - hidden_gate)))
    pull_final = mm3(split(pull_hidden), mix_hidden, ROWROW)
    pull_mixed = pull_final * (mixed_gate * (1.0 + mixed * (1.0 - mixed_gate)))
    pull_message = mm3(split(pull_mixed), mix_message, ROWROW)
    return hidden * hidden_gate * readout, pull_final, pull_message


def pull_features(grad_feat, pre_ref, gate_ref=None):
    by_scalar = grad_feat[:, 0:128]
    pre = pre_ref[:, 0:128]
    if gate_ref is None:
        own_gate, gate = sigmoid(pre), sigmoid(pre_ref[:, 128:256])
    else:
        own_gate, gate = gate_ref[:, 0:128], gate_ref[:, 128:256]
    by_gate = jnp.zeros_like(gate)
    by_vector = []
    for a in range(3):
        pulled = grad_feat[:, (a + 1) * 128 : (a + 2) * 128]
        by_gate = by_gate + pulled * pre_ref[:, (a + 2) * 128 : (a + 3) * 128]
        by_vector.append(pulled * gate)
    by_pre = by_scalar * (own_gate * (1.0 + pre * (1.0 - own_gate)))
    return jnp.concatenate([by_pre, by_gate * gate * (1.0 - gate)] + by_vector, axis=1)


def second_ghost_kernel(
    kinds,
    control_ref,
    mate_in,
    far_in,
    zmate_in,
    zfar_in,
    ghost_col,
    fold_high,
    fold_low,
    mix_high,
    mix_low,
    weight_ref,
    scalar_ref,
    message_in,
    pair_high,
    pair_low,
    swap_high,
    swap_low,
    mate_ref,
    far_ref,
    side_ref,
    feat_high,
    feat_low,
    pull_message,
    direct_ref,
    share_ref,
    message_ref,
    pre_ref,
    grad_feat,
    gate_ref,
):
    even_x, even_y = parities(control_ref)
    fold = (fold_high[...], fold_low[...])
    ghost_hist = pick_all((even_x, even_y, mate_in, far_in, zmate_in, zfar_in))
    pre_ref[...] = mm3(split(ghost_hist), fold)
    for block in range(2):
        make_features(
            block, ghost_col, kinds, weight_ref, pre_ref, feat_high, feat_low, None, gate_ref
        )
    message_ref[...] = message_in[...]

    ghost_tiles(
        control_ref,
        lambda tiles: add_messages(
            tiles, feat_high, feat_low, weight_ref, message_ref, pair_high, pair_low
        ),
    )

    share_ref[...], direct_ref[...], pull_message[...] = finish(
        message_ref[...], scalar_ref[...], mix_high, mix_low, weight_ref
    )
    grad_feat[...] = jnp.zeros_like(grad_feat)

    ghost_tiles(
        control_ref,
        lambda tiles: add_feature_pulls(
            tiles, [slot for slot, _, _ in tiles], pull_message, weight_ref, grad_feat,
            swap_high, swap_low,
        ),
    )

    ghost_pull = mm3(split(pull_features(grad_feat, pre_ref, gate_ref)), fold, ROWROW)
    put_packets(
        even_x,
        lambda slot: ghost_pull[slot * GHOSTS : slot * GHOSTS + GHOSTS],
        mate_ref,
        far_ref,
        side_ref,
    )


def own_pull_kernel(
    control_ref,
    col_ref,
    row_ref,
    fold_high,
    fold_low,
    weight_ref,
    pre_ref,
    pull_message,
    direct_ref,
    pull_hist_ref,
    grad_feat,
    swap_high,
    swap_low,
):
    grad_feat[:, 0:128] = direct_ref[...]
    grad_feat[:, 128:512] = jnp.zeros((direct_ref.shape[0], 384), F32)

    def backward(tiles):
        for place, (_, left, right) in enumerate(tiles):
            pair_swapped(
                col_ref, right, row_ref, left, left == right,
                swap_high.at[place], swap_low.at[place],
            )
        add_feature_pulls(
            tiles, range(len(tiles)), pull_message, weight_ref, grad_feat, swap_high, swap_low
        )

    own_tiles(control_ref, backward)
    pulled = pull_features(grad_feat, pre_ref)
    pull_hist_ref[...] = mm3(split(pulled), (fold_high[...], fold_low[...]), ROWROW)


def pair_pulls(tiles, pull_message, weight_ref, high_ref, low_ref, pull_ref):
    weighted = []
    for _, left, _ in tiles:
        cotangent = pull_message[block_rows(left), :]
        first = weighted_pull(cotangent, weight_ref, 2)
        second = weighted_pull(cotangent, weight_ref, 3)
        weighted.append(
            [jnp.concatenate([first[part], second[part]], axis=1) for part in range(2)]
        )
    found = [
        mm3(one, (high_ref[right], low_ref[right]), ROWROW)
        for one, (_, _, right) in zip(weighted, tiles)
    ]
    for one, (slot, _, _) in zip(found, tiles):
        pull_ref[slot] = one


def ghost_pair_kernel(control_ref, weight_ref, pull_message, ghost_high, ghost_low, pull_ref):
    ghost_tiles(
        control_ref,
        lambda tiles: pair_pulls(tiles, pull_message, weight_ref, ghost_high, ghost_low, pull_ref),
    )


def own_pair_kernel(
    control_ref, weight_ref, pull_message, share_ref, feat_high, feat_low, pull_ref, energy_ref
):
    energy_ref[...] = jnp.sum(share_ref[...].T, axis=0, keepdims=True)

    own_tiles(
        control_ref,
        lambda tiles: pair_pulls(tiles, pull_message, weight_ref, feat_high, feat_low, pull_ref),
    )


def add_position_pulls(
    tiles, total_ref, kind_ref, col_ref, row_ref, own, pull_in, pull_refs, grad_row, grad_col
):
    lane_basis = iota((1, 128), 1) // (4 * SPAN)
    built = []
    for _, left, right in tiles:
        parts = []
        for half in range(2):
            here = total_ref[block_rows(left), half * 128 : half * 128 + 128]
            parts += [jnp.where(lane_basis == n, here, 0.0) for n in range(4)]
        high, low = split(jnp.concatenate(parts, axis=0))
        table = kind_table(kind_ref, right)
        built.append(
            (jnp.concatenate([high, low], axis=1), jnp.concatenate([table, table], axis=1))
        )
    found = [mm(both, table, ROWROW) for both, table in built]
    for place, ((slot, _, _), one) in enumerate(zip(tiles, found)):
        pull_refs[place] = pull_in[slot] + one
    grads = [
        pair_backward(
            col_ref, left, row_ref, right, left == right if own else False, pull_refs.at[place]
        )
        for place, (_, left, right) in enumerate(tiles)
    ]
    for (_, left, right), (by_row, by_col) in zip(tiles, grads):
        grad_row[right] += by_row
        grad_col[block_rows(left), :] -= by_col


def third_ghost_kernel(
    control_ref,
    chosen_ref,
    pull_hist_ref,
    mate_in,
    far_in,
    zmate_in,
    zfar_in,
    col_ref,
    ghost_col,
    ghost_row,
    pull_in,
    out_ref,
    total_ref,
    grad_col,
    grad_ghost,
    pull_refs,
):
    even_x, even_y = parities(control_ref)
    returned = split(pick_all((even_x, even_y, mate_in, far_in, zmate_in, zfar_in)))
    chosen = chosen_ref[...]
    total_ref[...] = pull_hist_ref[...] + mm(chosen, returned[0]) + mm(chosen, returned[1])
    grad_ghost[...] = jnp.zeros_like(grad_ghost)
    grad_col[...] = jnp.zeros_like(grad_col)

    ghost_tiles(
        control_ref,
        lambda tiles: add_position_pulls(
            tiles, total_ref, ghost_col, col_ref, ghost_row, False, pull_in, pull_refs,
            grad_ghost, grad_col,
        ),
    )
    out_ref[...] = jnp.where(low_half(), grad_ghost[0], grad_ghost[1])


def third_own_kernel(
    control_ref,
    chosen_ref,
    total_ref,
    col_ref,
    row_ref,
    pull_in,
    grad_col_in,
    own_ref,
    turned_ref,
    grad_row,
    grad_col,
    pull_refs,
):
    blocks = total_ref.shape[0] // BLOCK
    turned_ref[...] = chosen_ref[...].astype(F32).T.astype(BF16)
    grad_row[...] = jnp.zeros_like(grad_row)
    grad_col[...] = grad_col_in[...]

    own_tiles(
        control_ref,
        lambda tiles: add_position_pulls(
            tiles, total_ref, col_ref, col_ref, row_ref, True, pull_in, pull_refs,
            grad_row, grad_col,
        ),
    )
    low = low_half()
    by_sender = jnp.concatenate(
        [jnp.where(low, grad_row[2 * k], grad_row[2 * k + 1]) for k in range(blocks // 2)], axis=1
    )
    own_ref[...] = by_sender + grad_col[...].T[0:8]


def last_kernel(control_ref, turned_ref, own_ref, mate_in, far_in, zmate_in, zfar_in, force_ref):
    even_x, even_y = parities(control_ref)
    returned = pick_rows(even_x, even_y, mate_in[...], far_in[...], zmate_in[...], zfar_in[...])
    total = own_ref[...] + exact_pick(returned, turned_ref[...])
    force_ref[...] = -total[0:3]


def partners(axis, far):
    count = lax.axis_size(axis)
    if far:
        return [(i, (i + (1 if i % 2 else -1)) % count) for i in range(count)]
    return [(i, i ^ 1) for i in range(count)]


def swap_both(axis, to_mate, to_far, far_first):
    def swap(value, far):
        return lax.ppermute(value, axis, partners(axis, far))

    if far_first:
        to_far, to_mate = lax.optimization_barrier((to_far, to_mate))
        far, mate = lax.optimization_barrier((swap(to_far, True), swap(to_mate, False)))
    else:
        to_mate, to_far = lax.optimization_barrier((to_mate, to_far))
        mate, far = lax.optimization_barrier((swap(to_mate, False), swap(to_far, True)))
    return mate, far


def exchange_rows(rows, beside):
    mate, far = swap_both("gx", rows, rows, True)
    far, mate, beside = lax.optimization_barrier((far, mate, beside))
    column = jnp.stack([rows, mate, far])
    zmate, zfar = swap_both("gy", column, column, False)
    return (mate, far, zmate, zfar), beside


def exchange_packets(even_y, to_mate, to_far, side, beside):
    mate, far = swap_both("gx", to_mate, to_far, True)
    far, mate, beside = lax.optimization_barrier((far, mate, beside))
    up = jnp.concatenate([mate[2:3], far[2:3], side[1:2]], axis=0)
    down = jnp.concatenate([mate[0:1], far[0:1], side[0:1]], axis=0)
    to_mate, to_far = jnp.where(even_y, up, down), jnp.where(even_y, down, up)
    zmate, zfar = swap_both("gy", to_mate, to_far, False)
    return (mate, far, zmate, zfar), beside


def struct(*shape, dtype=F32):
    return jax.ShapeDtypeStruct(shape, dtype)


def call(kernel, in_specs, outs, scratch=()):
    made = pl.pallas_call(
        kernel,
        in_specs=in_specs,
        out_specs=jax.tree.map(lambda _: VMEM, outs),
        out_shape=outs,
        scratch_shapes=list(scratch),
        compiler_params=PARAMS,
    )

    def run(*args):
        placed = [
            pltpu.with_memory_space_constraint(arg, pltpu.HBM if spec is HBM else pltpu.VMEM)
            for arg, spec in zip(args, in_specs, strict=True)
        ]
        return made(*placed)

    return run


def shards(fractions, species, send_list, tile_list, counts, embedding, radial, mixing, readout):
    atoms = fractions.shape[1]
    blocks = atoms // BLOCK
    kinds = embedding.shape[0]
    slots = tile_list.shape[1]
    parity = [lax.axis_index("gx") % 2, lax.axis_index("gy") % 2]
    even_y = parity[1] == 0
    words = jnp.stack([counts[0], *parity]).astype(jnp.int32)[None]
    far_arrays = (
        fractions,
        species[None],
        send_list,
        tile_list,
        embedding,
        radial.reshape(-1, radial.shape[2]),
        readout[None],
        mixing,
    )
    packets = [struct(3, 24, 128), struct(3, 24, 128), struct(2, 24, 128)]
    hist_struct = struct(atoms, HIST)
    col_struct = struct(atoms, 128)
    own_rows, ghost_rows = struct(blocks, 8, 128), struct(2, 8, 128)
    fold_halves = [struct(HIST, 640, dtype=BF16)] * 2
    mix_halves = [struct(2, 128, 128, dtype=BF16)] * 2
    own_halves = [struct(blocks, 256, 256, dtype=BF16)] * 2
    ghost_halves = [struct(2, 256, 256, dtype=BF16)] * 2
    pairs = [struct(slots, BASIS * BLOCK, 256, dtype=BF16)] * 2
    swaps = [struct(slots, 256, BASIS * BLOCK, dtype=BF16)] * 2
    pulls = struct(slots, BASIS * BLOCK, 256)

    site, rows, send, tiles = call(
        pack_kernel,
        [HBM] * 4,
        [
            struct(8, atoms), struct(8, 128),
            struct(*send_list.shape, dtype=jnp.int32), struct(8, 128, dtype=jnp.int32),
        ],
        [
            pltpu.VMEM(fractions.shape, F32),
            pltpu.VMEM((1, atoms), jnp.int32),
            pltpu.VMEM(tile_list.shape, jnp.int32),
            pltpu.SemaphoreType.DMA((4,)),
        ],
    )(*far_arrays[0:4])
    prepared = call(
        functools.partial(prepare_kernel, slots),
        [VMEM] * 4 + [HBM] * 4,
        [
            struct(8, 128, dtype=jnp.int32), col_struct, own_rows,
            struct(atoms, 128, dtype=BF16),
        ]
        + [struct(2 * SPAN + 4 * BASIS, 128), struct(*mixing.shape)],
        [pltpu.SemaphoreType.DMA((4,))],
    )(words, tiles, site, send, *far_arrays[4:])
    arrived, prepared = exchange_rows(rows, prepared)
    control, col, row, chosen, weights, mixers = prepared
    hist, own_high, own_low = call(
        own_histogram_kernel, [VMEM] * 3, [hist_struct] + pairs
    )(control, col, row)
    hist, to_mate, to_far, side, ghost_col, ghost_row, pair_high, pair_low = call(
        first_kernel,
        [VMEM] * 8,
        [hist_struct] + packets + [struct(8 * GHOSTS, 128), ghost_rows] + pairs,
        [
            pltpu.VMEM((8 * GHOSTS, HIST), F32),
            pltpu.SMEM(send_list.shape, jnp.int32),
            pltpu.SemaphoreType.DMA,
        ],
    )(control, send, hist, col, *arrived)
    features = call(
        functools.partial(feature_kernel, kinds),
        [VMEM] * 4,
        [struct(atoms, 640)] + own_halves + [col_struct] + fold_halves + mix_halves,
        [pltpu.VMEM((HIST, 640), F32)],
    )(hist, col, weights, mixers)
    arrived, features = exchange_packets(even_y, to_mate, to_far, side, features)
    pre, feat_high, feat_low, scalar, *folded = features
    fold, mix = folded[0:2], folded[2:4]
    message, swap_high, swap_low = call(message_kernel, [VMEM] * 8, [col_struct] + swaps)(
        control, row, ghost_col, weights, feat_high, feat_low, own_high, own_low
    )
    (
        to_mate, to_far, side, ghost_high, ghost_low, pull_message, direct, share,
    ) = call(
        functools.partial(second_ghost_kernel, kinds),
        [VMEM] * 17,
        packets + ghost_halves + [col_struct] * 3,
        [
            pltpu.VMEM((atoms, 128), F32),
            pltpu.VMEM((8 * GHOSTS, 640), F32),
            pltpu.VMEM((8 * GHOSTS, 512), F32),
            pltpu.VMEM((8 * GHOSTS, 256), F32),
        ],
    )(
        control, *arrived, ghost_col, *fold, *mix, weights, scalar, message,
        pair_high, pair_low, swap_high, swap_low,
    )
    pull = call(ghost_pair_kernel, [VMEM] * 5, pulls)(
        control, weights, pull_message, ghost_high, ghost_low
    )
    arrived, (pull, direct) = exchange_packets(even_y, to_mate, to_far, side, (pull, direct))
    pull_hist = call(
        own_pull_kernel,
        [VMEM] * 9,
        hist_struct,
        [pltpu.VMEM((atoms, 512), F32)] + [pltpu.VMEM((4, 256, BASIS * BLOCK), BF16)] * 2,
    )(control, col, row, *fold, weights, pre, pull_message, direct)
    rows, total, grad_col = call(
        third_ghost_kernel,
        [VMEM] * 11,
        [struct(8, 128), hist_struct, col_struct],
        [pltpu.VMEM((2, 8, 128), F32), pltpu.VMEM((4, BASIS * BLOCK, 256), F32)],
    )(control, chosen, pull_hist, *arrived, col, ghost_col, ghost_row, pull)
    share, rows = lax.optimization_barrier((share, rows))
    own_pair = call(own_pair_kernel, [VMEM] * 6, [pulls, struct(1, atoms)])(
        control, weights, pull_message, share, feat_high, feat_low
    )
    arrived, own_pair = exchange_rows(rows, own_pair)
    pull, energy = own_pair
    own, turned = call(
        third_own_kernel,
        [VMEM] * 7,
        [struct(8, atoms), struct(128, atoms, dtype=BF16)],
        [
            pltpu.VMEM((blocks, 8, 128), F32),
            pltpu.VMEM((atoms, 128), F32),
            pltpu.VMEM((4, BASIS * BLOCK, 256), F32),
        ],
    )(control, chosen, total, col, row, pull, grad_col)
    forces = call(last_kernel, [VMEM] * 7, struct(3, atoms))(control, turned, own, *arrived)
    return energy[0], forces


def solution(mesh):
    placed = (
        P(None, ("gx", "gy")),
        P(("gx", "gy")),
        P(None, ("gx", "gy")),
        P(None, ("gx", "gy")),
        P(("gx", "gy")),
        P(),
        P(),
        P(),
        P(),
    )
    return jax.shard_map(
        shards,
        mesh=mesh,
        in_specs=placed,
        out_specs=(P(("gx", "gy")), P(None, ("gx", "gy"))),
        check_vma=False,
    )
```

```python
import functools

import jax
import jax.numpy as jnp
from jax import lax
from jax.experimental import pallas as pl
from jax.experimental.pallas import tpu as pltpu
from jax.sharding import PartitionSpec as P

F32 = jnp.float32
BF16 = jnp.bfloat16

BASIS = 8
BLOCK = 64
GHOSTS = 16
SPAN = 8
HIST = BASIS * 4 * SPAN
OFFSETS = ((-1, -1), (-1, 0), (-1, 1), (0, -1), (0, 1), (1, -1), (1, 0), (1, 1))
WIDTHS = (12.0, 12.0, 36.0)
CUT_INV = 1.0 / 25.0
ROOT = 1.6986436005760381
STEP = ROOT * 0.6
MIDDLE = 1.0 + 0.6 * (BASIS - 1) / 2
REACH = 5.125
ROWS = 64

VMEM = pl.BlockSpec(memory_space=pltpu.VMEM)
HBM = pl.BlockSpec(memory_space=pltpu.HBM)
PARAMS = pltpu.CompilerParams(vmem_limit_bytes=16 * 1024 * 1024)

ROWROW = (((1,), (1,)), ((), ()))
ROWCOL = (((1,), (0,)), ((), ()))


def split(value):
    high = value.astype(BF16)
    return high, (value - high.astype(F32)).astype(BF16)


def mm(left, right, dims=ROWCOL):
    return lax.dot_general(left, right, dims, preferred_element_type=F32)


def mm3(left, right, dims=ROWCOL):
    (lh, ll), (rh, rl) = left, right
    summed = dims[0][1][0]
    return mm(
        jnp.concatenate([lh, ll, lh], axis=1), jnp.concatenate([rh, rh, rl], axis=summed), dims
    )


def sigmoid(value):
    return 1.0 / (1.0 + jnp.exp(-value))


def iota(shape, dim):
    return lax.broadcasted_iota(jnp.int32, shape, dim)


def low_half():
    return iota((1, 128), 1) < BLOCK


def pick_rows(even_x, even_y, mate, far, zmate, zfar):
    x_up, x_down = jnp.where(even_x, mate, far), jnp.where(even_x, far, mate)
    y_up = [jnp.where(even_y, zmate[i], zfar[i]) for i in range(3)]
    y_down = [jnp.where(even_y, zfar[i], zmate[i]) for i in range(3)]
    sources = {
        (1, 0): x_up,
        (-1, 0): x_down,
        (0, 1): y_up[0],
        (0, -1): y_down[0],
        (1, 1): jnp.where(even_x, y_up[1], y_up[2]),
        (-1, 1): jnp.where(even_x, y_up[2], y_up[1]),
        (1, -1): jnp.where(even_x, y_down[1], y_down[2]),
        (-1, -1): jnp.where(even_x, y_down[2], y_down[1]),
    }
    slot_of = iota((8, 128), 1) // GHOSTS
    total = jnp.zeros((8, 128), F32)
    for slot, offset in enumerate(OFFSETS):
        turned = pltpu.roll(sources[offset], ((2 * slot - 7) * GHOSTS) % 128, 1)
        total = jnp.where(slot_of == slot, turned, total)
    return total


def pick_slot(slot, even_x, even_y, mate, far, zmate, zfar):
    along_x, along_y = OFFSETS[slot]
    if along_y == 0:
        near = even_x if along_x == 1 else jnp.logical_not(even_x)
        return jnp.where(near, mate[1], far[1])
    near = even_y if along_y == 1 else jnp.logical_not(even_y)
    if along_x == 0:
        return jnp.where(near, zmate[2], zfar[2])
    first = even_x if along_x == 1 else jnp.logical_not(even_x)
    return jnp.where(
        near, jnp.where(first, zmate[0], zmate[1]), jnp.where(first, zfar[0], zfar[1])
    )


def pick_all(args):
    return jnp.concatenate([unpack(pick_slot(slot, *args)) for slot in range(8)], axis=0)


def pack(rows):
    free = iota((8, 128), 1) % SPAN >= 6
    carried = rows[8:16, 128:256]
    quarters = (rows[0:8, 0:128], rows[8:16, 0:128], rows[0:8, 128:256])
    return jnp.concatenate(
        [
            jnp.where(free, pltpu.roll(carried, 6 - 2 * part, 1), quarter)
            for part, quarter in enumerate(quarters)
        ],
        axis=0,
    )


def unpack(packet):
    place = iota((8, 128), 1) % SPAN
    turned = [
        pltpu.roll(packet[8 * part : 8 * part + 8], 128 - (6 - 2 * part), 1) for part in range(3)
    ]
    carried = jnp.where(place < 2, turned[0], jnp.where(place < 4, turned[1], turned[2]))
    return jnp.concatenate(
        [packet[0:16], jnp.concatenate([packet[16:24], carried], axis=0)], axis=1
    )


def put_packets(even_x, piece, mate_ref, far_ref, side_ref):
    for part in range(3):
        down, up = pack(piece(part)), pack(piece(5 + part))
        mate_ref[part] = jnp.where(even_x, up, down)
        far_ref[part] = jnp.where(even_x, down, up)
    side_ref[0] = pack(piece(3))
    side_ref[1] = pack(piece(4))


def send_columns(send):
    wide = jnp.concatenate([send] * 8, axis=1)
    own = iota((8, 128), 1) // GHOSTS == iota((8, 128), 0)
    return jnp.sum(jnp.where(own, wide, 0), axis=0, keepdims=True)


def chooser(send, atoms):
    return iota((atoms, 128), 0) == send_columns(send)


def block_rows(block, start=0, count=BLOCK):
    return pl.ds(pl.multiple_of(block * BLOCK, BLOCK) + start, count)


def separation(col_ref, col_block, row_ref, row_block, start, sign):
    mine = col_ref[block_rows(col_block, start, ROWS), :]
    other = row_ref[row_block]
    return [sign * (other[a : a + 1, :] - mine[:, a : a + 1]) for a in range(3)]


def envelope(parts, same, start):
    dist_sq = parts[0] * parts[0] + parts[1] * parts[1] + parts[2] * parts[2]
    soft = jnp.sqrt(dist_sq + 1.0)
    rows = iota((ROWS, 128), 0) + start
    columns = iota((ROWS, 128), 1) % BLOCK
    apart = jnp.where(jnp.logical_and(rows == columns, same), 0.0, 1.0)
    margin = jnp.maximum(1.0 - dist_sq * CUT_INV, 0.0) * apart
    return soft, margin


def angular(parts, inverse):
    u = [part * inverse for part in parts]
    low = low_half()
    return jnp.where(low, 1.0, u[0]), jnp.where(low, u[1], u[2])


def basis_scale(shape):
    step = (iota(shape, 0) % BASIS).astype(F32) - (BASIS - 1) / 2
    return jnp.exp2(-(STEP * STEP) * (step * step))


def centered(soft):
    return ROOT * (jnp.minimum(soft, REACH) - MIDDLE)


def pair_forward(col_ref, left, row_ref, right, same, high_ref, low_ref):
    for start in range(0, BLOCK, ROWS):
        parts = separation(col_ref, left, row_ref, right, start, 1.0)
        soft, margin = envelope(parts, same, start)
        first, second = angular(parts, 1.0 / soft)
        z = centered(soft)
        bell = jnp.exp2(-z * (z + (BASIS - 1) * STEP)) * (margin * margin)
        growth = jnp.exp2((2.0 * STEP) * z)
        for n in range(BASIS):
            here = pl.ds(n * BLOCK + start, ROWS)
            for half, factor in enumerate((first, second)):
                high, low = split(bell * factor)
                high_ref[here, half * 128 : half * 128 + 128] = high
                low_ref[here, half * 128 : half * 128 + 128] = low
            bell = bell * growth


def pair_swapped(col_ref, right, row_ref, left, same, high_ref, low_ref):
    low_lanes = low_half()
    for start in range(0, BLOCK, ROWS):
        parts = separation(col_ref, right, row_ref, left, start, -1.0)
        soft, margin = envelope(parts, same, start)
        inverse = 1.0 / soft
        u = [part * inverse for part in parts]
        z = centered(soft)
        bell = jnp.exp2(-z * (z + jnp.where(low_lanes, (BASIS - 1) * STEP, (BASIS - 3) * STEP)))
        bell = bell * (margin * margin)
        growth = jnp.exp2((4.0 * STEP) * z)
        for pair in range(BASIS // 2):
            for order in range(4):
                high, low = split(bell if order == 0 else bell * u[order - 1])
                here = pl.ds(order * BLOCK + start, ROWS)
                high_ref[here, pair * 128 : pair * 128 + 128] = high
                low_ref[here, pair * 128 : pair * 128 + 128] = low
            bell = bell * growth


def pair_backward(col_ref, left, row_ref, right, same, pull_ref):
    low_lanes = low_half()
    lane = iota((1, 128), 1)
    sums = [jnp.zeros((1, 128), F32) for _ in range(3)]
    columns = []
    for start in range(0, BLOCK, ROWS):
        parts = separation(col_ref, left, row_ref, right, start, 1.0)
        soft, margin = envelope(parts, same, start)
        inverse = 1.0 / soft
        first, second = angular(parts, inverse)
        z = centered(soft)
        bell = jnp.exp2(-z * (z - (BASIS - 1) * STEP))
        shrink = jnp.exp2((-2.0 * STEP) * z)
        by_first = jnp.zeros((ROWS, 128), F32)
        by_second = jnp.zeros((ROWS, 128), F32)
        count_first = jnp.zeros((ROWS, 128), F32)
        count_second = jnp.zeros((ROWS, 128), F32)
        for n in reversed(range(BASIS)):
            here = pl.ds(n * BLOCK + start, ROWS)
            by_first = by_first + bell * pull_ref[here, 0:128]
            by_second = by_second + bell * pull_ref[here, 128:256]
            if n > 0:
                count_first = count_first + by_first
                count_second = count_second + by_second
                bell = bell * shrink
        weight = margin * margin
        by_bell = first * by_first + second * by_second
        by_count = first * count_first + second * count_second
        by_bell = by_bell + pltpu.roll(by_bell, BLOCK, 1)
        by_count = by_count + pltpu.roll(by_count, BLOCK, 1)
        by_shift = (ROOT * (soft - 1.0) * by_bell - STEP * by_count) * weight
        by_first, by_second = by_first * weight, by_second * weight
        turned = pltpu.roll(by_second, BLOCK, 1)
        by_u = [
            jnp.where(low_lanes, pltpu.roll(by_first, BLOCK, 1), by_first),
            jnp.where(low_lanes, by_second, turned),
            jnp.where(low_lanes, turned, by_second),
        ]
        along = (by_u[0] * parts[0] + by_u[1] * parts[1] + by_u[2] * parts[2]) * inverse
        by_soft = by_shift * (-4.0 / ROOT) - along * inverse
        radial_part = by_soft * inverse + by_bell * (margin * (-4.0 * CUT_INV))
        column = jnp.zeros((ROWS, 128), F32)
        for a in range(3):
            force = by_u[a] * inverse + parts[a] * radial_part
            sums[a] = sums[a] + jnp.sum(force, axis=0, keepdims=True)
            total = jnp.sum(jnp.where(low_lanes, force, 0.0), axis=1, keepdims=True)
            column = jnp.where(lane == a, total, column)
        columns.append(column)
    return (
        jnp.concatenate(sums + [jnp.zeros((5, 128), F32)], axis=0),
        jnp.concatenate(columns, axis=0),
    )


def kind_table(col_ref, block):
    kind = col_ref[block_rows(block), 3:4].astype(jnp.int32)
    lane = iota((BLOCK, 128), 1)
    hit = kind == lane % SPAN
    return jnp.concatenate(
        [
            jnp.where(jnp.logical_and(hit, lane // SPAN % 4 == order), 1.0, 0.0)
            for order in range(4)
        ],
        axis=0,
    ).astype(BF16)


def parities(control_ref):
    return control_ref[1, 2] == 0, control_ref[2, 2] == 0


def fill_control(control_ref, words_ref, tiles_ref, slots, own_blocks):
    row, lane = iota((8, 128), 0), iota((8, 128), 1)
    live = words_ref[0, 0]
    table = jnp.where(lane < 2, tiles_ref[...], 0)
    lengths = [jnp.int32(0), jnp.int32(0)]
    for slot in range(2, slots):
        left, right = tiles_ref[slot, 0], tiles_ref[slot, 1]
        for which in range(2):
            ghost = which == 0
            sending = right - own_blocks if ghost else right
            member = (slot < live) & ((right >= own_blocks) if ghost else (right < own_blocks))
            first = 3 + 3 * which
            entry = jnp.where(lane == first, slot, jnp.where(lane == first + 1, left, sending))
            place = (lane >= first) & (lane < first + 3) & (row == lengths[which]) & member
            table = jnp.where(place, entry, table)
            lengths[which] = lengths[which] + member.astype(jnp.int32)
    for place, word in enumerate([live, words_ref[0, 1], words_ref[0, 2], *lengths]):
        table = jnp.where((lane == 2) & (row == place), word, table)
    control_ref[...] = table


def listed_tile(control_ref, which, place):
    first = 3 + 3 * which
    return tuple(control_ref[place, first + k] for k in range(3))


def single_tiles(control_ref, which, work, start):
    def step(place, carried):
        work([listed_tile(control_ref, which, place)])
        return carried

    lax.fori_loop(start, control_ref[3 + which, 2], step, 0)


def own_tiles(control_ref, work):
    count = control_ref[4, 2]

    def group(place, size):
        work([listed_tile(control_ref, 1, place + k) for k in range(size)])

    def step(quarter, carried):
        group(4 * quarter, 4)
        return carried

    lax.fori_loop(0, count // 4, step, 0)
    rest = count % 4

    @pl.when(rest >= 2)
    def _():
        group(count - rest, 2)

    @pl.when(rest % 2 == 1)
    def _():
        group(count - 1, 1)


def ghost_tiles(control_ref, work):
    more = control_ref[3, 2]

    def fixed():
        return [(slot, control_ref[slot, 0], slot) for slot in range(2)]

    @pl.when(more == 0)
    def _():
        work(fixed())

    @pl.when(more > 0)
    def _():
        @pl.when(more == 1)
        def _():
            work(fixed() + [listed_tile(control_ref, 0, 0)])

        @pl.when(more > 1)
        def _():
            work(fixed() + [listed_tile(control_ref, 0, place) for place in range(2)])
            single_tiles(control_ref, 0, work, 2)


def exact_pick(rows, chosen):
    high = rows.astype(BF16).astype(F32)
    rest = rows - high
    middle = rest.astype(BF16).astype(F32)
    stacked = jnp.concatenate(
        [high, middle, rest - middle, jnp.zeros_like(rows)], axis=0
    ).astype(BF16)
    picked = mm(stacked, chosen)
    return picked[0:8] + picked[8:16] + picked[16:24]


def fetch(pairs, sems):
    copies = [
        pltpu.make_async_copy(source, target, sems.at[i]) for i, (source, target) in enumerate(pairs)
    ]
    for copy in copies:
        copy.start()
    return copies


def pack_kernel(
    frac_in,
    kind_in,
    send_in,
    tile_in,
    site_ref,
    out_ref,
    send_ref,
    tiles_ref,
    frac_ref,
    kind_ref,
    tile_ref,
    sems,
):
    copies = fetch(
        (
            (frac_in, frac_ref),
            (kind_in, kind_ref),
            (send_in, send_ref),
            (tile_in, tile_ref),
        ),
        sems,
    )
    for copy in copies:
        copy.wait()
    atoms = frac_ref.shape[1]
    rows = jnp.concatenate(
        [frac_ref[...], kind_ref[...].astype(F32), jnp.zeros((4, atoms), F32)], axis=0
    )
    site_ref[...] = rows
    out_ref[...] = exact_pick(rows, chooser(send_ref[...], atoms).astype(F32).astype(BF16))
    slots = tile_ref.shape[1]
    lines = jnp.concatenate([tile_ref[...].astype(F32), jnp.zeros((2, 128 - slots), F32)], axis=1)
    lines = jnp.concatenate([lines, jnp.zeros((126, 128), F32)], axis=0)
    tiles_ref[...] = lines.T[0:8].astype(jnp.int32)


def doubled(rows, block):
    chunk = rows[:, block // 2 * 128 : block // 2 * 128 + 128]
    turned = pltpu.roll(chunk, BLOCK, 1)
    low = low_half()
    return jnp.where(low, chunk, turned) if block % 2 == 0 else jnp.where(low, turned, chunk)


def upright(rows):
    return jnp.concatenate([rows, jnp.zeros((120, rows.shape[1]), F32)], axis=0).T


def radial_row(weight_ref, path, n):
    row = SPAN + path * BASIS + n
    return weight_ref[row : row + 1, :]


def readout_row(weight_ref):
    row = SPAN + 4 * BASIS
    return weight_ref[row : row + 1, :]


def axis_scale():
    row = iota((8, 128), 0)
    return jnp.where(row < 2, WIDTHS[0], jnp.where(row == 2, WIDTHS[2], 1.0))


def add_histograms(tiles, col_ref, row_ref, own, kind_ref, hist_ref, pair_high, pair_low):
    for slot, left, right in tiles:
        same = left == right if own else False
        pair_forward(col_ref, left, row_ref, right, same, pair_high.at[slot], pair_low.at[slot])
    tables = [kind_table(kind_ref, right) for _, _, right in tiles]
    found = [
        mm(pair_high[slot], table) + mm(pair_low[slot], table)
        for (slot, _, _), table in zip(tiles, tables)
    ]
    lane_basis = iota((1, 128), 1) // (4 * SPAN)
    for (_, left, _), one in zip(tiles, found):
        for half in range(2):
            total = jnp.zeros((BLOCK, 128), F32)
            for n in range(4):
                begin = (half * 4 + n) * BLOCK
                total = jnp.where(lane_basis == n, one[begin : begin + BLOCK], total)
            hist_ref[block_rows(left), half * 128 : half * 128 + 128] += total


def own_histogram_kernel(
    control_ref, col_ref, row_ref, hist_ref, pair_high, pair_low
):
    hist_ref[...] = jnp.zeros_like(hist_ref)
    own_tiles(
        control_ref,
        lambda tiles: add_histograms(
            tiles, col_ref, row_ref, True, col_ref, hist_ref, pair_high, pair_low
        ),
    )


def prepare_kernel(
    slots,
    words_ref,
    tiles_ref,
    site_ref,
    send_ref,
    embed_in,
    radial_in,
    readout_in,
    mixing_in,
    control_ref,
    col_ref,
    row_ref,
    chosen_ref,
    weight_ref,
    mixing_ref,
    sems,
):
    kinds = embed_in.shape[0]
    paths = radial_in.shape[0]
    copies = fetch(
        (
            (embed_in, weight_ref.at[pl.ds(0, kinds)]),
            (radial_in, weight_ref.at[pl.ds(SPAN, paths)]),
            (readout_in, weight_ref.at[pl.ds(SPAN + paths, 1)]),
            (mixing_in, mixing_ref),
        ),
        sems,
    )
    atoms = site_ref.shape[1]
    blocks = atoms // BLOCK
    fill_control(control_ref, words_ref, tiles_ref, slots, blocks)
    own = site_ref[...] * axis_scale()[:, 0:1]
    col_ref[...] = upright(own)
    for block in range(blocks):
        row_ref[block] = doubled(own, block)
    chosen_ref[...] = chooser(send_ref[...], atoms).astype(F32).astype(BF16)
    for copy in copies:
        copy.wait()
    radial = weight_ref[SPAN : SPAN + paths, :]
    weight_ref[SPAN : SPAN + paths, :] = radial * basis_scale(radial.shape)


def first_kernel(
    control_ref,
    send_in,
    hist_in,
    col_ref,
    mate_in,
    far_in,
    zmate_in,
    zfar_in,
    hist_ref,
    mate_ref,
    far_ref,
    side_ref,
    ghost_col,
    ghost_row,
    pair_high,
    pair_low,
    gather_ref,
    send_ref,
    sem,
):
    fetching = pltpu.make_async_copy(send_in, send_ref, sem)
    fetching.start()
    even_x, even_y = parities(control_ref)
    ghosts = pick_rows(even_x, even_y, mate_in[...], far_in[...], zmate_in[...], zfar_in[...])
    row = iota((8, 128), 0)
    slot = iota((8, 128), 1) // GHOSTS
    shift_x = jnp.where(slot < 3, -1.0, jnp.where(slot < 5, 0.0, 1.0))
    down = (slot == 0) | (slot == 3) | (slot == 5)
    level = (slot == 1) | (slot == 6)
    shift_y = jnp.where(down, -1.0, jnp.where(level, 0.0, 1.0))
    shift = jnp.where(row == 0, shift_x, jnp.where(row == 1, shift_y, 0.0))
    ghosts = (ghosts + shift) * axis_scale()
    ghost_col[...] = upright(ghosts)
    for block in range(2):
        ghost_row[block] = doubled(ghosts, block)
    hist_ref[...] = hist_in[...]

    ghost_tiles(
        control_ref,
        lambda tiles: add_histograms(
            tiles, col_ref, ghost_row, False, ghost_col, hist_ref, pair_high, pair_low
        ),
    )
    fetching.wait()

    up, down = jnp.where(even_x, 5, 0), jnp.where(even_x, 0, 5)
    places = [(mate_ref, part, up + part) for part in range(3)]
    places += [(far_ref, part, down + part) for part in range(3)]
    places += [(side_ref, part, 3 + part) for part in range(2)]
    for place, (_, _, slot) in enumerate(places):
        for entry in range(GHOSTS):
            row = place * GHOSTS + entry
            gather_ref[row : row + 1, :] = hist_ref[pl.ds(send_ref[slot, entry], 1), :]
    for place, (ref, part, _) in enumerate(places):
        ref[part] = pack(gather_ref[place * GHOSTS : place * GHOSTS + GHOSTS, :])


def make_features(block, col_ref, kinds, weight_ref, pre_ref, feat_high, feat_low, scalar_ref):
    rows = block_rows(block)
    kind = col_ref[rows, 3:4].astype(jnp.int32)
    scalar = jnp.zeros((BLOCK, 128), F32)
    for species in range(kinds):
        scalar = jnp.where(kind == species, weight_ref[species : species + 1, :], scalar)
    pre = pre_ref[rows, 0:128]
    scalar = scalar + pre * sigmoid(pre)
    if scalar_ref is not None:
        scalar_ref[rows, :] = scalar
    gate = sigmoid(pre_ref[rows, 128:256])
    parts = [scalar] + [pre_ref[rows, (a + 2) * 128 : (a + 3) * 128] * gate for a in range(3)]
    empty = jnp.zeros((BLOCK, 128), BF16)
    for order, part in enumerate(parts):
        high, low = split(part)
        here = pl.ds(order * BLOCK, BLOCK)
        used = 0 if order == 0 else 128
        for ref, value in ((feat_high, high), (feat_low, low)):
            ref[block, here, used : used + 128] = value
            ref[block, here, 128 - used : 256 - used] = empty


def add_messages(tiles, feat_high, feat_low, weight_ref, message_ref, pair_high, pair_low):
    found = [
        mm3((pair_high[slot], pair_low[slot]), (feat_high[right], feat_low[right]))
        for slot, _, right in tiles
    ]
    for (_, left, _), one in zip(tiles, found):
        total = jnp.zeros((BLOCK, 128), F32)
        for n in range(BASIS):
            rows = slice(n * BLOCK, n * BLOCK + BLOCK)
            total = total + one[rows, 0:128] * radial_row(weight_ref, 2, n)
            total = total + one[rows, 128:256] * radial_row(weight_ref, 3, n)
        message_ref[block_rows(left), :] += total


def feature_kernel(
    kinds,
    hist_ref,
    col_ref,
    weight_ref,
    mixing_ref,
    pre_ref,
    feat_high,
    feat_low,
    scalar_ref,
    fold_high,
    fold_low,
    mix_high,
    mix_low,
    fold_ref,
):
    embed = jnp.where(iota((SPAN, 128), 0) < kinds, weight_ref[0:SPAN, :], 0.0)
    scalar = jnp.concatenate([radial_row(weight_ref, 0, n) * embed for n in range(BASIS)], axis=0)
    vector = jnp.concatenate([radial_row(weight_ref, 1, n) * embed for n in range(BASIS)], axis=0)
    scalar, vector = split(scalar), split(vector)
    to_self = mm3(scalar, split(mixing_ref[0]))
    to_gate = mm3(scalar, split(mixing_ref[2]))
    to_vector = mm3(vector, split(mixing_ref[1]))
    fold_ref[...] = jnp.zeros_like(fold_ref)
    for n in range(BASIS):
        rows = slice(n * SPAN, n * SPAN + SPAN)
        base = n * 4 * SPAN
        fold_ref[base : base + SPAN, 0:128] = to_self[rows]
        fold_ref[base : base + SPAN, 128:256] = to_gate[rows]
        for a in range(3):
            here = base + (a + 1) * SPAN
            fold_ref[here : here + SPAN, (a + 2) * 128 : (a + 3) * 128] = to_vector[rows]
    fold_high[...], fold_low[...] = split(fold_ref[...])
    for part in range(2):
        mix_high[part], mix_low[part] = split(mixing_ref[3 + part])
    blocks = hist_ref.shape[0] // BLOCK
    pre_ref[...] = mm3(split(hist_ref[...]), (fold_high[...], fold_low[...]))

    def features(block, carried):
        make_features(block, col_ref, kinds, weight_ref, pre_ref, feat_high, feat_low, scalar_ref)
        return carried

    lax.fori_loop(0, blocks, features, 0)


def message_kernel(
    control_ref,
    row_ref,
    ghost_col,
    weight_ref,
    feat_high,
    feat_low,
    pair_high,
    pair_low,
    message_ref,
    swap_high,
    swap_low,
):
    blocks = feat_high.shape[0]
    message_ref[...] = jnp.zeros_like(message_ref)

    own_tiles(
        control_ref,
        lambda tiles: add_messages(
            tiles, feat_high, feat_low, weight_ref, message_ref, pair_high, pair_low
        ),
    )

    def swapped(tiles):
        for slot, left, right in tiles:
            pair_swapped(
                ghost_col, right, row_ref, left, False, swap_high.at[slot], swap_low.at[slot]
            )

    for slot in range(2):
        swapped([(slot, control_ref[slot, 0], slot)])
    single_tiles(control_ref, 0, swapped, 0)


def weighted_pull(cotangent, weight_ref, path):
    return split(
        jnp.concatenate([cotangent * radial_row(weight_ref, path, n) for n in range(BASIS)], axis=0)
    )


def add_feature_pulls(tiles, places, pull_message, weight_ref, grad_feat, swap_high, swap_low):
    weighted = []
    for _, left, _ in tiles:
        cotangent = pull_message[block_rows(left), :]
        weighted.append([weighted_pull(cotangent, weight_ref, path) for path in (2, 3)])
    found = []
    for place, (by_scalar, by_vector) in zip(places, weighted):
        high, low = swap_high.at[place], swap_low.at[place]
        to_scalar = mm3((high[0:BLOCK, :], low[0:BLOCK, :]), by_scalar)
        to_vector = mm3((high[BLOCK:, :], low[BLOCK:, :]), by_vector)
        found.append((to_scalar, to_vector))
    for (_, _, right), (to_scalar, to_vector) in zip(tiles, found):
        rows = block_rows(right)
        grad_feat[rows, 0:128] += to_scalar
        for a in range(3):
            here = slice(a * BLOCK, (a + 1) * BLOCK)
            grad_feat[rows, (a + 1) * 128 : (a + 2) * 128] += to_vector[here]


def finish(message, scalar, mix_high, mix_low, weight_ref):
    mix_message, mix_hidden = (mix_high[0], mix_low[0]), (mix_high[1], mix_low[1])
    readout = readout_row(weight_ref)
    mixed = mm3(split(message), mix_message)
    mixed_gate = sigmoid(mixed)
    final = scalar + mixed * mixed_gate
    hidden = mm3(split(final), mix_hidden)
    hidden_gate = sigmoid(hidden)
    pull_hidden = readout * (hidden_gate * (1.0 + hidden * (1.0 - hidden_gate)))
    pull_final = mm3(split(pull_hidden), mix_hidden, ROWROW)
    pull_mixed = pull_final * (mixed_gate * (1.0 + mixed * (1.0 - mixed_gate)))
    pull_message = mm3(split(pull_mixed), mix_message, ROWROW)
    return hidden * hidden_gate * readout, pull_final, pull_message


def pull_features(grad_feat, pre_ref):
    by_scalar = grad_feat[:, 0:128]
    pre = pre_ref[:, 0:128]
    own_gate = sigmoid(pre)
    gate = sigmoid(pre_ref[:, 128:256])
    by_gate = jnp.zeros_like(gate)
    by_vector = []
    for a in range(3):
        pulled = grad_feat[:, (a + 1) * 128 : (a + 2) * 128]
        by_gate = by_gate + pulled * pre_ref[:, (a + 2) * 128 : (a + 3) * 128]
        by_vector.append(pulled * gate)
    by_pre = by_scalar * (own_gate * (1.0 + pre * (1.0 - own_gate)))
    return jnp.concatenate([by_pre, by_gate * gate * (1.0 - gate)] + by_vector, axis=1)


def second_ghost_kernel(
    kinds,
    control_ref,
    mate_in,
    far_in,
    zmate_in,
    zfar_in,
    ghost_col,
    fold_high,
    fold_low,
    mix_high,
    mix_low,
    weight_ref,
    scalar_ref,
    message_in,
    pair_high,
    pair_low,
    swap_high,
    swap_low,
    mate_ref,
    far_ref,
    side_ref,
    feat_high,
    feat_low,
    pull_message,
    direct_ref,
    share_ref,
    message_ref,
    pre_ref,
    grad_feat,
):
    even_x, even_y = parities(control_ref)
    fold = (fold_high[...], fold_low[...])
    ghost_hist = pick_all((even_x, even_y, mate_in, far_in, zmate_in, zfar_in))
    pre_ref[...] = mm3(split(ghost_hist), fold)
    for block in range(2):
        make_features(block, ghost_col, kinds, weight_ref, pre_ref, feat_high, feat_low, None)
    message_ref[...] = message_in[...]

    ghost_tiles(
        control_ref,
        lambda tiles: add_messages(
            tiles, feat_high, feat_low, weight_ref, message_ref, pair_high, pair_low
        ),
    )

    share_ref[...], direct_ref[...], pull_message[...] = finish(
        message_ref[...], scalar_ref[...], mix_high, mix_low, weight_ref
    )
    grad_feat[...] = jnp.zeros_like(grad_feat)

    ghost_tiles(
        control_ref,
        lambda tiles: add_feature_pulls(
            tiles, [slot for slot, _, _ in tiles], pull_message, weight_ref, grad_feat,
            swap_high, swap_low,
        ),
    )

    ghost_pull = mm3(split(pull_features(grad_feat, pre_ref)), fold, ROWROW)
    put_packets(
        even_x,
        lambda slot: ghost_pull[slot * GHOSTS : slot * GHOSTS + GHOSTS],
        mate_ref,
        far_ref,
        side_ref,
    )


def own_pull_kernel(
    control_ref,
    col_ref,
    row_ref,
    fold_high,
    fold_low,
    weight_ref,
    pre_ref,
    pull_message,
    direct_ref,
    pull_hist_ref,
    grad_feat,
    swap_high,
    swap_low,
):
    grad_feat[:, 0:128] = direct_ref[...]
    grad_feat[:, 128:512] = jnp.zeros((direct_ref.shape[0], 384), F32)

    def backward(tiles):
        for place, (_, left, right) in enumerate(tiles):
            pair_swapped(
                col_ref, right, row_ref, left, left == right,
                swap_high.at[place], swap_low.at[place],
            )
        add_feature_pulls(
            tiles, range(len(tiles)), pull_message, weight_ref, grad_feat, swap_high, swap_low
        )

    own_tiles(control_ref, backward)
    pulled = pull_features(grad_feat, pre_ref)
    pull_hist_ref[...] = mm3(split(pulled), (fold_high[...], fold_low[...]), ROWROW)


def pair_pulls(tiles, pull_message, weight_ref, high_ref, low_ref, pull_ref):
    weighted = []
    for _, left, _ in tiles:
        cotangent = pull_message[block_rows(left), :]
        first = weighted_pull(cotangent, weight_ref, 2)
        second = weighted_pull(cotangent, weight_ref, 3)
        weighted.append(
            [jnp.concatenate([first[part], second[part]], axis=1) for part in range(2)]
        )
    found = [
        mm3(one, (high_ref[right], low_ref[right]), ROWROW)
        for one, (_, _, right) in zip(weighted, tiles)
    ]
    for one, (slot, _, _) in zip(found, tiles):
        pull_ref[slot] = one


def ghost_pair_kernel(control_ref, weight_ref, pull_message, ghost_high, ghost_low, pull_ref):
    ghost_tiles(
        control_ref,
        lambda tiles: pair_pulls(tiles, pull_message, weight_ref, ghost_high, ghost_low, pull_ref),
    )


def own_pair_kernel(
    control_ref, weight_ref, pull_message, share_ref, feat_high, feat_low, pull_ref, energy_ref
):
    energy_ref[...] = jnp.sum(share_ref[...].T, axis=0, keepdims=True)

    own_tiles(
        control_ref,
        lambda tiles: pair_pulls(tiles, pull_message, weight_ref, feat_high, feat_low, pull_ref),
    )


def add_position_pulls(
    tiles, total_ref, kind_ref, col_ref, row_ref, own, pull_in, pull_refs, grad_row, grad_col
):
    lane_basis = iota((1, 128), 1) // (4 * SPAN)
    built = []
    for _, left, right in tiles:
        parts = []
        for half in range(2):
            here = total_ref[block_rows(left), half * 128 : half * 128 + 128]
            parts += [jnp.where(lane_basis == n, here, 0.0) for n in range(4)]
        high, low = split(jnp.concatenate(parts, axis=0))
        table = kind_table(kind_ref, right)
        built.append(
            (jnp.concatenate([high, low], axis=1), jnp.concatenate([table, table], axis=1))
        )
    found = [mm(both, table, ROWROW) for both, table in built]
    for place, ((slot, _, _), one) in enumerate(zip(tiles, found)):
        pull_refs[place] = pull_in[slot] + one
    grads = [
        pair_backward(
            col_ref, left, row_ref, right, left == right if own else False, pull_refs.at[place]
        )
        for place, (_, left, right) in enumerate(tiles)
    ]
    for (_, left, right), (by_row, by_col) in zip(tiles, grads):
        grad_row[right] += by_row
        grad_col[block_rows(left), :] -= by_col


def third_ghost_kernel(
    control_ref,
    chosen_ref,
    pull_hist_ref,
    mate_in,
    far_in,
    zmate_in,
    zfar_in,
    col_ref,
    ghost_col,
    ghost_row,
    pull_in,
    out_ref,
    total_ref,
    grad_col,
    grad_ghost,
    pull_refs,
):
    even_x, even_y = parities(control_ref)
    returned = split(pick_all((even_x, even_y, mate_in, far_in, zmate_in, zfar_in)))
    chosen = chosen_ref[...]
    total_ref[...] = pull_hist_ref[...] + mm(chosen, returned[0]) + mm(chosen, returned[1])
    grad_ghost[...] = jnp.zeros_like(grad_ghost)
    grad_col[...] = jnp.zeros_like(grad_col)

    ghost_tiles(
        control_ref,
        lambda tiles: add_position_pulls(
            tiles, total_ref, ghost_col, col_ref, ghost_row, False, pull_in, pull_refs,
            grad_ghost, grad_col,
        ),
    )
    out_ref[...] = jnp.where(low_half(), grad_ghost[0], grad_ghost[1])


def third_own_kernel(
    control_ref,
    chosen_ref,
    total_ref,
    col_ref,
    row_ref,
    pull_in,
    grad_col_in,
    own_ref,
    turned_ref,
    grad_row,
    grad_col,
    pull_refs,
):
    blocks = total_ref.shape[0] // BLOCK
    turned_ref[...] = chosen_ref[...].astype(F32).T.astype(BF16)
    grad_row[...] = jnp.zeros_like(grad_row)
    grad_col[...] = grad_col_in[...]

    own_tiles(
        control_ref,
        lambda tiles: add_position_pulls(
            tiles, total_ref, col_ref, col_ref, row_ref, True, pull_in, pull_refs,
            grad_row, grad_col,
        ),
    )
    low = low_half()
    by_sender = jnp.concatenate(
        [jnp.where(low, grad_row[2 * k], grad_row[2 * k + 1]) for k in range(blocks // 2)], axis=1
    )
    own_ref[...] = by_sender + grad_col[...].T[0:8]


def last_kernel(control_ref, turned_ref, own_ref, mate_in, far_in, zmate_in, zfar_in, force_ref):
    even_x, even_y = parities(control_ref)
    returned = pick_rows(even_x, even_y, mate_in[...], far_in[...], zmate_in[...], zfar_in[...])
    total = own_ref[...] + exact_pick(returned, turned_ref[...])
    force_ref[...] = -total[0:3]


def partners(axis, far):
    count = lax.axis_size(axis)
    if far:
        return [(i, (i + (1 if i % 2 else -1)) % count) for i in range(count)]
    return [(i, i ^ 1) for i in range(count)]


def swap_both(axis, to_mate, to_far, far_first):
    def swap(value, far):
        return lax.ppermute(value, axis, partners(axis, far))

    if far_first:
        to_far, to_mate = lax.optimization_barrier((to_far, to_mate))
        far, mate = lax.optimization_barrier((swap(to_far, True), swap(to_mate, False)))
    else:
        to_mate, to_far = lax.optimization_barrier((to_mate, to_far))
        mate, far = lax.optimization_barrier((swap(to_mate, False), swap(to_far, True)))
    return mate, far


def exchange_rows(rows, beside):
    mate, far = swap_both("gx", rows, rows, True)
    far, mate, beside = lax.optimization_barrier((far, mate, beside))
    column = jnp.stack([rows, mate, far])
    zmate, zfar = swap_both("gy", column, column, False)
    return (mate, far, zmate, zfar), beside


def exchange_packets(even_y, to_mate, to_far, side, beside):
    mate, far = swap_both("gx", to_mate, to_far, True)
    far, mate, beside = lax.optimization_barrier((far, mate, beside))
    up = jnp.concatenate([mate[2:3], far[2:3], side[1:2]], axis=0)
    down = jnp.concatenate([mate[0:1], far[0:1], side[0:1]], axis=0)
    to_mate, to_far = jnp.where(even_y, up, down), jnp.where(even_y, down, up)
    zmate, zfar = swap_both("gy", to_mate, to_far, False)
    return (mate, far, zmate, zfar), beside


def struct(*shape, dtype=F32):
    return jax.ShapeDtypeStruct(shape, dtype)


def call(kernel, in_specs, outs, scratch=()):
    made = pl.pallas_call(
        kernel,
        in_specs=in_specs,
        out_specs=jax.tree.map(lambda _: VMEM, outs),
        out_shape=outs,
        scratch_shapes=list(scratch),
        compiler_params=PARAMS,
    )

    def run(*args):
        placed = [
            pltpu.with_memory_space_constraint(arg, pltpu.HBM if spec is HBM else pltpu.VMEM)
            for arg, spec in zip(args, in_specs, strict=True)
        ]
        return made(*placed)

    return run


def shards(fractions, species, send_list, tile_list, counts, embedding, radial, mixing, readout):
    atoms = fractions.shape[1]
    blocks = atoms // BLOCK
    kinds = embedding.shape[0]
    slots = tile_list.shape[1]
    parity = [lax.axis_index("gx") % 2, lax.axis_index("gy") % 2]
    even_y = parity[1] == 0
    words = jnp.stack([counts[0], *parity]).astype(jnp.int32)[None]
    far_arrays = (
        fractions,
        species[None],
        send_list,
        tile_list,
        embedding,
        radial.reshape(-1, radial.shape[2]),
        readout[None],
        mixing,
    )
    packets = [struct(3, 24, 128), struct(3, 24, 128), struct(2, 24, 128)]
    hist_struct = struct(atoms, HIST)
    col_struct = struct(atoms, 128)
    own_rows, ghost_rows = struct(blocks, 8, 128), struct(2, 8, 128)
    fold_halves = [struct(HIST, 640, dtype=BF16)] * 2
    mix_halves = [struct(2, 128, 128, dtype=BF16)] * 2
    own_halves = [struct(blocks, 256, 256, dtype=BF16)] * 2
    ghost_halves = [struct(2, 256, 256, dtype=BF16)] * 2
    pairs = [struct(slots, BASIS * BLOCK, 256, dtype=BF16)] * 2
    swaps = [struct(slots, 256, BASIS * BLOCK, dtype=BF16)] * 2
    pulls = struct(slots, BASIS * BLOCK, 256)

    site, rows, send, tiles = call(
        pack_kernel,
        [HBM] * 4,
        [
            struct(8, atoms), struct(8, 128),
            struct(*send_list.shape, dtype=jnp.int32), struct(8, 128, dtype=jnp.int32),
        ],
        [
            pltpu.VMEM(fractions.shape, F32),
            pltpu.VMEM((1, atoms), jnp.int32),
            pltpu.VMEM(tile_list.shape, jnp.int32),
            pltpu.SemaphoreType.DMA((4,)),
        ],
    )(*far_arrays[0:4])
    prepared = call(
        functools.partial(prepare_kernel, slots),
        [VMEM] * 4 + [HBM] * 4,
        [
            struct(8, 128, dtype=jnp.int32), col_struct, own_rows,
            struct(atoms, 128, dtype=BF16),
        ]
        + [struct(2 * SPAN + 4 * BASIS, 128), struct(*mixing.shape)],
        [pltpu.SemaphoreType.DMA((4,))],
    )(words, tiles, site, send, *far_arrays[4:])
    arrived, prepared = exchange_rows(rows, prepared)
    control, col, row, chosen, weights, mixers = prepared
    hist, own_high, own_low = call(
        own_histogram_kernel, [VMEM] * 3, [hist_struct] + pairs
    )(control, col, row)
    hist, to_mate, to_far, side, ghost_col, ghost_row, pair_high, pair_low = call(
        first_kernel,
        [VMEM] * 8,
        [hist_struct] + packets + [struct(8 * GHOSTS, 128), ghost_rows] + pairs,
        [
            pltpu.VMEM((8 * GHOSTS, HIST), F32),
            pltpu.SMEM(send_list.shape, jnp.int32),
            pltpu.SemaphoreType.DMA,
        ],
    )(control, send, hist, col, *arrived)
    features = call(
        functools.partial(feature_kernel, kinds),
        [VMEM] * 4,
        [struct(atoms, 640)] + own_halves + [col_struct] + fold_halves + mix_halves,
        [pltpu.VMEM((HIST, 640), F32)],
    )(hist, col, weights, mixers)
    arrived, features = exchange_packets(even_y, to_mate, to_far, side, features)
    pre, feat_high, feat_low, scalar, *folded = features
    fold, mix = folded[0:2], folded[2:4]
    message, swap_high, swap_low = call(message_kernel, [VMEM] * 8, [col_struct] + swaps)(
        control, row, ghost_col, weights, feat_high, feat_low, own_high, own_low
    )
    (
        to_mate, to_far, side, ghost_high, ghost_low, pull_message, direct, share,
    ) = call(
        functools.partial(second_ghost_kernel, kinds),
        [VMEM] * 17,
        packets + ghost_halves + [col_struct] * 3,
        [
            pltpu.VMEM((atoms, 128), F32),
            pltpu.VMEM((8 * GHOSTS, 640), F32),
            pltpu.VMEM((8 * GHOSTS, 512), F32),
        ],
    )(
        control, *arrived, ghost_col, *fold, *mix, weights, scalar, message,
        pair_high, pair_low, swap_high, swap_low,
    )
    pull = call(ghost_pair_kernel, [VMEM] * 5, pulls)(
        control, weights, pull_message, ghost_high, ghost_low
    )
    arrived, (pull, direct) = exchange_packets(even_y, to_mate, to_far, side, (pull, direct))
    pull_hist = call(
        own_pull_kernel,
        [VMEM] * 9,
        hist_struct,
        [pltpu.VMEM((atoms, 512), F32)] + [pltpu.VMEM((4, 256, BASIS * BLOCK), BF16)] * 2,
    )(control, col, row, *fold, weights, pre, pull_message, direct)
    rows, total, grad_col = call(
        third_ghost_kernel,
        [VMEM] * 11,
        [struct(8, 128), hist_struct, col_struct],
        [pltpu.VMEM((2, 8, 128), F32), pltpu.VMEM((4, BASIS * BLOCK, 256), F32)],
    )(control, chosen, pull_hist, *arrived, col, ghost_col, ghost_row, pull)
    share, rows = lax.optimization_barrier((share, rows))
    own_pair = call(own_pair_kernel, [VMEM] * 6, [pulls, struct(1, atoms)])(
        control, weights, pull_message, share, feat_high, feat_low
    )
    arrived, own_pair = exchange_rows(rows, own_pair)
    pull, energy = own_pair
    own, turned = call(
        third_own_kernel,
        [VMEM] * 7,
        [struct(8, atoms), struct(128, atoms, dtype=BF16)],
        [
            pltpu.VMEM((blocks, 8, 128), F32),
            pltpu.VMEM((atoms, 128), F32),
            pltpu.VMEM((4, BASIS * BLOCK, 256), F32),
        ],
    )(control, chosen, total, col, row, pull, grad_col)
    forces = call(last_kernel, [VMEM] * 7, struct(3, atoms))(control, turned, own, *arrived)
    return energy[0], forces


def solution(mesh):
    placed = (
        P(None, ("gx", "gy")),
        P(("gx", "gy")),
        P(None, ("gx", "gy")),
        P(None, ("gx", "gy")),
        P(("gx", "gy")),
        P(),
        P(),
        P(),
        P(),
    )
    return jax.shard_map(
        shards,
        mesh=mesh,
        in_specs=placed,
        out_specs=(P(("gx", "gy")), P(None, ("gx", "gy"))),
        check_vma=False,
    )
```
